32 devices in a mesh: samp: 2 (over y), band: 16 (over z, x, core).
Axes of the slice: x: 2, y: 2, z: 4, core: 2. Of those that a mesh axis runs over, the one named last changes fastest.
Arguments:
- fields: bfloat16 [4, 2048, 1024], P('samp', 'band'), may hold values from -6 to 6
- lead_bucket: int32 [4], P('samp'), may hold values from 0 to 55
- cotangent: float32 [4, 2048, 1024], P('samp', 'band'), may hold values from -6 to 6
- lead_table: bfloat16 [56, 1024], replicated, may hold values from -3 to 3
- ln1_gain: float32 [1024], replicated, may hold values from 0.25 to 1.75
- ln1_bias: float32 [1024], replicated, may hold values from -1.8 to 1.8
- w_qkv: bfloat16 [1024, 3072], replicated, may hold values from -0.25 to 0.25
- q_bias: float32 [1024], replicated, may hold values from -1.8 to 1.8
- v_bias: float32 [1024], replicated, may hold values from -0.6 to 0.6
- w_out: bfloat16 [1024, 1024], replicated, may hold values from -1 to 1
- out_bias: float32 [1024], replicated, may hold values from -1.8 to 1.8
- ln2_gain: float32 [1024], replicated, may hold values from 0.25 to 1.75
- ln2_bias: float32 [1024], replicated, may hold values from -1.8 to 1.8
- w_up: bfloat16 [1024, 4096], replicated, may hold values from -0.1875 to 0.1875
- up_bias: float32 [4096], replicated, may hold values from -1.8 to 1.8
- w_down: bfloat16 [4096, 1024], replicated, may hold values from -0.09375 to 0.09375
- down_bias: float32 [1024], replicated, may hold values from -1.8 to 1.8
Outputs:
- result: bfloat16 [4, 2048, 1024], P('samp', 'band')
- fields_grad: float32 [4, 2048, 1024], P('samp', 'band')
- lead_table_grad: float32 [56, 1024], P(None, 'band')
- ln1_gain_grad: float32 [1024], P('band')
- ln1_bias_grad: float32 [1024], P('band')
- w_qkv_grad: float32 [1024, 3072], P(None, 'band')
- q_bias_grad: float32 [1024], P('band')
- v_bias_grad: float32 [1024], P('band')
- w_out_grad: float32 [1024, 1024], P(None, 'band')
- out_bias_grad: float32 [1024], P('band')
- ln2_gain_grad: float32 [1024], P('band')
- ln2_bias_grad: float32 [1024], P('band')
- w_up_grad: float32 [1024, 4096], P(None, 'band')
- up_bias_grad: float32 [4096], P('band')
- w_down_grad: float32 [4096, 1024], P(None, 'band')
- down_bias_grad: float32 [1024], P('band')
The draws below stay inside these ranges and needn't reach their ends.
All inputs are finite; a program needn't handle non-finite values.
Results may differ from the reference program's by a relative error of at most 0.019.
Values may be sent and summed in bfloat16 or wider, within the bound.
No kernel may reach another device: no remote copies, remote signals or barrier semaphores. Data moves between devices by JAX's collectives and lax.ppermute only.
A program may use at most 256 MiB of HBM per device.

```python
import math
import jax
import jax.numpy as jnp
import numpy as np
from jax import lax

D = 1024
H = 16
HD = 64
FF = 4096
LEADS = 56
PATCHES = 2048
STEPS = 2
SAMPLES = 4


def set_ends(values, stream_key, least, high):
    shape = values.shape
    spot = [jax.random.randint(jax.random.fold_in(stream_key, axis), (), 0, shape[axis]) for axis in range(len(shape))]
    values = values.at[tuple(spot)].set(least)
    longest = shape.index(max(shape))
    spot[longest] = (spot[longest] + 1) % shape[longest]
    return values.at[tuple(spot)].set(high)


def with_spikes(array, own_key, source, target, parts, factor):
    owner, partner = [(jnp.arange(array.shape[position]) // (array.shape[position] // parts)).reshape([-1 if axis == position else 1 for axis in range(array.ndim)]) for position in (source, target)]
    chosen = jax.random.permutation(own_key, parts)[partner]
    strong = (owner == chosen) | (owner == (partner + parts // 2) % parts)
    return jnp.where(strong, factor * array, array)


def levels(key, extent, split, least, largest):
    gain = 1.0
    for dim, parts in split:
        draws = jax.random.uniform(jax.random.fold_in(jax.random.fold_in(key, 6), dim), (parts,), jnp.float32, least / len(split), largest / len(split))
        gain = gain * jnp.repeat(jnp.exp(draws), extent[dim] // parts).reshape((-1,) + (1,) * (len(extent) - 1 - dim))
    return gain


def cumulative_ranks(count, lean):
    portions = [(1 << 20) // math.isqrt(standing ** lean) + 1 for standing in range(1, count + 1)]
    spread = 1 + sum(portions) // (1 << 30)
    return np.cumsum(np.array([max(1, weight // spread) for weight in portions]))


def ranked(key, shape, count, slope):
    table = cumulative_ranks(count, slope)
    lot = jax.random.randint(jax.random.fold_in(key, 1), shape, 0, int(table[count - 1]))
    rank = jnp.searchsorted(jnp.asarray(table, jnp.int32), lot, side="right")
    return jax.random.permutation(jax.random.fold_in(key, 2), count)[rank].astype(jnp.int32)


def bell_draw(key, dims, deviation, most, shards=(), held_as=jnp.bfloat16):
    factor_of = levels(key, dims, shards, -0.22, 0.18) if shards else 1.0
    entries = jax.random.normal(key, dims, jnp.float32) * deviation * factor_of
    return jnp.minimum(jnp.maximum(entries, -most), most).astype(held_as)


def heavy_noise(rng, extent, spread, reach, shards, heavy, kind=jnp.bfloat16):
    entries = spread * jax.random.normal(rng, extent, jnp.float32)
    if shards:
        entries = entries * levels(rng, extent, shards, -0.22, 0.18)
    return jnp.clip(with_spikes(entries, jax.random.fold_in(rng, 3), *heavy), -reach, reach).astype(kind)


def setup_inputs(seed: int = 0) -> dict:
    seeds = jax.random.split(jax.random.key(seed), 18)
    fields = bell_draw(seeds[0], (SAMPLES, PATCHES, D), 1.0, 6.0, ((0, 2), (1, 16)))
    lead_bucket = set_ends(ranked(seeds[1], (SAMPLES,), LEADS, 2), jax.random.fold_in(seeds[1], 3), 0, LEADS - 1).astype(jnp.int32)
    cotangent = heavy_noise(seeds[2], (SAMPLES, PATCHES, D), 1.0, 6.0, ((0, 2), (1, 16)), (1, 2, 16, 2.0), jnp.float32)
    lead_table = bell_draw(seeds[3], (LEADS, D), 0.5, 3.0)
    ln1_gain = jnp.clip(1.0 + 0.15 * jax.random.normal(seeds[4], (D,), jnp.float32), 0.25, 1.75)
    ln1_bias = bell_draw(seeds[5], (D,), 0.3, 1.8, (), jnp.float32)
    w_qkv = bell_draw(seeds[6], (D, 3 * D), (D // 2) ** -0.5, 0.25)
    q_bias = bell_draw(seeds[7], (D,), 0.3, 1.8, (), jnp.float32)
    v_bias = bell_draw(seeds[8], (D,), 0.1, 0.6, (), jnp.float32)
    w_out = bell_draw(seeds[9], (D, D), (D // 32) ** -0.5, 1.0)
    out_bias = bell_draw(seeds[10], (D,), 0.3, 1.8, (), jnp.float32)
    ln2_gain = jnp.clip(1.0 + 0.15 * jax.random.normal(seeds[11], (D,), jnp.float32), 0.25, 1.75)
    ln2_bias = bell_draw(seeds[12], (D,), 0.3, 1.8, (), jnp.float32)
    w_up = bell_draw(seeds[13], (D, FF), D ** -0.5, 0.1875)
    up_bias = bell_draw(seeds[14], (FF,), 0.3, 1.8, (), jnp.float32)
    w_down = bell_draw(seeds[15], (FF, D), FF ** -0.5, 0.09375)
    down_bias = bell_draw(seeds[16], (D,), 0.3, 1.8, (), jnp.float32)
    return dict(fields=fields, lead_bucket=lead_bucket, cotangent=cotangent, lead_table=lead_table, ln1_gain=ln1_gain, ln1_bias=ln1_bias, w_qkv=w_qkv, q_bias=q_bias, v_bias=v_bias, w_out=w_out, out_bias=out_bias, ln2_gain=ln2_gain, ln2_bias=ln2_bias, w_up=w_up, up_bias=up_bias, w_down=w_down, down_bias=down_bias)


@jax.custom_vjp
def low(v):
    return lax.optimization_barrier(v.astype(jnp.bfloat16)).astype(jnp.float32)

@jax.custom_vjp
def low_back(v):
    return v

def low_keep(v):
    return (low(v), None)

def low_pass(kept, grad):
    return (grad,)

def back_keep(v):
    return (v, None)

def back_low(kept, grad):
    return (low(grad),)
low.defvjp(low_keep, low_pass)
low_back.defvjp(back_keep, back_low)
exact_mode = lax.Precision.HIGHEST
norm_epsilon = 1e-05

def layer_norm(values, norm_gain, norm_shift):
    average = lax.optimization_barrier(jnp.mean(values, axis=-1, keepdims=True))
    centred = values - average
    variance = lax.optimization_barrier(jnp.mean(centred * centred, axis=-1, keepdims=True))
    return centred * lax.rsqrt(variance + norm_epsilon) * norm_gain + norm_shift

def attend(projected):
    queries = projected[:, :D].reshape(PATCHES, H, HD)
    keys = projected[:, D:2 * D].reshape(PATCHES, H, HD)
    values = projected[:, 2 * D:].reshape(PATCHES, H, HD)
    scores = low_back(jnp.einsum('qhd,khd->hqk', queries, keys, precision=exact_mode) * 0.125)
    probability = jax.nn.softmax(scores, axis=-1)
    attended = jnp.einsum('hqk,khd->qhd', low(probability), values, precision=exact_mode)
    return attended.reshape(PATCHES, D)

def trunk_block(inputs, params):
    lead_table, ln1_gain, ln1_bias, w_qkv, q_bias, v_bias, w_out, out_bias, ln2_gain, ln2_bias, w_up, up_bias, w_down, down_bias = params
    normed = low(layer_norm(inputs, ln1_gain, ln1_bias))
    qkv_bias = jnp.concatenate([q_bias, jnp.zeros_like(q_bias), v_bias])
    projected = low_back(low(jnp.dot(normed, w_qkv, precision=exact_mode) + qkv_bias))
    attended = low_back(low(attend(projected)))
    branch = low_back(jnp.dot(attended, w_out, precision=exact_mode) + out_bias)
    middle = inputs + branch
    normed_two = low(layer_norm(middle, ln2_gain, ln2_bias))
    hidden = low_back(jnp.dot(normed_two, w_up, precision=exact_mode) + up_bias)
    activated = low(jax.nn.gelu(hidden, approximate=True))
    branch_two = low_back(jnp.dot(activated, w_down, precision=exact_mode) + down_bias)
    return middle + branch_two

def two_steps(sample_fields, bucket, params):
    one_hot = (jnp.arange(LEADS, dtype=jnp.int32) == bucket).astype(jnp.float32)
    lead_row = jnp.dot(one_hot, params[0], precision=exact_mode)
    carried = sample_fields
    for step_index in range(STEPS):
        carried = trunk_block(carried + lead_row[None, :], params)
    return carried

def reference(fields, lead_bucket, cotangent, lead_table, ln1_gain, ln1_bias, w_qkv, q_bias, v_bias, w_out, out_bias, ln2_gain, ln2_bias, w_up, up_bias, w_down, down_bias):
    params = tuple((weight.astype(jnp.float32) for weight in (lead_table, ln1_gain, ln1_bias, w_qkv, q_bias, v_bias, w_out, out_bias, ln2_gain, ln2_bias, w_up, up_bias, w_down, down_bias)))

    def forward(fields_float, weights):

        def per_sample(sample_item):
            sample_fields, bucket = sample_item
            checked = jax.checkpoint(lambda values, inner_weights: two_steps(values, bucket, inner_weights))
            return checked(sample_fields, weights)
        return lax.map(per_sample, (fields_float, lead_bucket))
    final_state, pullback = jax.vjp(forward, fields.astype(jnp.float32), params)
    fields_grad, param_grads = pullback(cotangent)
    return (final_state.astype(jnp.bfloat16), fields_grad, param_grads[0], param_grads[1], param_grads[2], param_grads[3], param_grads[4], param_grads[5], param_grads[6], param_grads[7], param_grads[8], param_grads[9], param_grads[10], param_grads[11], param_grads[12], param_grads[13])
```

```python
import functools

import jax
import jax.numpy as jnp
from jax import lax
from jax.experimental import pallas as pl
from jax.experimental.pallas import tpu as pltpu
from jax.sharding import Mesh
from jax.sharding import PartitionSpec as P

HD = 64
STEPS = 2
EPS = 1e-05
EXP_SCALE = 0.125 * 1.4426950408889634
GELU_A = 0.7978845608028654
GELU_B = 0.044715
SWAP = [(0, 1), (1, 0)]
f32 = jnp.float32
bf16 = jnp.bfloat16


def contract(a, b, a_dim, b_dim):
    return lax.dot_general(a, b, (((a_dim,), (b_dim,)), ((), ())), preferred_element_type=f32)


def head_part(x, h, heads):
    if heads == 1:
        return x
    lane = lax.broadcasted_iota(jnp.int32, x.shape, 1)
    return jnp.where(lane // HD == h, x, jnp.zeros_like(x))


def attend_kernel(q_ref, k_ref, v_ref, o_ref, *, heads):
    q, k, v = q_ref[...], k_ref[...], v_ref[...]
    out = None
    for h in range(heads):
        s = contract(head_part(q, h, heads), k, 1, 1)
        top = jnp.max(s, axis=-1, keepdims=True)
        e = jnp.exp2((s - top) * EXP_SCALE)
        total = jnp.sum(e, axis=-1, keepdims=True)
        o = head_part(contract(e.astype(bf16), v, 1, 0) / total, h, heads)
        out = o if out is None else out + o
    o_ref[...] = out.astype(bf16)


def attend(q, k, v):
    rows, width = q.shape
    count = k.shape[0]
    block = 2 * HD
    own = pl.BlockSpec((rows, block), lambda j: (0, j))
    full = pl.BlockSpec((count, block), lambda j: (0, j))
    return pl.pallas_call(
        functools.partial(attend_kernel, heads=block // HD),
        grid=(width // block,),
        in_specs=[own, full, full],
        out_specs=own,
        out_shape=jax.ShapeDtypeStruct((rows, width), bf16),
        compiler_params=pltpu.CompilerParams(vmem_limit_bytes=48 * 2**20),
        cost_estimate=pl.CostEstimate(
            flops=4 * rows * count * width,
            bytes_accessed=4 * (rows + count) * width,
            transcendentals=rows * count * width // HD,
        ),
        name="attend",
    )(q, k, v)


def attend_back_kernel(q_ref, k_ref, v_ref, do_ref, dq_ref, dk_ref, dv_ref, dk_sum, dv_sum, *, heads):
    step = pl.program_id(0)

    @pl.when(step == 0)
    def _():
        dk_sum[...] = jnp.zeros_like(dk_sum)
        dv_sum[...] = jnp.zeros_like(dv_sum)

    q, k, v, do = q_ref[...], k_ref[...], v_ref[...], do_ref[...]
    dq = None
    for h in range(heads):
        qh, doh = head_part(q, h, heads), head_part(do, h, heads)
        s = contract(qh, k, 1, 1)
        dp = contract(doh, v, 1, 1)
        top = jnp.max(s, axis=-1, keepdims=True)
        e = jnp.exp2((s - top) * EXP_SCALE)
        inverse = 1.0 / jnp.sum(e, axis=-1, keepdims=True)
        inner = jnp.sum(e * dp, axis=-1, keepdims=True) * inverse
        p = e * inverse
        ds = (p * (dp - inner)).astype(bf16)
        part = head_part(contract(ds, k, 1, 0), h, heads)
        dq = part if dq is None else dq + part
        dk_sum[...] += contract(ds, qh, 0, 0)
        dv_sum[...] += contract(p.astype(bf16), doh, 0, 0)
    dq_ref[...] = (dq * 0.125).astype(bf16)

    @pl.when(step == pl.num_programs(0) - 1)
    def _():
        dk_ref[...] = (dk_sum[...] * 0.125).astype(bf16)
        dv_ref[...] = dv_sum[...].astype(bf16)


def attend_back(q, k, v, do):
    count, width = q.shape
    rows = 256
    part = pl.BlockSpec((rows, width), lambda i: (i, 0))
    full = pl.BlockSpec((count, width), lambda i: (0, 0))
    out = jax.ShapeDtypeStruct((count, width), bf16)
    return pl.pallas_call(
        functools.partial(attend_back_kernel, heads=width // HD),
        grid=(count // rows,),
        in_specs=[part, full, full, part],
        out_specs=[part, full, full],
        out_shape=[out, out, out],
        scratch_shapes=[pltpu.VMEM((count, width), f32), pltpu.VMEM((count, width), f32)],
        compiler_params=pltpu.CompilerParams(vmem_limit_bytes=48 * 2**20),
        cost_estimate=pl.CostEstimate(
            flops=10 * count * count * width,
            bytes_accessed=14 * count * width,
            transcendentals=count * count * width // HD,
        ),
        name="attend_back",
    )(q, k, v, do)


def norm_parts(v):
    centred = v - jnp.mean(v, axis=-1, keepdims=True)
    r = lax.rsqrt(jnp.mean(centred * centred, axis=-1, keepdims=True) + EPS)
    return centred * r, r


def norm_back(dy, n, r, gain):
    dyg = dy * gain
    mean_one = jnp.mean(dyg, axis=-1, keepdims=True)
    mean_two = jnp.mean(dyg * n, axis=-1, keepdims=True)
    dv = r * (dyg - mean_one - n * mean_two)
    return dv, jnp.sum(dy * n, axis=0), jnp.sum(dy, axis=0)


def gelu(x):
    return 0.5 * x * (1.0 + jnp.tanh(GELU_A * (x + GELU_B * x * x * x)))


def gelu_slope(x):
    t = jnp.tanh(GELU_A * (x + GELU_B * x * x * x))
    return 0.5 * (1.0 + t) + 0.5 * x * (1.0 - t * t) * (GELU_A * (1.0 + 3.0 * GELU_B * x * x))


def dot(a, b):
    return jnp.dot(a, b, preferred_element_type=f32)


def dot_t(a, b):
    return contract(a, b, 1, 1)


def token_dot(pairs):
    a = jnp.concatenate([p[0] for p in pairs])
    b = jnp.concatenate([p[1] for p in pairs])
    return contract(a, b, 0, 0).astype(bf16)


def swap(x, axis):
    return lax.ppermute(x, axis, SWAP)


def half_sum(x, axis, dim):
    me = lax.axis_index(axis)
    there = lax.dynamic_index_in_dim(x, 1 - me, dim, keepdims=False)
    here = lax.dynamic_index_in_dim(x, me, dim, keepdims=False)
    return (here.astype(f32) + swap(there, axis).astype(f32)).astype(bf16)


def add_pair(x, axis):
    return (x.astype(f32) + swap(x, axis).astype(f32)).astype(bf16)


def add_samples(x, two):
    return add_pair(x, "samp") if two else lax.psum(x, "samp")


def body(
    fields,
    lead_bucket,
    cotangent,
    lead_table,
    ln1_gain,
    ln1_bias,
    w_qkv,
    q_bias,
    v_bias,
    w_out,
    out_bias,
    ln2_gain,
    ln2_bias,
    w_up,
    up_bias,
    w_down,
    down_bias,
    *,
    axes,
    x_axes,
    samp_count,
):
    band = tuple(axes)
    low = ("core", "zl") + x_axes[::-1]
    members = 2 ** len(low)
    order = x_axes + ("zl", "core")
    D = w_out.shape[0]
    W = D // members
    half = fields.shape[1]
    rows = 2 * half
    two = samp_count == 2
    zh = lax.axis_index("zh")
    me = lax.axis_index(low)

    def pick(x, i):
        return lax.dynamic_index_in_dim(x, i, 0, keepdims=False)

    def to_sample(x):
        return jnp.concatenate([pick(x, zh), swap(pick(x, 1 - zh), "zh")])

    def to_band(x):
        own = x[:half]
        other = swap(x[half:].astype(bf16), "zh").astype(x.dtype)
        return jnp.where(zh == 0, jnp.stack([own, other]), jnp.stack([other, own]))

    def gather(x):
        if len(x_axes) == 1:
            x_axis = x_axes[0]
            cut = x.shape[0] // 2
            by_x = swap(x, x_axis)
            by_z = swap(x, "zl")
            far = [swap(by_x[:cut], "zl"), swap(by_z[cut:], x_axis)]
            pieces = [(x, 0, 0), (by_x, 1, 0), (by_z, 2, 0), (far[0], 3, 0), (far[1], 3, cut)]
            pieces += [(swap(p, "core"), 4 + k, o) for p, k, o in pieces]
        else:
            pieces = [(x, 0, 0)]
            for bit, axis in enumerate(order):
                pieces += [(swap(p, axis), k + 2**bit, 0) for p, k, _ in pieces]
        out = jnp.zeros((members * rows, D), bf16)
        for piece, k, offset in pieces:
            out = lax.dynamic_update_slice(out, piece, ((me ^ k) * rows + offset, 0))
        return out

    lead_row = pick(lead_table, pick(lead_bucket, zh)).astype(f32)
    kv_bias = jnp.concatenate([jnp.zeros_like(v_bias), v_bias])
    carried = to_sample(fields).astype(f32)
    out_grad = to_sample(cotangent)

    def member_columns(x, block):
        return lax.dynamic_slice_in_dim(x, block * D + me * W, W, x.ndim - 1)

    kept = []
    for _ in range(STEPS):
        inputs = carried + lead_row
        n1, r1 = norm_parts(inputs)
        normed = (n1 * ln1_gain + ln1_bias).astype(bf16)
        normed_all = gather(normed)
        queries = (dot(normed, w_qkv[:, :D]) + q_bias).astype(bf16)
        keys_values = (dot(normed_all, w_qkv[:, D:]) + kv_bias).astype(bf16)
        keys, values = keys_values[:, :D], keys_values[:, D:]
        attended = attend(queries, keys, values)
        q_own = (
            dot(normed_all, member_columns(w_qkv, 0)) + member_columns(q_bias, 0)
        ).astype(bf16)
        k_own = member_columns(keys, 0)
        v_own = member_columns(values, 0)
        middle = inputs + dot(attended, w_out) + out_bias
        n2, r2 = norm_parts(middle)
        normed_two = (n2 * ln2_gain + ln2_bias).astype(bf16)
        hidden = dot(normed_two, w_up) + up_bias
        activated = gelu(hidden).astype(bf16)
        carried = middle + dot(activated, w_down) + down_bias
        kept.append((n1, r1, normed, q_own, k_own, v_own, attended, n2, r2, normed_two, hidden, activated))
    result = to_band(carried.astype(bf16))

    grad = out_grad
    small = None
    pairs = {"qkv": [], "out": [], "up": [], "down": []}
    for n1, r1, normed, q_own, k_own, v_own, attended, n2, r2, normed_two, hidden, activated in kept[::-1]:
        down_grad = grad.astype(bf16)
        hidden_grad = (gelu_slope(hidden) * dot_t(down_grad, w_down)).astype(bf16)
        dv, gain_two, bias_two = norm_back(dot_t(hidden_grad, w_up), n2, r2, ln2_gain)
        middle_grad = grad + dv
        branch_grad = middle_grad.astype(bf16)
        pairs["down"].append((down_grad, activated))
        pairs["up"].append((hidden_grad, normed_two))
        pairs["out"].append((branch_grad, attended))
        attended_grad = dot_t(branch_grad, w_out).astype(bf16)
        sent = attended_grad.reshape(rows, members, W).transpose(1, 0, 2)
        own_grad = lax.all_to_all(sent, low, 0, 0, tiled=True).reshape(members * rows, W)
        dq, dk, dval = attend_back(q_own, k_own, v_own, own_grad)
        sent = jnp.stack([t.reshape(members, rows, W) for t in (dq, dk, dval)], axis=1)
        back = lax.all_to_all(sent, low, 0, 0, tiled=True)
        projected_grad = back.transpose(2, 1, 0, 3).reshape(rows, 3 * D)
        pairs["qkv"].append((projected_grad, normed))
        dv, gain_one, bias_one = norm_back(dot_t(projected_grad, w_qkv), n1, r1, ln1_gain)
        grad = middle_grad + dv
        step_small = (
            gain_one,
            bias_one,
            jnp.sum(projected_grad[:, :D], axis=0, dtype=f32),
            jnp.sum(projected_grad[:, 2 * D :], axis=0, dtype=f32),
            jnp.sum(branch_grad, axis=0, dtype=f32),
            gain_two,
            bias_two,
            jnp.sum(hidden_grad, axis=0, dtype=f32),
            jnp.sum(down_grad, axis=0, dtype=f32),
            jnp.sum(grad, axis=0),
        )
        small = step_small if small is None else tuple(a + b for a, b in zip(small, step_small))
    fields_grad = to_band(grad)

    def blocks(x):
        return x.reshape((2,) * len(axes) + (x.shape[0] // 2 ** len(axes), x.shape[1]))

    def share(x, first_y, turn):
        x = blocks(x)
        left = list(axes)
        x = half_sum(x, "core", left.index("core"))
        left.remove("core")
        if first_y and two:
            x = x.reshape(x.shape[:-2] + (2, x.shape[-2] // 2, x.shape[-1]))
            x = half_sum(x, "samp", len(left))
        for axis in turn:
            x = half_sum(x, axis, left.index(axis))
            left.remove(axis)
        if first_y and two:
            y = lax.axis_index("samp")
            other = swap(x, "samp")
            x = jnp.concatenate([jnp.where(y == 0, x, other), jnp.where(y == 0, other, x)])
        else:
            x = add_samples(x, two)
        return x.astype(f32).T

    x_first = x_axes + ("zl", "zh")
    z_first = ("zl", "zh") + x_axes
    w_down_grad = share(token_dot(pairs["down"]), True, x_first)
    w_up_grad = share(token_dot(pairs["up"]), False, x_first)
    w_out_grad = share(token_dot(pairs["out"]), False, z_first)
    w_qkv_grad = share(token_dot(pairs["qkv"]), True, z_first)

    bands = 2 ** len(axes)
    lead = small[-1]
    leads = [jnp.where(zh == i, lead, 0.0) for i in range(2)]
    vectors = list(small[:-1]) + leads
    packed = jnp.concatenate([v.reshape(bands, -1) for v in vectors], axis=1)
    summed = jnp.sum(lax.all_to_all(packed, band, 0, 0, tiled=True), axis=0)
    widths = [v.shape[0] // bands for v in vectors]
    starts = [sum(widths[:i]) for i in range(len(widths) + 1)]
    lead_sums = summed[starts[-3] :].reshape(2, -1)
    one_hot = (lead_bucket[:, None] == jnp.arange(lead_table.shape[0], dtype=jnp.int32)[None, :]).astype(f32)
    lead_part = jnp.dot(one_hot.T, lead_sums, precision=lax.Precision.HIGHEST)
    joined = jnp.concatenate([summed[: starts[-3]], lead_part.reshape(-1)])
    if two:
        joined = joined + swap(joined, "samp")
    else:
        joined = lax.psum(joined, "samp")
    g = [joined[starts[i] : starts[i + 1]] for i in range(len(widths) - 2)]
    lead_grad = joined[starts[-3] :].reshape(lead_part.shape)
    return (
        result,
        fields_grad,
        lead_grad,
        g[0],
        g[1],
        w_qkv_grad,
        g[2],
        g[3],
        w_out_grad,
        g[4],
        g[5],
        g[6],
        w_up_grad,
        g[7],
        w_down_grad,
        g[8],
    )


def solution(mesh):
    samp_count, band_count = mesh.shape["samp"], mesh.shape["band"]
    x_axes = tuple(f"x{i}" for i in range((band_count // 8).bit_length() - 1))
    axes = ("zh", "zl") + x_axes + ("core",)
    assert 2 ** len(axes) == band_count
    fine = Mesh(mesh.devices.reshape((samp_count,) + (2,) * len(axes)), ("samp",) + axes)
    tokens = P("samp", axes, None)
    columns, vector = P(None, axes), P(axes)
    in_specs = (tokens, P("samp"), tokens) + (P(),) * 14
    out_specs = (
        tokens,
        tokens,
        columns,
        vector,
        vector,
        columns,
        vector,
        vector,
        columns,
        vector,
        vector,
        vector,
        columns,
        vector,
        columns,
        vector,
    )
    run = functools.partial(body, axes=axes, x_axes=x_axes, samp_count=samp_count)
    return jax.shard_map(run, mesh=fine, in_specs=in_specs, out_specs=out_specs, check_vma=False)
```

```python
import functools
import math

import jax
import jax.numpy as jnp
import numpy as np
from jax import lax
from jax.experimental import pallas as pl
from jax.experimental.pallas import tpu as pltpu
from jax.sharding import Mesh
from jax.sharding import PartitionSpec as P

HD = 64
STEPS = 2
EPS = 1e-05
EXP_SCALE = 0.125 * 1.4426950408889634
GELU_A = 0.7978845608028654
GELU_B = 0.044715
MIB = 2**20
SWAP = [(0, 1), (1, 0)]
f32 = jnp.float32
bf16 = jnp.bfloat16


def cost(us):
    return pl.CostEstimate(flops=int(us * 1.15e9), bytes_accessed=1000, transcendentals=0)


def contract(a, b, a_dim, b_dim):
    return lax.dot_general(a, b, (((a_dim,), (b_dim,)), ((), ())), preferred_element_type=f32)


def head_part(x, h, heads):
    if heads == 1:
        return x
    lane = lax.broadcasted_iota(jnp.int32, x.shape, 1)
    return jnp.where(lane // HD == h, x, jnp.zeros_like(x))


def attend_kernel(q_ref, n_ref, wk_ref, wv_ref, b_ref, o_ref):
    normed = n_ref[...]
    keys = contract(normed, wk_ref[...], 1, 0).astype(bf16)
    values = (contract(normed, wv_ref[...], 1, 0) + b_ref[...]).astype(bf16)
    pair = 2 * HD
    for start in range(0, q_ref.shape[1], pair):
        q, k, v = q_ref[:, start : start + pair], keys[:, start : start + pair], values[:, start : start + pair]
        out = None
        for h in range(2):
            s = contract(head_part(q, h, 2), k, 1, 1)
            top = jnp.max(s, axis=-1, keepdims=True)
            e = jnp.exp2((s - top) * EXP_SCALE)
            total = jnp.sum(e, axis=-1, keepdims=True)
            o = head_part(contract(e.astype(bf16), v, 1, 0) / total, h, 2)
            out = o if out is None else out + o
        o_ref[:, start : start + pair] = out.astype(bf16)


def attend(q, normed_all, w_qkv, v_bias):
    rows, width = q.shape
    count = normed_all.shape[0]
    block = 4 * HD
    own = spec((rows, block), lambda j: (0, j))
    shift = width // block
    return pl.pallas_call(
        attend_kernel,
        grid=(width // block,),
        in_specs=[
            own,
            spec((count, width), lambda j: (0, 0)),
            spec((width, block), lambda j: (0, shift + j)),
            spec((width, block), lambda j: (0, 2 * shift + j)),
            spec((1, block), lambda j: (0, j)),
        ],
        out_specs=own,
        out_shape=jax.ShapeDtypeStruct((rows, width), bf16),
        compiler_params=pltpu.CompilerParams(vmem_limit_bytes=40 * MIB),
        cost_estimate=cost(24),
        name="attend",
    )(q, normed_all, w_qkv, w_qkv, v_bias.reshape(1, width))


def attend_back_kernel(q_ref, k_ref, v_ref, do_ref, *rest, heads, some):
    out_ref, dk_sum, dv_sum = rest[-3:]
    step = pl.program_id(0)
    rows = q_ref.shape[0]

    @pl.when(step == 0)
    def _():
        dk_sum[...] = jnp.zeros_like(dk_sum)
        dv_sum[...] = jnp.zeros_like(dv_sum)

    q, k, v, do = q_ref[...], k_ref[...], v_ref[...], do_ref[...]
    dq = None
    for h in some:
        qh, doh = head_part(q, h, heads), head_part(do, h, heads)
        s = contract(qh, k, 1, 1)
        dp = contract(doh, v, 1, 1)
        top = jnp.max(s, axis=-1, keepdims=True)
        e = jnp.exp2((s - top) * EXP_SCALE)
        inverse = 1.0 / jnp.sum(e, axis=-1, keepdims=True)
        inner = jnp.sum(e * dp, axis=-1, keepdims=True) * inverse
        p = e * inverse
        ds = (p * (dp - inner)).astype(bf16)
        part = head_part(contract(ds, k, 1, 0), h, heads)
        dq = part if dq is None else dq + part
        dk_sum[...] += contract(ds, qh, 0, 0)
        dv_sum[...] += contract(p.astype(bf16), doh, 0, 0)

    def put(m, i, x):
        if len(rest) == 4:
            x = x + rest[0][m, i].astype(f32)
        out_ref[m, i] = x.astype(bf16)

    put(step, 0, dq * 0.125)

    @pl.when(step == pl.num_programs(0) - 1)
    def _():
        for m in range(out_ref.shape[0]):
            put(m, 1, dk_sum[m * rows : (m + 1) * rows, :] * 0.125)
            put(m, 2, dv_sum[m * rows : (m + 1) * rows, :])


def attend_back(q, k, v, do, members, some=None, add=None):
    count, width = q.shape
    rows = count // members
    heads = width // HD
    part = pl.BlockSpec((rows, width), lambda i: (i, 0))
    full = pl.BlockSpec((count, width), lambda i: (0, 0))
    shape = (members, 3, rows, width)
    out = pl.BlockSpec(shape, lambda i: (0, 0, 0, 0))
    extra = [] if add is None else [add]
    return pl.pallas_call(
        functools.partial(attend_back_kernel, heads=heads, some=some or range(heads)),
        grid=(members,),
        in_specs=[part, full, full, part] + [out] * len(extra),
        out_specs=out,
        out_shape=jax.ShapeDtypeStruct(shape, bf16),
        scratch_shapes=[pltpu.VMEM((count, width), f32), pltpu.VMEM((count, width), f32)],
        compiler_params=pltpu.CompilerParams(vmem_limit_bytes=60 * MIB),
        cost_estimate=cost(33 if some is None else 17),
        name="attend_back",
    )(q, k, v, do, *extra)


def spec(block, index):
    return pl.BlockSpec(block, index)


def grad_rows_kernel(c_ref, l1, l0, r1, r0, other_ref, own_ref, sums):
    sums[...] = contract(l1[...], r1[...], 0, 0) + contract(l0[...], r0[...], 0, 0)
    count, n, _ = own_ref.shape
    for j in range(count):
        for ref, core in ((other_ref, 1 - c_ref[0]), (own_ref, c_ref[0])):
            ref[j] = sums[pl.ds(pl.multiple_of((2 * j + core) * n, n), n), :].astype(bf16)


def grad_rows(core, left, right, bands, part, parts):
    tokens, m = left[0].shape
    n = right[0].shape[1] // parts
    block = min(n, 512)
    first = part * (n // block)
    out = spec((bands // 2, m // bands, block), lambda j, c: (0, 0, j))
    whole = spec((tokens, m), lambda j, c: (0, 0))
    part = spec((tokens, block), lambda j, c: (0, first + j))
    return pl.pallas_call(
        grad_rows_kernel,
        grid_spec=pltpu.PrefetchScalarGridSpec(
            num_scalar_prefetch=1,
            grid=(n // block,),
            in_specs=[whole, whole, part, part],
            out_specs=[out, out],
            scratch_shapes=[pltpu.VMEM((m, block), f32)],
        ),
        out_shape=[jax.ShapeDtypeStruct((bands // 2, m // bands, n), bf16)] * 2,
        compiler_params=pltpu.CompilerParams(vmem_limit_bytes=16 * MIB),
        cost_estimate=cost(8),
        name="grad_rows",
    )(core.reshape(1), *left, *right)


def block_forward_kernel(
    x_ref, a_ref, wo_ref, bo_ref, g_ref, b_ref, wu_ref, bu_ref, wd_ref, bd_ref, lead_ref, g1_ref, b1_ref,
    n2_ref, r2_ref, low2_ref, hidden_ref, act_ref, *rest, last
):
    total = rest[-1]
    step = pl.program_id(0)

    @pl.when(step == 0)
    def _():
        middle = x_ref[...] + contract(a_ref[...], wo_ref[...], 1, 0) + bo_ref[...]
        n, r = norm_parts(middle)
        n2_ref[...] = n
        r2_ref[...] = r
        low2_ref[...] = (n * g_ref[...] + b_ref[...]).astype(bf16)
        total[...] = middle + bd_ref[...]

    hidden = contract(low2_ref[...], wu_ref[...], 1, 0) + bu_ref[...]
    hidden_ref[...] = hidden
    act = gelu(hidden).astype(bf16)
    act_ref[...] = act
    total[...] += contract(act, wd_ref[...], 1, 0)

    @pl.when(step == pl.num_programs(0) - 1)
    def _():
        carried = total[...]
        if last:
            rest[0][...] = carried.astype(bf16)
        else:
            x = carried + lead_ref[...]
            n, r = norm_parts(x)
            rest[0][...] = x
            rest[1][...] = n
            rest[2][...] = r
            rest[3][...] = (n * g1_ref[...] + b1_ref[...]).astype(bf16)


def block_forward(inputs, attended, weights, last):
    w_out, out_bias, ln2_gain, ln2_bias, w_up, up_bias, w_down, down_bias, lead, ln1_gain, ln1_bias = weights
    t, d = inputs.shape
    f = w_up.shape[1]
    block = 512
    row = lambda v: v.reshape(1, -1)
    full = spec((t, d), lambda i: (0, 0))
    vec = spec((1, d), lambda i: (0, 0))
    one = spec((t, 1), lambda i: (0, 0))
    wide = spec((t, block), lambda i: (0, i))
    shape = jax.ShapeDtypeStruct
    outs = [full, one, full, wide, wide] + ([full] if last else [full, full, one, full])
    shapes = [shape((t, d), f32), shape((t, 1), f32), shape((t, d), bf16), shape((t, f), f32), shape((t, f), bf16)]
    shapes += [shape((t, d), bf16)] if last else [
        shape((t, d), f32), shape((t, d), f32), shape((t, 1), f32), shape((t, d), bf16)
    ]
    return pl.pallas_call(
        functools.partial(block_forward_kernel, last=last),
        grid=(f // block,),
        in_specs=[
            full, full, spec((d, d), lambda i: (0, 0)), vec, vec, vec,
            spec((d, block), lambda i: (0, i)), spec((1, block), lambda i: (0, i)),
            spec((block, d), lambda i: (i, 0)), vec, vec, vec, vec,
        ],
        out_specs=outs,
        out_shape=shapes,
        scratch_shapes=[pltpu.VMEM((t, d), f32)],
        compiler_params=pltpu.CompilerParams(vmem_limit_bytes=40 * MIB),
        cost_estimate=cost(12),
        name="block_forward",
    )(
        inputs, attended, w_out, row(out_bias), row(ln2_gain), row(ln2_bias), w_up, row(up_bias), w_down,
        row(down_bias), row(lead), row(ln1_gain), row(ln1_bias),
    )


def put_sums(ref, *sums):
    for i, v in enumerate(sums):
        ref[i : i + 1, :] = v


def column_sum(x):
    return jnp.sum(x.astype(f32), axis=0, keepdims=True)


def block_backward_kernel(c_ref, grad_ref, h_ref, wd_ref, wu_ref, wo_ref, n_ref, r_ref, g_ref, *rest, grads, bands):
    if grads:
        l1_ref, x1_ref, x0_ref = rest[:3]
        z_other, x_other, z_own, x_own = rest[9:13]
        sums, rest = rest[14], rest[3:9] + rest[13:14]
    hg_ref, hsum_ref, middle_ref, branch_ref, sent_ref, sums_ref, total = rest
    step = pl.program_id(0)
    down = grad_ref[...].astype(bf16)
    low = (gelu_slope(h_ref[...]) * contract(down, wd_ref[...], 1, 1)).astype(bf16)
    hg_ref[...] = low
    hsum_ref[...] = column_sum(low)
    part = contract(low, wu_ref[...], 1, 1)
    if grads:
        sums[...] = contract(l1_ref[...], x1_ref[...], 0, 0) + contract(low, x0_ref[...], 0, 0)
        pairs = z_own.shape[0]
        n = sums.shape[0] // (2 * pairs)
        for q in range(pairs):
            for z, x, core in ((z_other, x_other, 1 - c_ref[0]), (z_own, x_own, c_ref[0])):
                start = pl.multiple_of((2 * q + core) * n, n)
                z[q] = sums[pl.ds(start, n // 2), :].astype(bf16)
                x[q] = sums[pl.ds(start + n // 2, n // 2), :].astype(bf16)

    @pl.when(step == 0)
    def _():
        total[...] = part

    @pl.when(step > 0)
    def _():
        total[...] += part

    @pl.when(step == pl.num_programs(0) - 1)
    def _():
        dv, gain, bias = norm_back(total[...], n_ref[...], r_ref[...], g_ref[...])
        middle = grad_ref[...] + dv
        middle_ref[...] = middle
        branch = middle.astype(bf16)
        branch_ref[...] = branch
        put_sums(sums_ref, gain, bias, column_sum(branch), column_sum(down))
        w = sent_ref.shape[2]
        attended = contract(branch, wo_ref[...], 1, 1).astype(bf16)
        for m in range(sent_ref.shape[0]):
            sent_ref[m] = attended[:, m * w : (m + 1) * w]


def block_backward(core, grad, hidden, w_down, w_up, w_out, n2, r2, gain, members, grads=()):
    t, d = grad.shape
    f = hidden.shape[1]
    block = 512
    bands = 2 * members
    full = spec((t, d), lambda i, c: (0, 0))
    wide = spec((t, block), lambda i, c: (0, i))
    sent = (members, t, d // members)
    shape = jax.ShapeDtypeStruct
    outs = [
        wide, spec((1, block), lambda i, c: (0, i)), full, full,
        spec(sent, lambda i, c: (0, 0, 0)), spec((8, d), lambda i, c: (0, 0)),
    ]
    shapes = [
        shape((t, f), bf16), shape((1, f), f32), shape((t, d), f32), shape((t, d), bf16),
        shape(sent, bf16), shape((8, d), f32),
    ]
    scratch = [pltpu.VMEM((t, d), f32)]
    if grads:
        n = f // bands
        pairs = block // (2 * n)
        part = spec((pairs, n // 2, d), lambda i, c: (i, 0, 0))
        outs += [part] * 4
        shapes += [shape((bands // 2, n // 2, d), bf16), shape((bands // 2, n // 2 + d // bands, d), bf16)] * 2
        scratch += [pltpu.VMEM((block, d), f32)]
    return pl.pallas_call(
        functools.partial(block_backward_kernel, grads=bool(grads), bands=bands),
        grid_spec=pltpu.PrefetchScalarGridSpec(
            num_scalar_prefetch=1,
            grid=(f // block,),
            in_specs=[
                full, wide, spec((block, d), lambda i, c: (i, 0)), spec((d, block), lambda i, c: (0, i)),
                spec((d, d), lambda i, c: (0, 0)), full, spec((t, 1), lambda i, c: (0, 0)),
                spec((1, d), lambda i, c: (0, 0)),
            ] + [wide, full, full][: len(grads)],
            out_specs=outs,
            scratch_shapes=scratch,
        ),
        out_shape=shapes,
        compiler_params=pltpu.CompilerParams(vmem_limit_bytes=48 * MIB),
        cost_estimate=cost(18 if grads else 14),
        name="block_backward",
    )(core.reshape(1), grad, hidden, w_down, w_up, w_out, n2, r2, gain.reshape(1, d), *grads)


def grad_out_kernel(c_ref, l1, l0, r1, r0, _, __, other_ref, own_ref, sums, *, pairs):
    sums[...] = contract(l1[...], r1[...], 0, 0) + contract(l0[...], r0[...], 0, 0)
    n = own_ref.shape[1]
    for q in range(pairs):
        for ref, core in ((other_ref, 1 - c_ref[0]), (own_ref, c_ref[0])):
            ref[q] = sums[pl.ds(pl.multiple_of((2 * q + core) * n, n), n), :].astype(bf16)


def grad_out(core, left, right, bands, other, own):
    tokens, m = left[0].shape
    count, height, d = own.shape
    n = m // bands
    pairs = max(1, 256 // (2 * n))
    columns = spec((tokens, 2 * n * pairs), lambda j, c: (0, j))
    whole = spec((tokens, d), lambda j, c: (0, 0))
    out = spec((pairs, n, d), lambda j, c: (j, height // n - 1, 0))
    anywhere = pl.BlockSpec(memory_space=pl.ANY)
    return pl.pallas_call(
        functools.partial(grad_out_kernel, pairs=pairs),
        grid_spec=pltpu.PrefetchScalarGridSpec(
            num_scalar_prefetch=1,
            grid=(count // pairs,),
            in_specs=[columns, columns, whole, whole, anywhere, anywhere],
            out_specs=[out, out],
            scratch_shapes=[pltpu.VMEM((2 * n * pairs, d), f32)],
        ),
        out_shape=[jax.ShapeDtypeStruct(own.shape, bf16)] * 2,
        input_output_aliases={5: 0, 6: 1},
        compiler_params=pltpu.CompilerParams(vmem_limit_bytes=16 * MIB),
        cost_estimate=cost(3),
        name="grad_out",
    )(core.reshape(1), *left, *right, other, own)


def qkv_backward_kernel(b_ref, wq_ref, wk_ref, wv_ref, m_ref, n_ref, r_ref, g_ref, grad_ref, low_ref, sums_ref, qv_ref, total):
    step = pl.program_id(0)
    w = b_ref.shape[3]
    part = None
    for m in range(b_ref.shape[0]):
        for i, ref in enumerate((wq_ref, wk_ref, wv_ref)):
            x = contract(b_ref[m, i], ref[:, m * w : (m + 1) * w], 1, 1)
            part = x if part is None else part + x
        qv_ref[0:1, m * w : (m + 1) * w] = column_sum(b_ref[m, 0])
        qv_ref[1:2, m * w : (m + 1) * w] = column_sum(b_ref[m, 2])

    @pl.when(step == 0)
    def _():
        total[...] = part

    @pl.when(step > 0)
    def _():
        total[...] += part

    @pl.when(step == pl.num_programs(0) - 1)
    def _():
        dv, gain, bias = norm_back(total[...], n_ref[...], r_ref[...], g_ref[...])
        grad = m_ref[...] + dv
        grad_ref[...] = grad
        half = low_ref.shape[1]
        low_ref[0] = grad[:half].astype(bf16)
        low_ref[1] = grad[half:].astype(bf16)
        put_sums(sums_ref, gain, bias, column_sum(grad))


def qkv_backward(back, w_qkv, middle_grad, n1, r1, gain):
    members, _, t, w = back.shape
    d = members * w
    at_once = max(2, 128 // w)
    block = at_once * w
    shift = d // block
    full = spec((t, d), lambda i: (0, 0))
    weight = [spec((d, block), lambda i, s=s: (0, s * shift + i)) for s in range(3)]
    shape = jax.ShapeDtypeStruct
    return pl.pallas_call(
        qkv_backward_kernel,
        grid=(members // at_once,),
        in_specs=[spec((at_once, 3, t, w), lambda i: (i, 0, 0, 0))] + weight + [
            full, full, spec((t, 1), lambda i: (0, 0)), spec((1, d), lambda i: (0, 0)),
        ],
        out_specs=[
            full, spec((2, t // 2, d), lambda i: (0, 0, 0)), spec((8, d), lambda i: (0, 0)),
            spec((8, block), lambda i: (0, i)),
        ],
        out_shape=[
            shape((t, d), f32), shape((2, t // 2, d), bf16), shape((8, d), f32), shape((8, d), f32),
        ],
        scratch_shapes=[pltpu.VMEM((t, d), f32)],
        compiler_params=pltpu.CompilerParams(vmem_limit_bytes=40 * MIB),
        cost_estimate=cost(6),
        name="qkv_backward",
    )(back, w_qkv, w_qkv, w_qkv, middle_grad, n1, r1, gain.reshape(1, d))


def grad_heads_kernel(d_ref, n_ref, *rest):
    out_ref = rest[-1]
    rows = d_ref.shape[2]
    for i in range(3):
        total = rest[0][i] if len(rest) == 2 else jnp.zeros(out_ref.shape[1:], f32)
        for m in range(d_ref.shape[0]):
            total += contract(d_ref[m, i], n_ref[m * rows : (m + 1) * rows, :], 0, 0)
        out_ref[i] = total.astype(out_ref.dtype)


def grad_heads(d, normed_all, add, kind):
    members, _, rows, width = d.shape
    dim = normed_all.shape[1]
    shape = (3, width, dim)
    out = spec((3, width, dim // 4), lambda i: (0, 0, i))
    extra = [] if add is None else [add]
    return pl.pallas_call(
        grad_heads_kernel,
        grid=(4,),
        in_specs=[
            spec(d.shape, lambda i: (0, 0, 0, 0)),
            spec((members * rows, dim // 4), lambda i: (0, i)),
        ]
        + [out] * len(extra),
        out_specs=out,
        out_shape=jax.ShapeDtypeStruct(shape, kind),
        compiler_params=pltpu.CompilerParams(vmem_limit_bytes=16 * MIB),
        cost_estimate=cost(5),
        name="grad_heads",
    )(d, normed_all, *extra)


def take_kernel(table, *refs):
    for i in range(refs[-1].shape[0]):
        total = refs[0][table[i]].astype(f32)
        for r in refs[1:-1]:
            total = total + r[table[i]].astype(f32)
        refs[-1][i] = total.astype(bf16)


def take(terms, table):
    shape = terms[0].shape
    count = table.shape[0]
    return pl.pallas_call(
        take_kernel,
        grid_spec=pltpu.PrefetchScalarGridSpec(
            num_scalar_prefetch=1,
            grid=(1,),
            in_specs=[spec(shape, lambda i, t: (0, 0, 0))] * len(terms),
            out_specs=spec((count,) + shape[1:], lambda i, t: (0, 0, 0)),
        ),
        out_shape=jax.ShapeDtypeStruct((count,) + shape[1:], bf16),
        compiler_params=pltpu.CompilerParams(vmem_limit_bytes=8 * MIB),
        cost_estimate=cost(3),
        name="take",
    )(table, *terms)


def unit_tables(bands, x_count, width, dim):
    members = bands // 2
    unit = math.gcd(HD, 3 * dim // bands)
    per_band = 3 * dim // bands // unit
    made, slots, place = [], [], {}
    for g in range(members):
        units = [(b * dim + g * width) // unit + i for b in range(3) for i in range(width // unit)]
        by_low = [[] for _ in range(members)]
        for local, u in enumerate(units):
            band = u // per_band
            core, x, zl = band % 2, band // 2 % x_count, band // (2 * x_count) % 2
            low = (core * 2 + zl) * x_count + x
            place[u] = (g, len(by_low[low]))
            by_low[low].append(local)
        made.append(by_low)
    most = max(len(l) for by_low in made for l in by_low)
    send = np.zeros((members, members * most), np.int32)
    for g, by_low in enumerate(made):
        for low, locals_ in enumerate(by_low):
            for m, local in enumerate(locals_):
                send[g, low * most + m] = local
    keep = np.zeros((members, 2, per_band), np.int32)
    for u, (g, m) in place.items():
        band = u // per_band
        core, x, zl = band % 2, band // 2 % x_count, band // (2 * x_count) % 2
        low = (core * 2 + zl) * x_count + x
        keep[low, band // members, u % per_band] = g * most + m
    return unit, send, keep


def norm_parts(v):
    centred = v - jnp.mean(v, axis=-1, keepdims=True)
    r = lax.rsqrt(jnp.mean(centred * centred, axis=-1, keepdims=True) + EPS)
    return centred * r, r


def norm_back(dy, n, r, gain):
    dyg = dy * gain
    mean_one = jnp.mean(dyg, axis=-1, keepdims=True)
    mean_two = jnp.mean(dyg * n, axis=-1, keepdims=True)
    dv = r * (dyg - mean_one - n * mean_two)
    return dv, jnp.sum(dy * n, axis=0, keepdims=True), jnp.sum(dy, axis=0, keepdims=True)


def gelu(x):
    return 0.5 * x * (1.0 + jnp.tanh(GELU_A * (x + GELU_B * x * x * x)))


def gelu_slope(x):
    t = jnp.tanh(GELU_A * (x + GELU_B * x * x * x))
    return 0.5 * (1.0 + t) + 0.5 * x * (1.0 - t * t) * (GELU_A * (1.0 + 3.0 * GELU_B * x * x))


def dot(a, b):
    return jnp.dot(a, b, preferred_element_type=f32)


def dot_t(a, b):
    return contract(a, b, 1, 1)


def swap(x, axis):
    return lax.ppermute(x, axis, SWAP)


def pin(x, *first):
    return lax.optimization_barrier((x,) + first)[0]


def total(terms):
    out = terms[0].astype(f32)
    for t in terms[1:]:
        out = out + t.astype(f32)
    return out


class Share:
    def __init__(self, terms, names):
        self.terms = list(terms)
        self.names = list(names)

    def halve(self, axis, *first):
        if axis not in self.names:
            return self.terms[-1]
        dim = self.names.index(axis)
        i = lax.axis_index(axis)
        terms = [pin(t, *first) if first else t for t in self.terms[-1:]] + self.terms[:-1]
        there = [lax.dynamic_index_in_dim(t, 1 - i, dim, keepdims=False) for t in terms]
        self.terms = [lax.dynamic_index_in_dim(t, i, dim, keepdims=False) for t in terms]
        self.names.remove(axis)
        sent = total(there).astype(bf16)
        self.terms.append(swap(sent, axis))
        return sent


def body(
    fields,
    lead_bucket,
    cotangent,
    lead_table,
    ln1_gain,
    ln1_bias,
    w_qkv,
    q_bias,
    v_bias,
    w_out,
    out_bias,
    ln2_gain,
    ln2_bias,
    w_up,
    up_bias,
    w_down,
    down_bias,
    *,
    axes,
    x_axes,
    samp_count,
):
    band = tuple(axes)
    low = ("core", "zl") + x_axes[::-1]
    members = 2 ** len(low)
    order = x_axes + ("zl", "core")
    D = w_out.shape[0]
    W = D // members
    half = fields.shape[1]
    rows = 2 * half
    two = samp_count == 2
    zh = lax.axis_index("zh")
    me = lax.axis_index(low)

    def pick(x, i):
        return lax.dynamic_index_in_dim(x, i, 0, keepdims=False)

    def to_sample(x):
        return jnp.concatenate([pick(x, zh), swap(pick(x, 1 - zh), "zh")])

    def to_band(x):
        own = x[:half]
        other = swap(x[half:].astype(bf16), "zh").astype(x.dtype)
        return jnp.where(zh == 0, jnp.stack([own, other]), jnp.stack([other, own]))

    def gather(x):
        if len(x_axes) == 1:
            x_axis = x_axes[0]
            cut = x.shape[0] // 2
            by_x = swap(x, x_axis)
            by_z = swap(x, "zl")
            far = [swap(by_x[:cut], "zl"), swap(by_z[cut:], x_axis)]
            pieces = [(x, 0, 0), (by_x, 1, 0), (by_z, 2, 0), (far[0], 3, 0), (far[1], 3, cut)]
            pieces += [(swap(p, "core"), 4 + k, o) for p, k, o in pieces]
        else:
            pieces = [(x, 0, 0)]
            for bit, axis in enumerate(order):
                pieces += [(swap(p, axis), k + 2**bit, 0) for p, k, _ in pieces]
        out = jnp.zeros((members * rows, D), bf16)
        for piece, k, offset in pieces:
            out = lax.dynamic_update_slice(out, piece, ((me ^ k) * rows + offset, 0))
        return out

    lead_row = pick(lead_table, pick(lead_bucket, zh)).astype(f32)
    carried = to_sample(fields).astype(f32)

    def member_columns(x, block):
        return lax.dynamic_slice_in_dim(x, block * D + me * W, W, x.ndim - 1)

    kept = []
    inputs = carried + lead_row
    n1, r1 = norm_parts(inputs)
    normed = (n1 * ln1_gain + ln1_bias).astype(bf16)
    weights = (w_out, out_bias, ln2_gain, ln2_bias, w_up, up_bias, w_down, down_bias, lead_row, ln1_gain, ln1_bias)
    for index in range(STEPS):
        normed_all = gather(normed)
        queries = (dot(normed, w_qkv[:, :D]) + q_bias).astype(bf16)
        if index == 0:
            out_grad = to_sample(pin(cotangent, normed_all))
        attended = attend(queries, normed_all, w_qkv, v_bias)
        if index == 0:
            attended, out_grad = pin((attended, out_grad))
        last = index == STEPS - 1
        n2, r2, normed_two, hidden, activated, *after = block_forward(inputs, attended, weights, last)
        kept.append((n1, r1, normed_all, attended, n2, r2, normed_two, hidden, activated))
        if not last:
            inputs, n1, r1, normed = after
    carried = after[0]
    result = to_band(carried)

    grad = out_grad
    small = None
    core = lax.axis_index("core")
    y = lax.axis_index("samp")
    bands = 2 ** len(axes)
    names = axes[:-1]
    cube = (2,) * len(names)
    later = None
    w_heads = None
    unit, send_table, keep_table = unit_tables(bands, 2 ** len(x_axes), W, D)
    def split_rows(x, rows_two):
        n, r, c = x.shape
        return x.reshape(cube + ((2, r // 2) if rows_two else (r,)) + (c,))

    own_weight = jnp.concatenate([member_columns(w_qkv, i) for i in range(3)], axis=1)
    own_bias = jnp.concatenate([member_columns(q_bias, 0), jnp.zeros((W,), f32), member_columns(v_bias, 0)])

    def own_part(index):
        own = (dot(kept[index][2], own_weight) + own_bias).astype(bf16)
        return own[:, :W], own[:, W : 2 * W], own[:, 2 * W :]

    owns = {}
    for index in reversed(range(STEPS)):
        n1, r1, normed_all, attended, n2, r2, normed_two, hidden, activated = kept[index]
        last = index == 0
        if last:
            left, right = (later[0], down_grad), (later[1], activated)
            y_other, y_own = grad_rows(core, left, right, bands, 0, 2)
            y_core = swap(y_other, "core")
            right = (later[1], pin(activated, y_other))
            x_other, x_own = grad_rows(core, left, right, bands, 1, 2)
            x_core = swap(x_other, "core")
            grad = pin(grad, x_other)
            grads = (later[2], later[3], normed_two)
        else:
            down_grad = grad.astype(bf16)
            grads = ()
        hidden_grad, hidden_sum, middle_grad, branch_grad, sent, sums_two, *ups = block_backward(
            core, grad, hidden, w_down, w_up, w_out, n2, r2, ln2_gain, members, grads
        )
        if last:
            (y_own, y_core), (x_own, x_core) = pin(((y_own, y_core), (x_own, x_core)), hidden_grad)
            down_y = Share([split_rows(y_own, two), split_rows(y_core, two)], names + ("samp",) * two)
            down_x = Share([split_rows(x_own, two), split_rows(x_core, two)], names + ("samp",) * two)
            first = (down_y.halve("samp"), down_x.halve(x_axes[0]))
            sent = pin(sent, *first)
        own_grad = lax.all_to_all(sent, low, 0, 0, tiled=True).reshape(members * rows, W)
        if last:
            z_other, x_other, z_own, x_own = ups
            z_core = swap(z_other, "core")
            x_other, x_own = grad_out(
                core, (later[4], pin(branch_grad, sent)), (later[5], attended), bands, x_other, x_own
            )
            x_core = swap(x_other, "core")
            own_grad, z_own, z_core = pin((own_grad, z_own, z_core), x_other)
            z_share = Share([split_rows(z_own, two), split_rows(z_core, two)], names + ("samp",) * two)
            x_share = Share([split_rows(t, two) for t in (x_own, x_core)], names + ("samp",) * two)
            sent = [z_share.halve("zh"), x_share.halve(x_axes[0])]
            own_grad = pin(own_grad, *sent)
            heads = W // HD
            d_heads = attend_back(*owns[0], own_grad, members, range((heads + 1) // 2))
            waits = pin((own_grad, d_heads, down_y.terms[-1], down_x.terms[-1]))
            own_grad, d_heads, down_y.terms[-1], down_x.terms[-1] = waits
            sent = [down_y.halve("zl"), down_x.halve("samp")]
            if heads > 1:
                own_grad, d_heads = pin((own_grad, d_heads), *sent)
                d_heads = attend_back(*owns[0], own_grad, members, range(heads // 2, heads), d_heads)
            waits = pin((d_heads, z_share.terms[-1], x_share.terms[-1], down_y.terms[-1], down_x.terms[-1]))
            d_heads, z_share.terms[-1], x_share.terms[-1], down_y.terms[-1], down_x.terms[-1] = waits
            sent = [x_share.halve("samp"), z_share.halve("samp")] + [down_y.halve(a) for a in x_axes]
            sent += [down_x.halve(a) for a in x_axes[1:] + ("zl",)]
            d_heads = pin(d_heads, *sent)
        else:
            own_grad = pin(own_grad, result)
            later = (down_grad, activated, hidden_grad, normed_two, branch_grad, attended)
            owns[index] = own_part(index)
            d_heads = attend_back(*owns[index], own_grad, members)
        back = lax.all_to_all(d_heads, low, 0, 0, tiled=True)
        w_heads = grad_heads(d_heads, normed_all, w_heads, bf16 if last else f32)
        if last:
            units = w_heads.reshape(-1, unit, D)
            if two:
                there = lax.dynamic_slice_in_dim(units, (1 - y) * (D // 2), D // 2, 2)
                here = lax.dynamic_slice_in_dim(units, y * (D // 2), D // 2, 2)
                units = [here, swap(there, "samp")]
            else:
                there, units = units, [units]
            back = pin(back, there)
            waits = pin((x_share.terms[-1], z_share.terms[-1], down_y.terms[-1], down_x.terms[-1]), back)
            x_share.terms[-1], z_share.terms[-1], down_y.terms[-1], down_x.terms[-1] = waits
            sent = [x_share.halve(a) for a in x_axes[1:] + ("zl",)] + [z_share.halve("zl")]
            sent += [down_y.halve("zh"), down_x.halve("zh")]
            units[-1] = pin(units[-1], *sent)
            outgoing = take(units, pick(jnp.asarray(send_table), me))
            incoming = lax.all_to_all(outgoing, low, 0, 0, tiled=True)
            back = pin(back, outgoing)
        else:
            owns[0] = own_part(0)
            back = pin(back, w_heads, *owns[0])
        grad, low_grad, sums_one, sums_qv = qkv_backward(back, w_qkv, middle_grad, n1, r1, ln1_gain)
        down_grad = low_grad.reshape(rows, D)
        step_small = (sums_one[:3], sums_qv[:2], sums_two[:4], hidden_sum)
        small = step_small if small is None else tuple(a + b for a, b in zip(small, step_small))
    fields_own = grad[:half]
    fields_sent = low_grad[1]
    fields_other = swap(fields_sent, "zh")
    one, qv, two_sums, up_sum = small
    samples = 2 * samp_count
    slot = 2 * y + zh
    mine = lax.broadcasted_iota(jnp.int32, (samples, 1), 0) == slot
    leads = jnp.where(mine, one[2:3], 0.0)
    lane = lax.broadcasted_iota(jnp.int32, (bands, 1, D // bands), 2) == slot
    bucket = jnp.where(lane & (me == 0) & (zh == slot % 2), pick(lead_bucket, zh).astype(f32), 0.0)
    vectors = jnp.concatenate([one[:2], qv, two_sums, leads])
    vectors = vectors.reshape(-1, bands, D // bands).transpose(1, 0, 2)
    ups = up_sum.reshape(bands, -1, D // bands)
    vectors = jnp.concatenate([vectors, ups, bucket], axis=1)
    incoming, vectors = pin((incoming, vectors), fields_sent)
    vectors = lax.all_to_all(vectors, band, 0, 0, tiled=True)

    def both(x):
        x = x.astype(bf16)
        if not two:
            return lax.psum(x, "samp").astype(f32)
        other = swap(x, "samp")
        return jnp.concatenate([jnp.where(y == 0, x, other), jnp.where(y == 0, other, x)]).astype(f32)

    def both_cut(x, n):
        if not two:
            x = both(x)
            return x[:n], x[n:]
        x = x.astype(bf16)
        other = swap(x, "samp")
        first, second = jnp.where(y == 0, x, other), jnp.where(y == 0, other, x)
        x = jnp.concatenate([first, second]).astype(f32)
        return x[:n], x[n:]

    waits = pin((z_share.terms[-1], x_share.terms[-1], down_y.terms[-1], down_x.terms[-1], incoming), fields_sent)
    z_share.terms[-1], x_share.terms[-1], down_y.terms[-1], down_x.terms[-1], incoming = waits
    sent = [x_share.halve("zh")] + [z_share.halve(a) for a in x_axes]
    down = jnp.concatenate([total(down_y.terms), total(down_x.terms)], axis=1).astype(bf16)
    incoming, fields_other, x_share.terms[-1], z_share.terms[-1], vectors = pin(
        (incoming, fields_other, x_share.terms[-1], z_share.terms[-1], vectors), down, *sent
    )
    vectors = jnp.sum(vectors, axis=0)
    vectors = vectors + swap(vectors, "samp") if two else lax.psum(vectors, "samp")
    keep_table = pick(jnp.asarray(keep_table), me)
    other = swap(take([incoming], pick(keep_table, 1 - zh)), "zh")
    own = take([incoming], pick(keep_table, zh))
    own = total([own, other]).astype(bf16).reshape(3 * D // bands, -1)
    if two:
        other = swap(own, "samp")
        own = jnp.concatenate([jnp.where(y == 0, own, other), jnp.where(y == 0, other, own)], axis=1)
    else:
        own = lax.psum(own, "samp")
    w_qkv_grad = own.astype(f32).T

    w_down_grad = both(down).T
    n_up = w_up.shape[1] // bands
    bottom = both_cut(total(x_share.terms), n_up // 2)
    w_out_grad = bottom[1].T
    w_up_grad = jnp.concatenate([both(total(z_share.terms)), bottom[0]]).T
    fields_other = fields_other.astype(f32)
    fields_grad = jnp.where(
        zh == 0, jnp.stack([fields_own, fields_other]), jnp.stack([fields_other, fields_own])
    )

    leads = vectors[8 : 8 + samples]
    up_grad = vectors[8 + samples : -1].reshape(-1)
    buckets = vectors[-1, :samples].astype(jnp.int32)
    one_hot = (buckets[:, None] == jnp.arange(lead_table.shape[0], dtype=jnp.int32)[None, :]).astype(f32)
    lead_grad = jnp.dot(one_hot.T, leads, precision=lax.Precision.HIGHEST)
    g = [vectors[i] for i in (0, 1, 2, 3, 6, 4, 5)] + [up_grad, vectors[7]]
    return (
        result,
        fields_grad,
        lead_grad,
        g[0],
        g[1],
        w_qkv_grad,
        g[2],
        g[3],
        w_out_grad,
        g[4],
        g[5],
        g[6],
        w_up_grad,
        g[7],
        w_down_grad,
        g[8],
    )


def solution(mesh):
    samp_count, band_count = mesh.shape["samp"], mesh.shape["band"]
    x_axes = tuple(f"x{i}" for i in range((band_count // 8).bit_length() - 1))
    axes = ("zh", "zl") + x_axes + ("core",)
    assert 2 ** len(axes) == band_count
    fine = Mesh(mesh.devices.reshape((samp_count,) + (2,) * len(axes)), ("samp",) + axes)
    tokens = P("samp", axes, None)
    columns, vector = P(None, axes), P(axes)
    in_specs = (tokens, P("samp"), tokens) + (P(),) * 14
    out_specs = (
        tokens,
        tokens,
        columns,
        vector,
        vector,
        columns,
        vector,
        vector,
        columns,
        vector,
        vector,
        vector,
        columns,
        vector,
        columns,
        vector,
    )
    run = functools.partial(body, axes=axes, x_axes=x_axes, samp_count=samp_count)
    return jax.shard_map(run, mesh=fine, in_specs=in_specs, out_specs=out_specs, check_vma=False)
```

```python
import functools
import math

import jax
import jax.numpy as jnp
import numpy as np
from jax import lax
from jax.experimental import pallas as pl
from jax.experimental.pallas import tpu as pltpu
from jax.sharding import Mesh
from jax.sharding import PartitionSpec as P

HD = 64
STEPS = 2
EPS = 1e-05
EXP_SCALE = 0.125 * 1.4426950408889634
GELU_A = 0.7978845608028654
GELU_B = 0.044715
MIB = 2**20
SWAP = [(0, 1), (1, 0)]
f32 = jnp.float32
bf16 = jnp.bfloat16


def cost(us):
    return pl.CostEstimate(flops=int(us * 1.15e9), bytes_accessed=1000, transcendentals=0)


def contract(a, b, a_dim, b_dim):
    return lax.dot_general(a, b, (((a_dim,), (b_dim,)), ((), ())), preferred_element_type=f32)


def head_part(x, h, heads):
    if heads == 1:
        return x
    lane = lax.broadcasted_iota(jnp.int32, x.shape, 1)
    return jnp.where(lane // HD == h, x, jnp.zeros_like(x))


def attend_kernel(q_ref, n_ref, wk_ref, wv_ref, b_ref, o_ref):
    normed = n_ref[...]
    keys = contract(normed, wk_ref[...], 1, 0).astype(bf16)
    values = (contract(normed, wv_ref[...], 1, 0) + b_ref[...]).astype(bf16)
    pair = 2 * HD
    for start in range(0, q_ref.shape[1], pair):
        q, k, v = q_ref[:, start : start + pair], keys[:, start : start + pair], values[:, start : start + pair]
        out = None
        for h in range(2):
            s = contract(head_part(q, h, 2), k, 1, 1)
            top = jnp.max(s, axis=-1, keepdims=True)
            e = jnp.exp2((s - top) * EXP_SCALE)
            total = jnp.sum(e, axis=-1, keepdims=True)
            o = head_part(contract(e.astype(bf16), v, 1, 0) / total, h, 2)
            out = o if out is None else out + o
        o_ref[:, start : start + pair] = out.astype(bf16)


def attend(q, normed_all, w_qkv, v_bias):
    rows, width = q.shape
    count = normed_all.shape[0]
    block = 4 * HD
    own = spec((rows, block), lambda j: (0, j))
    shift = width // block
    return pl.pallas_call(
        attend_kernel,
        grid=(width // block,),
        in_specs=[
            own,
            spec((count, width), lambda j: (0, 0)),
            spec((width, block), lambda j: (0, shift + j)),
            spec((width, block), lambda j: (0, 2 * shift + j)),
            spec((1, block), lambda j: (0, j)),
        ],
        out_specs=own,
        out_shape=jax.ShapeDtypeStruct((rows, width), bf16),
        compiler_params=pltpu.CompilerParams(vmem_limit_bytes=40 * MIB),
        cost_estimate=cost(24),
        name="attend",
    )(q, normed_all, w_qkv, w_qkv, v_bias.reshape(1, width))


def attend_back_kernel(q_ref, k_ref, v_ref, do_ref, *rest, heads, some):
    out_ref, dk_sum, dv_sum = rest[-3:]
    step = pl.program_id(0)
    rows = q_ref.shape[0]

    @pl.when(step == 0)
    def _():
        dk_sum[...] = jnp.zeros_like(dk_sum)
        dv_sum[...] = jnp.zeros_like(dv_sum)

    q, k, v, do = q_ref[...], k_ref[...], v_ref[...], do_ref[...]
    dq = None
    for h in some:
        qh, doh = head_part(q, h, heads), head_part(do, h, heads)
        s = contract(qh, k, 1, 1)
        dp = contract(doh, v, 1, 1)
        top = jnp.max(s, axis=-1, keepdims=True)
        e = jnp.exp2((s - top) * EXP_SCALE)
        inverse = 1.0 / jnp.sum(e, axis=-1, keepdims=True)
        inner = jnp.sum(e * dp, axis=-1, keepdims=True) * inverse
        p = e * inverse
        ds = (p * (dp - inner)).astype(bf16)
        part = head_part(contract(ds, k, 1, 0), h, heads)
        dq = part if dq is None else dq + part
        dk_sum[...] += contract(ds, qh, 0, 0)
        dv_sum[...] += contract(p.astype(bf16), doh, 0, 0)

    def put(m, i, x):
        if len(rest) == 4:
            x = x + rest[0][m, i].astype(f32)
        out_ref[m, i] = x.astype(bf16)

    put(step, 0, dq * 0.125)

    @pl.when(step == pl.num_programs(0) - 1)
    def _():
        for m in range(out_ref.shape[0]):
            put(m, 1, dk_sum[m * rows : (m + 1) * rows, :] * 0.125)
            put(m, 2, dv_sum[m * rows : (m + 1) * rows, :])


def attend_back(q, k, v, do, members, some=None, add=None):
    count, width = q.shape
    rows = count // members
    heads = width // HD
    part = pl.BlockSpec((rows, width), lambda i: (i, 0))
    full = pl.BlockSpec((count, width), lambda i: (0, 0))
    shape = (members, 3, rows, width)
    out = pl.BlockSpec(shape, lambda i: (0, 0, 0, 0))
    extra = [] if add is None else [add]
    return pl.pallas_call(
        functools.partial(attend_back_kernel, heads=heads, some=some or range(heads)),
        grid=(members,),
        in_specs=[part, full, full, part] + [out] * len(extra),
        out_specs=out,
        out_shape=jax.ShapeDtypeStruct(shape, bf16),
        scratch_shapes=[pltpu.VMEM((count, width), f32), pltpu.VMEM((count, width), f32)],
        compiler_params=pltpu.CompilerParams(vmem_limit_bytes=60 * MIB),
        cost_estimate=cost(33 if some is None else 17),
        name="attend_back",
    )(q, k, v, do, *extra)


def spec(block, index):
    return pl.BlockSpec(block, index)


def grad_rows_kernel(c_ref, l1, l0, r1, r0, other_ref, own_ref, sums):
    sums[...] = contract(l1[...], r1[...], 0, 0) + contract(l0[...], r0[...], 0, 0)
    count, n, _ = own_ref.shape
    for j in range(count):
        for ref, core in ((other_ref, 1 - c_ref[0]), (own_ref, c_ref[0])):
            ref[j] = sums[pl.ds(pl.multiple_of((2 * j + core) * n, n), n), :].astype(bf16)


def grad_rows(core, left, right, bands, part, parts):
    tokens, m = left[0].shape
    n = right[0].shape[1] // parts
    block = min(n, 512)
    first = part * (n // block)
    out = spec((bands // 2, m // bands, block), lambda j, c: (0, 0, j))
    whole = spec((tokens, m), lambda j, c: (0, 0))
    part = spec((tokens, block), lambda j, c: (0, first + j))
    return pl.pallas_call(
        grad_rows_kernel,
        grid_spec=pltpu.PrefetchScalarGridSpec(
            num_scalar_prefetch=1,
            grid=(n // block,),
            in_specs=[whole, whole, part, part],
            out_specs=[out, out],
            scratch_shapes=[pltpu.VMEM((m, block), f32)],
        ),
        out_shape=[jax.ShapeDtypeStruct((bands // 2, m // bands, n), bf16)] * 2,
        compiler_params=pltpu.CompilerParams(vmem_limit_bytes=16 * MIB),
        cost_estimate=cost(8),
        name="grad_rows",
    )(core.reshape(1), *left, *right)


def block_forward_kernel(
    x_ref, a_ref, wo_ref, bo_ref, g_ref, b_ref, wu_ref, bu_ref, wd_ref, bd_ref, lead_ref, g1_ref, b1_ref,
    n2_ref, r2_ref, low2_ref, hidden_ref, act_ref, *rest, last
):
    total = rest[-1]
    step = pl.program_id(0)

    @pl.when(step == 0)
    def _():
        middle = x_ref[...] + contract(a_ref[...], wo_ref[...], 1, 0) + bo_ref[...]
        n, r = norm_parts(middle)
        n2_ref[...] = n
        r2_ref[...] = r
        low2_ref[...] = (n * g_ref[...] + b_ref[...]).astype(bf16)
        total[...] = middle + bd_ref[...]

    hidden = contract(low2_ref[...], wu_ref[...], 1, 0) + bu_ref[...]
    hidden_ref[...] = hidden
    act = gelu(hidden).astype(bf16)
    act_ref[...] = act
    total[...] += contract(act, wd_ref[...], 1, 0)

    @pl.when(step == pl.num_programs(0) - 1)
    def _():
        carried = total[...]
        if last:
            rest[0][...] = carried.astype(bf16)
        else:
            x = carried + lead_ref[...]
            n, r = norm_parts(x)
            rest[0][...] = x
            rest[1][...] = n
            rest[2][...] = r
            rest[3][...] = (n * g1_ref[...] + b1_ref[...]).astype(bf16)


def block_forward(inputs, attended, weights, last):
    w_out, out_bias, ln2_gain, ln2_bias, w_up, up_bias, w_down, down_bias, lead, ln1_gain, ln1_bias = weights
    t, d = inputs.shape
    f = w_up.shape[1]
    block = 512
    row = lambda v: v.reshape(1, -1)
    full = spec((t, d), lambda i: (0, 0))
    vec = spec((1, d), lambda i: (0, 0))
    one = spec((t, 1), lambda i: (0, 0))
    wide = spec((t, block), lambda i: (0, i))
    shape = jax.ShapeDtypeStruct
    outs = [full, one, full, wide, wide] + ([full] if last else [full, full, one, full])
    shapes = [shape((t, d), f32), shape((t, 1), f32), shape((t, d), bf16), shape((t, f), f32), shape((t, f), bf16)]
    shapes += [shape((t, d), bf16)] if last else [
        shape((t, d), f32), shape((t, d), f32), shape((t, 1), f32), shape((t, d), bf16)
    ]
    return pl.pallas_call(
        functools.partial(block_forward_kernel, last=last),
        grid=(f // block,),
        in_specs=[
            full, full, spec((d, d), lambda i: (0, 0)), vec, vec, vec,
            spec((d, block), lambda i: (0, i)), spec((1, block), lambda i: (0, i)),
            spec((block, d), lambda i: (i, 0)), vec, vec, vec, vec,
        ],
        out_specs=outs,
        out_shape=shapes,
        scratch_shapes=[pltpu.VMEM((t, d), f32)],
        compiler_params=pltpu.CompilerParams(vmem_limit_bytes=40 * MIB),
        cost_estimate=cost(12),
        name="block_forward",
    )(
        inputs, attended, w_out, row(out_bias), row(ln2_gain), row(ln2_bias), w_up, row(up_bias), w_down,
        row(down_bias), row(lead), row(ln1_gain), row(ln1_bias),
    )


def put_sums(ref, *sums):
    for i, v in enumerate(sums):
        ref[i : i + 1, :] = v


def column_sum(x):
    return jnp.sum(x.astype(f32), axis=0, keepdims=True)


def block_backward_kernel(c_ref, grad_ref, h_ref, wd_ref, wu_ref, wo_ref, n_ref, r_ref, g_ref, *rest, grads, bands):
    if grads:
        l1_ref, x1_ref, x0_ref = rest[:3]
        z_other, x_other, z_own, x_own = rest[9:13]
        sums, rest = rest[14], rest[3:9] + rest[13:14]
    hg_ref, hsum_ref, middle_ref, branch_ref, sent_ref, sums_ref, total = rest
    step = pl.program_id(0)
    down = grad_ref[...].astype(bf16)
    low = (gelu_slope(h_ref[...]) * contract(down, wd_ref[...], 1, 1)).astype(bf16)
    hg_ref[...] = low
    hsum_ref[...] = column_sum(low)
    part = contract(low, wu_ref[...], 1, 1)
    if grads:
        sums[...] = contract(l1_ref[...], x1_ref[...], 0, 0) + contract(low, x0_ref[...], 0, 0)
        pairs = z_own.shape[0]
        n = sums.shape[0] // (2 * pairs)
        for q in range(pairs):
            for z, x, core in ((z_other, x_other, 1 - c_ref[0]), (z_own, x_own, c_ref[0])):
                start = pl.multiple_of((2 * q + core) * n, n)
                z[q] = sums[pl.ds(start, n // 2), :].astype(bf16)
                x[q] = sums[pl.ds(start + n // 2, n // 2), :].astype(bf16)

    @pl.when(step == 0)
    def _():
        total[...] = part

    @pl.when(step > 0)
    def _():
        total[...] += part

    @pl.when(step == pl.num_programs(0) - 1)
    def _():
        dv, gain, bias = norm_back(total[...], n_ref[...], r_ref[...], g_ref[...])
        middle = grad_ref[...] + dv
        middle_ref[...] = middle
        branch = middle.astype(bf16)
        branch_ref[...] = branch
        put_sums(sums_ref, gain, bias, column_sum(branch), column_sum(down))
        w = sent_ref.shape[2]
        attended = contract(branch, wo_ref[...], 1, 1).astype(bf16)
        for m in range(sent_ref.shape[0]):
            sent_ref[m] = attended[:, m * w : (m + 1) * w]


def block_backward(core, grad, hidden, w_down, w_up, w_out, n2, r2, gain, members, grads=()):
    t, d = grad.shape
    f = hidden.shape[1]
    block = 512
    bands = 2 * members
    full = spec((t, d), lambda i, c: (0, 0))
    wide = spec((t, block), lambda i, c: (0, i))
    sent = (members, t, d // members)
    shape = jax.ShapeDtypeStruct
    outs = [
        wide, spec((1, block), lambda i, c: (0, i)), full, full,
        spec(sent, lambda i, c: (0, 0, 0)), spec((8, d), lambda i, c: (0, 0)),
    ]
    shapes = [
        shape((t, f), bf16), shape((1, f), f32), shape((t, d), f32), shape((t, d), bf16),
        shape(sent, bf16), shape((8, d), f32),
    ]
    scratch = [pltpu.VMEM((t, d), f32)]
    if grads:
        n = f // bands
        pairs = block // (2 * n)
        part = spec((pairs, n // 2, d), lambda i, c: (i, 0, 0))
        outs += [part] * 4
        shapes += [shape((bands // 2, n // 2, d), bf16), shape((bands // 2, n // 2 + d // bands, d), bf16)] * 2
        scratch += [pltpu.VMEM((block, d), f32)]
    return pl.pallas_call(
        functools.partial(block_backward_kernel, grads=bool(grads), bands=bands),
        grid_spec=pltpu.PrefetchScalarGridSpec(
            num_scalar_prefetch=1,
            grid=(f // block,),
            in_specs=[
                full, wide, spec((block, d), lambda i, c: (i, 0)), spec((d, block), lambda i, c: (0, i)),
                spec((d, d), lambda i, c: (0, 0)), full, spec((t, 1), lambda i, c: (0, 0)),
                spec((1, d), lambda i, c: (0, 0)),
            ] + [wide, full, full][: len(grads)],
            out_specs=outs,
            scratch_shapes=scratch,
        ),
        out_shape=shapes,
        compiler_params=pltpu.CompilerParams(vmem_limit_bytes=48 * MIB),
        cost_estimate=cost(18 if grads else 14),
        name="block_backward",
    )(core.reshape(1), grad, hidden, w_down, w_up, w_out, n2, r2, gain.reshape(1, d), *grads)


def grad_out_kernel(c_ref, l1, l0, r1, r0, _, __, other_ref, own_ref, sums, *, pairs):
    sums[...] = contract(l1[...], r1[...], 0, 0) + contract(l0[...], r0[...], 0, 0)
    n = own_ref.shape[1]
    for q in range(pairs):
        for ref, core in ((other_ref, 1 - c_ref[0]), (own_ref, c_ref[0])):
            ref[q] = sums[pl.ds(pl.multiple_of((2 * q + core) * n, n), n), :].astype(bf16)


def grad_out(core, left, right, bands, other, own):
    tokens, m = left[0].shape
    count, height, d = own.shape
    n = m // bands
    pairs = max(1, 256 // (2 * n))
    columns = spec((tokens, 2 * n * pairs), lambda j, c: (0, j))
    whole = spec((tokens, d), lambda j, c: (0, 0))
    out = spec((pairs, n, d), lambda j, c: (j, height // n - 1, 0))
    anywhere = pl.BlockSpec(memory_space=pl.ANY)
    return pl.pallas_call(
        functools.partial(grad_out_kernel, pairs=pairs),
        grid_spec=pltpu.PrefetchScalarGridSpec(
            num_scalar_prefetch=1,
            grid=(count // pairs,),
            in_specs=[columns, columns, whole, whole, anywhere, anywhere],
            out_specs=[out, out],
            scratch_shapes=[pltpu.VMEM((2 * n * pairs, d), f32)],
        ),
        out_shape=[jax.ShapeDtypeStruct(own.shape, bf16)] * 2,
        input_output_aliases={5: 0, 6: 1},
        compiler_params=pltpu.CompilerParams(vmem_limit_bytes=16 * MIB),
        cost_estimate=cost(3),
        name="grad_out",
    )(core.reshape(1), *left, *right, other, own)


def qkv_backward_kernel(b_ref, wq_ref, wk_ref, wv_ref, m_ref, n_ref, r_ref, g_ref, grad_ref, low_ref, sums_ref, qv_ref, total):
    step = pl.program_id(0)
    w = b_ref.shape[3]
    part = None
    for m in range(b_ref.shape[0]):
        for i, ref in enumerate((wq_ref, wk_ref, wv_ref)):
            x = contract(b_ref[m, i], ref[:, m * w : (m + 1) * w], 1, 1)
            part = x if part is None else part + x
        qv_ref[0:1, m * w : (m + 1) * w] = column_sum(b_ref[m, 0])
        qv_ref[1:2, m * w : (m + 1) * w] = column_sum(b_ref[m, 2])

    @pl.when(step == 0)
    def _():
        total[...] = part

    @pl.when(step > 0)
    def _():
        total[...] += part

    @pl.when(step == pl.num_programs(0) - 1)
    def _():
        dv, gain, bias = norm_back(total[...], n_ref[...], r_ref[...], g_ref[...])
        grad = m_ref[...] + dv
        grad_ref[...] = grad
        low_ref[...] = grad[grad.shape[0] - low_ref.shape[0] :].astype(bf16)
        put_sums(sums_ref, gain, bias, column_sum(grad))


def qkv_backward(back, w_qkv, middle_grad, n1, r1, gain, low):
    members, _, t, w = back.shape
    d = members * w
    at_once = max(2, 128 // w)
    block = at_once * w
    shift = d // block
    full = spec((t, d), lambda i: (0, 0))
    weight = [spec((d, block), lambda i, s=s: (0, s * shift + i)) for s in range(3)]
    shape = jax.ShapeDtypeStruct
    return pl.pallas_call(
        qkv_backward_kernel,
        grid=(members // at_once,),
        in_specs=[spec((at_once, 3, t, w), lambda i: (i, 0, 0, 0))] + weight + [
            full, full, spec((t, 1), lambda i: (0, 0)), spec((1, d), lambda i: (0, 0)),
        ],
        out_specs=[
            full, spec((low, d), lambda i: (0, 0)), spec((8, d), lambda i: (0, 0)),
            spec((8, block), lambda i: (0, i)),
        ],
        out_shape=[
            shape((t, d), f32), shape((low, d), bf16), shape((8, d), f32), shape((8, d), f32),
        ],
        scratch_shapes=[pltpu.VMEM((t, d), f32)],
        compiler_params=pltpu.CompilerParams(vmem_limit_bytes=60 * MIB),
        cost_estimate=cost(12),
        name="qkv_backward",
    )(back, w_qkv, w_qkv, w_qkv, middle_grad, n1, r1, gain.reshape(1, d))


def grad_heads_kernel(d_ref, n_ref, *rest):
    out_ref = rest[-1]
    rows = d_ref.shape[2]
    for i in range(3):
        total = rest[0][i] if len(rest) == 2 else jnp.zeros(out_ref.shape[1:], f32)
        for m in range(d_ref.shape[0]):
            total += contract(d_ref[m, i], n_ref[m * rows : (m + 1) * rows, :], 0, 0)
        out_ref[i] = total.astype(out_ref.dtype)


def grad_heads(d, normed_all, add, kind):
    members, _, rows, width = d.shape
    dim = normed_all.shape[1]
    shape = (3, width, dim)
    out = spec((3, width, dim // 4), lambda i: (0, 0, i))
    extra = [] if add is None else [add]
    return pl.pallas_call(
        grad_heads_kernel,
        grid=(4,),
        in_specs=[
            spec(d.shape, lambda i: (0, 0, 0, 0)),
            spec((members * rows, dim // 4), lambda i: (0, i)),
        ]
        + [out] * len(extra),
        out_specs=out,
        out_shape=jax.ShapeDtypeStruct(shape, kind),
        compiler_params=pltpu.CompilerParams(vmem_limit_bytes=16 * MIB),
        cost_estimate=cost(5),
        name="grad_heads",
    )(d, normed_all, *extra)


def take_kernel(table, *refs):
    for i in range(refs[-1].shape[0]):
        total = refs[0][table[i]].astype(f32)
        for r in refs[1:-1]:
            total = total + r[table[i]].astype(f32)
        refs[-1][i] = total.astype(bf16)


def take(terms, table):
    shape = terms[0].shape
    count = table.shape[0]
    return pl.pallas_call(
        take_kernel,
        grid_spec=pltpu.PrefetchScalarGridSpec(
            num_scalar_prefetch=1,
            grid=(1,),
            in_specs=[spec(shape, lambda i, t: (0, 0, 0))] * len(terms),
            out_specs=spec((count,) + shape[1:], lambda i, t: (0, 0, 0)),
        ),
        out_shape=jax.ShapeDtypeStruct((count,) + shape[1:], bf16),
        compiler_params=pltpu.CompilerParams(vmem_limit_bytes=8 * MIB),
        cost_estimate=cost(3),
        name="take",
    )(table, *terms)


def join_kernel(i_ref, own_ref, other_ref, out_ref):
    half = other_ref.shape[0]
    out_ref[i_ref[0]] = own_ref[:half]
    out_ref[1 - i_ref[0]] = other_ref[...].astype(f32)


def join(index, own, other):
    half, d = other.shape
    full = spec((half, d), lambda i, c: (0, 0))
    return pl.pallas_call(
        join_kernel,
        grid_spec=pltpu.PrefetchScalarGridSpec(
            num_scalar_prefetch=1,
            grid=(1,),
            in_specs=[full, full],
            out_specs=spec((2, half, d), lambda i, c: (0, 0, 0)),
        ),
        out_shape=jax.ShapeDtypeStruct((2, half, d), f32),
        compiler_params=pltpu.CompilerParams(vmem_limit_bytes=8 * MIB),
        cost_estimate=cost(2),
        name="join",
    )(index.reshape(1), own, other)


def unit_tables(bands, x_count, width, dim):
    members = bands // 2
    unit = math.gcd(HD, 3 * dim // bands)
    per_band = 3 * dim // bands // unit
    made, slots, place = [], [], {}
    for g in range(members):
        units = [(b * dim + g * width) // unit + i for b in range(3) for i in range(width // unit)]
        by_low = [[] for _ in range(members)]
        for local, u in enumerate(units):
            band = u // per_band
            core, x, zl = band % 2, band // 2 % x_count, band // (2 * x_count) % 2
            low = (core * 2 + zl) * x_count + x
            place[u] = (g, len(by_low[low]))
            by_low[low].append(local)
        made.append(by_low)
    most = max(len(l) for by_low in made for l in by_low)
    send = np.zeros((members, members * most), np.int32)
    for g, by_low in enumerate(made):
        for low, locals_ in enumerate(by_low):
            for m, local in enumerate(locals_):
                send[g, low * most + m] = local
    keep = np.zeros((members, 2, per_band), np.int32)
    for u, (g, m) in place.items():
        band = u // per_band
        core, x, zl = band % 2, band // 2 % x_count, band // (2 * x_count) % 2
        low = (core * 2 + zl) * x_count + x
        keep[low, band // members, u % per_band] = g * most + m
    return unit, send, keep


def norm_parts(v):
    centred = v - jnp.mean(v, axis=-1, keepdims=True)
    r = lax.rsqrt(jnp.mean(centred * centred, axis=-1, keepdims=True) + EPS)
    return centred * r, r


def norm_back(dy, n, r, gain):
    dyg = dy * gain
    mean_one = jnp.mean(dyg, axis=-1, keepdims=True)
    mean_two = jnp.mean(dyg * n, axis=-1, keepdims=True)
    dv = r * (dyg - mean_one - n * mean_two)
    return dv, jnp.sum(dy * n, axis=0, keepdims=True), jnp.sum(dy, axis=0, keepdims=True)


def gelu(x):
    return 0.5 * x * (1.0 + jnp.tanh(GELU_A * (x + GELU_B * x * x * x)))


def gelu_slope(x):
    t = jnp.tanh(GELU_A * (x + GELU_B * x * x * x))
    return 0.5 * (1.0 + t) + 0.5 * x * (1.0 - t * t) * (GELU_A * (1.0 + 3.0 * GELU_B * x * x))


def dot(a, b):
    return jnp.dot(a, b, preferred_element_type=f32)


def dot_t(a, b):
    return contract(a, b, 1, 1)


def swap(x, axis):
    return lax.ppermute(x, axis, SWAP)


def pin(x, *first):
    return lax.optimization_barrier((x,) + first)[0]


def total(terms):
    out = terms[0].astype(f32)
    for t in terms[1:]:
        out = out + t.astype(f32)
    return out


class Share:
    def __init__(self, terms, names):
        self.terms = list(terms)
        self.names = list(names)

    def halve(self, axis, *first):
        if axis not in self.names:
            return self.terms[-1]
        dim = self.names.index(axis)
        i = lax.axis_index(axis)
        terms = [pin(t, *first) if first else t for t in self.terms[-1:]] + self.terms[:-1]
        there = [lax.dynamic_index_in_dim(t, 1 - i, dim, keepdims=False) for t in terms]
        self.terms = [lax.dynamic_index_in_dim(t, i, dim, keepdims=False) for t in terms]
        self.names.remove(axis)
        sent = total(there).astype(bf16)
        self.terms.append(swap(sent, axis))
        return sent


def body(
    fields,
    lead_bucket,
    cotangent,
    lead_table,
    ln1_gain,
    ln1_bias,
    w_qkv,
    q_bias,
    v_bias,
    w_out,
    out_bias,
    ln2_gain,
    ln2_bias,
    w_up,
    up_bias,
    w_down,
    down_bias,
    *,
    axes,
    x_axes,
    samp_count,
):
    band = tuple(axes)
    low = ("core", "zl") + x_axes[::-1]
    members = 2 ** len(low)
    order = x_axes + ("zl", "core")
    D = w_out.shape[0]
    W = D // members
    half = fields.shape[1]
    rows = 2 * half
    two = samp_count == 2
    zh = lax.axis_index("zh")
    me = lax.axis_index(low)

    def pick(x, i):
        return lax.dynamic_index_in_dim(x, i, 0, keepdims=False)

    def to_sample(x):
        return jnp.concatenate([pick(x, zh), swap(pick(x, 1 - zh), "zh")])

    def to_band(x):
        own = x[:half]
        other = swap(x[half:].astype(bf16), "zh").astype(x.dtype)
        return jnp.where(zh == 0, jnp.stack([own, other]), jnp.stack([other, own]))

    def gather(x):
        if len(x_axes) == 1:
            x_axis = x_axes[0]
            cut = x.shape[0] // 2
            by_x = swap(x, x_axis)
            by_z = swap(x, "zl")
            far = [swap(by_x[:cut], "zl"), swap(by_z[cut:], x_axis)]
            pieces = [(x, 0, 0), (by_x, 1, 0), (by_z, 2, 0), (far[0], 3, 0), (far[1], 3, cut)]
            pieces += [(swap(p, "core"), 4 + k, o) for p, k, o in pieces]
        else:
            pieces = [(x, 0, 0)]
            for bit, axis in enumerate(order):
                pieces += [(swap(p, axis), k + 2**bit, 0) for p, k, _ in pieces]
        out = jnp.zeros((members * rows, D), bf16)
        for piece, k, offset in pieces:
            out = lax.dynamic_update_slice(out, piece, ((me ^ k) * rows + offset, 0))
        return out

    lead_row = pick(lead_table, pick(lead_bucket, zh)).astype(f32)
    carried = to_sample(fields).astype(f32)

    def member_columns(x, block):
        return lax.dynamic_slice_in_dim(x, block * D + me * W, W, x.ndim - 1)

    kept = []
    inputs = carried + lead_row
    n1, r1 = norm_parts(inputs)
    normed = (n1 * ln1_gain + ln1_bias).astype(bf16)
    weights = (w_out, out_bias, ln2_gain, ln2_bias, w_up, up_bias, w_down, down_bias, lead_row, ln1_gain, ln1_bias)
    for index in range(STEPS):
        normed_all = gather(normed)
        queries = (dot(normed, w_qkv[:, :D]) + q_bias).astype(bf16)
        if index == 0:
            out_grad = to_sample(pin(cotangent, normed_all))
        attended = attend(queries, normed_all, w_qkv, v_bias)
        if index == 0:
            attended, out_grad = pin((attended, out_grad))
        last = index == STEPS - 1
        n2, r2, normed_two, hidden, activated, *after = block_forward(inputs, attended, weights, last)
        kept.append((n1, r1, normed_all, attended, n2, r2, normed_two, hidden, activated))
        if not last:
            inputs, n1, r1, normed = after
    carried = after[0]
    result = to_band(carried)

    grad = out_grad
    small = None
    core = lax.axis_index("core")
    y = lax.axis_index("samp")
    bands = 2 ** len(axes)
    names = axes[:-1]
    cube = (2,) * len(names)
    later = None
    w_heads = None
    unit, send_table, keep_table = unit_tables(bands, 2 ** len(x_axes), W, D)
    send_row, keep_row = pick(jnp.asarray(send_table), me), pick(jnp.asarray(keep_table), me)
    keep_rows = pick(keep_row, zh), pick(keep_row, 1 - zh)
    def split_rows(x, rows_two):
        n, r, c = x.shape
        return x.reshape(cube + ((2, r // 2) if rows_two else (r,)) + (c,))

    own_weight = jnp.concatenate([member_columns(w_qkv, i) for i in range(3)], axis=1)
    own_bias = jnp.concatenate([member_columns(q_bias, 0), jnp.zeros((W,), f32), member_columns(v_bias, 0)])

    def own_part(index):
        own = (dot(kept[index][2], own_weight) + own_bias).astype(bf16)
        return own[:, :W], own[:, W : 2 * W], own[:, 2 * W :]

    owns = {}
    for index in reversed(range(STEPS)):
        n1, r1, normed_all, attended, n2, r2, normed_two, hidden, activated = kept[index]
        last = index == 0
        if last:
            grads = (later[2], later[3], normed_two)
        else:
            down_grad = grad.astype(bf16)
            grads = ()
        hidden_grad, hidden_sum, middle_grad, branch_grad, sent, sums_two, *ups = block_backward(
            core, grad, hidden, w_down, w_up, w_out, n2, r2, ln2_gain, members, grads
        )
        own_grad = lax.all_to_all(sent, low, 0, 0, tiled=True).reshape(members * rows, W)
        if last:
            z_other, x_other, z_own, x_own = ups
            z_core = swap(z_other, "core")
            x_other, x_own = grad_out(
                core, (later[4], pin(branch_grad, sent)), (later[5], attended), bands, x_other, x_own
            )
            x_core = swap(x_other, "core")
            left, right = (later[0], pin(down_grad, x_other)), (later[1], activated)
            one_other, one_own = grad_rows(core, left, right, bands, 0, 2)
            one_core = swap(one_other, "core")
            samp = ("samp",) * two
            z_terms = pin((z_own, z_core), one_other)
            z_share = Share([split_rows(t, two) for t in z_terms], names + samp)
            left = (later[0], pin(down_grad, z_share.halve("zl")))
            two_other, two_own = grad_rows(core, left, right, bands, 1, 2)
            two_core = swap(two_other, "core")
            x_terms = pin((x_own, x_core), two_other)
            x_share = Share([split_rows(t, two) for t in x_terms], names + samp)
            own_grad, one_own = pin((own_grad, one_own), x_share.halve(x_axes[0]))
            down_one = Share([split_rows(t, two) for t in (one_own, one_core)], names + samp)
            own_grad = pin(own_grad, down_one.halve("samp"))
            heads = W // HD
            d_heads = attend_back(*owns[0], own_grad, members, range((heads + 1) // 2))
            waits = pin((own_grad, d_heads, z_share.terms[-1], down_one.terms[-1], two_own, two_core))
            own_grad, d_heads, z_share.terms[-1], down_one.terms[-1], two_own, two_core = waits
            down_two = Share([split_rows(t, two) for t in (two_own, two_core)], names + samp)
            sent = [z_share.halve("zh"), down_one.halve("zl"), down_two.halve("samp")]
            if heads > 1:
                own_grad, d_heads = pin((own_grad, d_heads), *sent)
                d_heads = attend_back(*owns[0], own_grad, members, range(heads // 2, heads), d_heads)
            shares = (z_share, x_share, down_one, down_two)
            waits = pin((d_heads, *(t.terms[-1] for t in shares)))
            d_heads = waits[0]
            for t, value in zip(shares, waits[1:]):
                t.terms[-1] = value
            sent = [x_share.halve("samp"), down_two.halve("zh"), z_share.halve("samp")]
            sent += [down_one.halve(a) for a in x_axes]
            d_heads = pin(d_heads, *sent)
        else:
            own_grad, send_row, keep_rows = pin((own_grad, send_row, keep_rows), result)
            later = (down_grad, activated, hidden_grad, normed_two, branch_grad, attended)
            owns[index] = own_part(index)
            d_heads = attend_back(*owns[index], own_grad, members)
        back = lax.all_to_all(d_heads, low, 0, 0, tiled=True)
        w_heads = grad_heads(d_heads, normed_all, w_heads, bf16 if last else f32)
        if last:
            units = w_heads.reshape(-1, unit, D)
            if two:
                there = lax.dynamic_slice_in_dim(units, (1 - y) * (D // 2), D // 2, 2)
                here = lax.dynamic_slice_in_dim(units, y * (D // 2), D // 2, 2)
                units = [here, swap(there, "samp")]
            else:
                there, units = units, [units]
            back = pin(back, there)
            waits = pin(tuple(t.terms[-1] for t in shares), back)
            for t, value in zip(shares, waits):
                t.terms[-1] = value
            sent = [x_share.halve(a) for a in x_axes[1:] + ("zl",)]
            sent += [down_one.halve("zh")] + [t.halve(a) for t in (down_two, z_share) for a in x_axes]
            units[-1] = pin(units[-1], *sent)
            outgoing = take(units, send_row)
            incoming = lax.all_to_all(outgoing, low, 0, 0, tiled=True)
            back = pin(back, outgoing)
        else:
            owns[0] = own_part(0)
            back = pin(back, w_heads, *owns[0])
        grad, low_grad, sums_one, sums_qv = qkv_backward(
            back, w_qkv, middle_grad, n1, r1, ln1_gain, half if last else rows
        )
        down_grad = low_grad
        step_small = (sums_one[:3], sums_qv[:2], sums_two[:4], hidden_sum)
        small = step_small if small is None else tuple(a + b for a, b in zip(small, step_small))
    fields_sent = low_grad
    fields_other = swap(fields_sent, "zh")
    x_share.terms[-1] = pin(x_share.terms[-1], fields_sent)
    x_sent = x_share.halve("zh")
    one, qv, two_sums, up_sum = pin(small, x_sent)
    samples = 2 * samp_count
    slot = 2 * y + zh
    mine = lax.broadcasted_iota(jnp.int32, (samples, 1), 0) == slot
    leads = jnp.where(mine, one[2:3], 0.0)
    lane = lax.broadcasted_iota(jnp.int32, (bands, D // bands), 1) == slot
    bucket = jnp.where(lane & (me == 0), pick(lead_bucket, zh).astype(f32), 0.0)
    vectors = jnp.concatenate([one[:2], qv, two_sums, leads])
    vectors = vectors.reshape(-1, bands, D // bands).transpose(1, 0, 2).reshape(bands, -1)
    vectors = jnp.concatenate([vectors, up_sum.reshape(bands, -1), bucket], axis=1)
    incoming, vectors = pin((incoming, vectors), fields_sent)
    vectors = lax.all_to_all(vectors, band, 0, 0, tiled=True)

    def both(x):
        x = x.astype(bf16)
        if not two:
            return lax.psum(x, "samp").astype(f32)
        other = swap(x, "samp")
        return jnp.concatenate([jnp.where(y == 0, x, other), jnp.where(y == 0, other, x)]).astype(f32)

    def both_cut(x, n):
        if not two:
            x = both(x)
            return x[:n], x[n:]
        x = x.astype(bf16)
        other = swap(x, "samp")
        first, second = jnp.where(y == 0, x, other), jnp.where(y == 0, other, x)
        x = jnp.concatenate([first, second]).astype(f32)
        return x[:n], x[n:]

    incoming, down_two.terms[-1] = pin((incoming, down_two.terms[-1]), x_sent)
    sent = down_two.halve("zl")
    waits = pin((incoming, fields_other, vectors, *(t.terms[-1] for t in shares)), sent)
    incoming, fields_other, vectors = waits[:3]
    for t, value in zip(shares, waits[3:]):
        t.terms[-1] = value
    down = jnp.concatenate([total(down_one.terms), total(down_two.terms)], axis=1)
    vectors = jnp.sum(vectors, axis=0)
    vectors = vectors + swap(vectors, "samp") if two else lax.psum(vectors, "samp")
    other = swap(take([incoming], keep_rows[1]), "zh")
    own = take([incoming], keep_rows[0])
    own = total([own, other]).astype(bf16).reshape(3 * D // bands, -1)
    if two:
        other = swap(own, "samp")
        own = jnp.concatenate([jnp.where(y == 0, own, other), jnp.where(y == 0, other, own)], axis=1)
    else:
        own = lax.psum(own, "samp")
    w_qkv_grad = own.astype(f32).T

    w_down_grad = both(down).T
    n_up = w_up.shape[1] // bands
    bottom = both_cut(total(x_share.terms), n_up // 2)
    w_out_grad = bottom[1].T
    w_up_grad = jnp.concatenate([both(total(z_share.terms)), bottom[0]]).T
    fields_grad = join(zh, grad, fields_other)

    w = D // bands
    leads = vectors[8 * w : (8 + samples) * w].reshape(samples, w)
    up_grad = vectors[(8 + samples) * w : -w]
    buckets = vectors[-w:][:samples].astype(jnp.int32)
    one_hot = (buckets[:, None] == jnp.arange(lead_table.shape[0], dtype=jnp.int32)[None, :]).astype(f32)
    lead_grad = jnp.dot(one_hot.T, leads, precision=lax.Precision.HIGHEST)
    rows_of = lambda i: vectors[i * w : (i + 1) * w]
    g = [rows_of(i) for i in (0, 1, 2, 3, 6, 4, 5)] + [up_grad, rows_of(7)]
    return (
        result,
        fields_grad,
        lead_grad,
        g[0],
        g[1],
        w_qkv_grad,
        g[2],
        g[3],
        w_out_grad,
        g[4],
        g[5],
        g[6],
        w_up_grad,
        g[7],
        w_down_grad,
        g[8],
    )


def solution(mesh):
    samp_count, band_count = mesh.shape["samp"], mesh.shape["band"]
    x_axes = tuple(f"x{i}" for i in range((band_count // 8).bit_length() - 1))
    axes = ("zh", "zl") + x_axes + ("core",)
    assert 2 ** len(axes) == band_count
    fine = Mesh(mesh.devices.reshape((samp_count,) + (2,) * len(axes)), ("samp",) + axes)
    tokens = P("samp", axes, None)
    columns, vector = P(None, axes), P(axes)
    in_specs = (tokens, P("samp"), tokens) + (P(),) * 14
    out_specs = (
        tokens,
        tokens,
        columns,
        vector,
        vector,
        columns,
        vector,
        vector,
        columns,
        vector,
        vector,
        vector,
        columns,
        vector,
        columns,
        vector,
    )
    run = functools.partial(body, axes=axes, x_axes=x_axes, samp_count=samp_count)
    return jax.shard_map(run, mesh=fine, in_specs=in_specs, out_specs=out_specs, check_vma=False)
```

```python
import functools
import math

import jax
import jax.numpy as jnp
import numpy as np
from jax import lax
from jax.experimental import pallas as pl
from jax.experimental.pallas import tpu as pltpu
from jax.sharding import Mesh
from jax.sharding import PartitionSpec as P

HD = 64
STEPS = 2
EPS = 1e-05
EXP_SCALE = 0.125 * 1.4426950408889634
GELU_A = 0.7978845608028654
GELU_B = 0.044715
MIB = 2**20
SWAP = [(0, 1), (1, 0)]
f32 = jnp.float32
bf16 = jnp.bfloat16


def cost(us):
    return pl.CostEstimate(flops=int(us * 1.15e9), bytes_accessed=1000, transcendentals=0)


def contract(a, b, a_dim, b_dim):
    return lax.dot_general(a, b, (((a_dim,), (b_dim,)), ((), ())), preferred_element_type=f32)


def head_part(x, h, heads):
    if heads == 1:
        return x
    lane = lax.broadcasted_iota(jnp.int32, x.shape, 1)
    return jnp.where(lane // HD == h, x, jnp.zeros_like(x))


def attend_kernel(q_ref, n_ref, wk_ref, wv_ref, b_ref, o_ref):
    normed = n_ref[...]
    keys = contract(normed, wk_ref[...], 1, 0).astype(bf16)
    values = (contract(normed, wv_ref[...], 1, 0) + b_ref[...]).astype(bf16)
    pair = 2 * HD
    for start in range(0, q_ref.shape[1], pair):
        q, k, v = q_ref[:, start : start + pair], keys[:, start : start + pair], values[:, start : start + pair]
        out = None
        for h in range(2):
            s = contract(head_part(q, h, 2), k, 1, 1)
            top = jnp.max(s, axis=-1, keepdims=True)
            e = jnp.exp2((s - top) * EXP_SCALE)
            total = jnp.sum(e, axis=-1, keepdims=True)
            o = head_part(contract(e.astype(bf16), v, 1, 0) / total, h, 2)
            out = o if out is None else out + o
        o_ref[:, start : start + pair] = out.astype(bf16)


def attend(q, normed_all, w_qkv, v_bias):
    rows, width = q.shape
    count = normed_all.shape[0]
    block = 4 * HD
    own = spec((rows, block), lambda j: (0, j))
    shift = width // block
    return pl.pallas_call(
        attend_kernel,
        grid=(width // block,),
        in_specs=[
            own,
            spec((count, width), lambda j: (0, 0)),
            spec((width, block), lambda j: (0, shift + j)),
            spec((width, block), lambda j: (0, 2 * shift + j)),
            spec((1, block), lambda j: (0, j)),
        ],
        out_specs=own,
        out_shape=jax.ShapeDtypeStruct((rows, width), bf16),
        compiler_params=pltpu.CompilerParams(vmem_limit_bytes=40 * MIB),
        cost_estimate=cost(24),
        name="attend",
    )(q, normed_all, w_qkv, w_qkv, v_bias.reshape(1, width))


def attend_back_kernel(q_ref, k_ref, v_ref, do_ref, *rest, heads, some):
    out_ref, dk_sum, dv_sum = rest[-3:]
    step = pl.program_id(0)
    rows = q_ref.shape[0]

    @pl.when(step == 0)
    def _():
        dk_sum[...] = jnp.zeros_like(dk_sum)
        dv_sum[...] = jnp.zeros_like(dv_sum)

    q, k, v, do = q_ref[...], k_ref[...], v_ref[...], do_ref[...]
    queries = [head_part(q, h, heads) for h in some]
    grads = [head_part(do, h, heads) for h in some]
    scores = [contract(x, k, 1, 1) for x in queries]
    prob_grads = [contract(x, v, 1, 1) for x in grads]
    dq = dk = dv = 0.0
    for h, qh, doh, s, dp in zip(some, queries, grads, scores, prob_grads):
        top = jnp.max(s, axis=-1, keepdims=True)
        e = jnp.exp2((s - top) * EXP_SCALE)
        inverse = 1.0 / jnp.sum(e, axis=-1, keepdims=True)
        inner = jnp.sum(e * dp, axis=-1, keepdims=True) * inverse
        p = e * inverse
        ds = (p * (dp - inner)).astype(bf16)
        dq = dq + head_part(contract(ds, k, 1, 0), h, heads)
        dk = dk + contract(ds, qh, 0, 0)
        dv = dv + contract(p.astype(bf16), doh, 0, 0)
    dk_sum[...] += dk
    dv_sum[...] += dv

    def put(m, i, x):
        if len(rest) == 4:
            x = x + rest[0][m, i].astype(f32)
        out_ref[m, i] = x.astype(bf16)

    put(step, 0, dq * 0.125)

    @pl.when(step == pl.num_programs(0) - 1)
    def _():
        for m in range(out_ref.shape[0]):
            put(m, 1, dk_sum[m * rows : (m + 1) * rows, :] * 0.125)
            put(m, 2, dv_sum[m * rows : (m + 1) * rows, :])


def attend_back(q, k, v, do, members, some=None, add=None):
    count, width = q.shape
    rows = count // members
    heads = width // HD
    part = pl.BlockSpec((rows, width), lambda i: (i, 0))
    full = pl.BlockSpec((count, width), lambda i: (0, 0))
    shape = (members, 3, rows, width)
    out = pl.BlockSpec(shape, lambda i: (0, 0, 0, 0))
    extra = [] if add is None else [add]
    return pl.pallas_call(
        functools.partial(attend_back_kernel, heads=heads, some=some or range(heads)),
        grid=(members,),
        in_specs=[part, full, full, part] + [out] * len(extra),
        out_specs=out,
        out_shape=jax.ShapeDtypeStruct(shape, bf16),
        scratch_shapes=[pltpu.VMEM((count, width), f32), pltpu.VMEM((count, width), f32)],
        compiler_params=pltpu.CompilerParams(vmem_limit_bytes=60 * MIB),
        cost_estimate=cost(33 if some is None else 17),
        name="attend_back",
    )(q, k, v, do, *extra)


def spec(block, index):
    return pl.BlockSpec(block, index)


def grad_rows_kernel(c_ref, l1, l0, r1, r0, other_ref, own_ref, sums):
    sums[...] = contract(l1[...], r1[...], 0, 0) + contract(l0[...], r0[...], 0, 0)
    count, n, _ = own_ref.shape
    for j in range(count):
        for ref, core in ((other_ref, 1 - c_ref[0]), (own_ref, c_ref[0])):
            ref[j] = sums[pl.ds(pl.multiple_of((2 * j + core) * n, n), n), :].astype(bf16)


def grad_rows(core, left, right, bands, part, parts):
    tokens, m = left[0].shape
    n = right[0].shape[1] // parts
    block = min(n, 512)
    first = part * (n // block)
    out = spec((bands // 2, m // bands, block), lambda j, c: (0, 0, j))
    whole = spec((tokens, m), lambda j, c: (0, 0))
    part = spec((tokens, block), lambda j, c: (0, first + j))
    return pl.pallas_call(
        grad_rows_kernel,
        grid_spec=pltpu.PrefetchScalarGridSpec(
            num_scalar_prefetch=1,
            grid=(n // block,),
            in_specs=[whole, whole, part, part],
            out_specs=[out, out],
            scratch_shapes=[pltpu.VMEM((m, block), f32)],
        ),
        out_shape=[jax.ShapeDtypeStruct((bands // 2, m // bands, n), bf16)] * 2,
        compiler_params=pltpu.CompilerParams(vmem_limit_bytes=60 * MIB),
        cost_estimate=cost(8),
        name="grad_rows",
    )(core.reshape(1), *left, *right)


def block_forward_kernel(
    x_ref, a_ref, wo_ref, bo_ref, g_ref, b_ref, wu_ref, bu_ref, wd_ref, bd_ref, lead_ref, g1_ref, b1_ref,
    n2_ref, r2_ref, low2_ref, hidden_ref, act_ref, *rest, last
):
    total = rest[-1]
    step = pl.program_id(0)

    @pl.when(step == 0)
    def _():
        middle = x_ref[...] + contract(a_ref[...], wo_ref[...], 1, 0) + bo_ref[...]
        n, r = norm_parts(middle)
        n2_ref[...] = n
        r2_ref[...] = r
        low2_ref[...] = (n * g_ref[...] + b_ref[...]).astype(bf16)
        total[...] = middle + bd_ref[...]

    hidden = contract(low2_ref[...], wu_ref[...], 1, 0) + bu_ref[...]
    hidden_ref[...] = hidden
    act = gelu(hidden).astype(bf16)
    act_ref[...] = act
    total[...] += contract(act, wd_ref[...], 1, 0)

    @pl.when(step == pl.num_programs(0) - 1)
    def _():
        carried = total[...]
        if last:
            rest[0][...] = carried.astype(bf16)
        else:
            x = carried + lead_ref[...]
            n, r = norm_parts(x)
            rest[0][...] = x
            rest[1][...] = n
            rest[2][...] = r
            rest[3][...] = (n * g1_ref[...] + b1_ref[...]).astype(bf16)


def block_forward(inputs, attended, weights, last):
    w_out, out_bias, ln2_gain, ln2_bias, w_up, up_bias, w_down, down_bias, lead, ln1_gain, ln1_bias = weights
    t, d = inputs.shape
    f = w_up.shape[1]
    block = 512
    row = lambda v: v.reshape(1, -1)
    full = spec((t, d), lambda i: (0, 0))
    vec = spec((1, d), lambda i: (0, 0))
    one = spec((t, 1), lambda i: (0, 0))
    wide = spec((t, block), lambda i: (0, i))
    shape = jax.ShapeDtypeStruct
    outs = [full, one, full, wide, wide] + ([full] if last else [full, full, one, full])
    shapes = [shape((t, d), f32), shape((t, 1), f32), shape((t, d), bf16), shape((t, f), f32), shape((t, f), bf16)]
    shapes += [shape((t, d), bf16)] if last else [
        shape((t, d), f32), shape((t, d), f32), shape((t, 1), f32), shape((t, d), bf16)
    ]
    return pl.pallas_call(
        functools.partial(block_forward_kernel, last=last),
        grid=(f // block,),
        in_specs=[
            full, full, spec((d, d), lambda i: (0, 0)), vec, vec, vec,
            spec((d, block), lambda i: (0, i)), spec((1, block), lambda i: (0, i)),
            spec((block, d), lambda i: (i, 0)), vec, vec, vec, vec,
        ],
        out_specs=outs,
        out_shape=shapes,
        scratch_shapes=[pltpu.VMEM((t, d), f32)],
        compiler_params=pltpu.CompilerParams(vmem_limit_bytes=40 * MIB),
        cost_estimate=cost(12),
        name="block_forward",
    )(
        inputs, attended, w_out, row(out_bias), row(ln2_gain), row(ln2_bias), w_up, row(up_bias), w_down,
        row(down_bias), row(lead), row(ln1_gain), row(ln1_bias),
    )


def put_sums(ref, *sums):
    for i, v in enumerate(sums):
        ref[i : i + 1, :] = v


def column_sum(x):
    return jnp.sum(x.astype(f32), axis=0, keepdims=True)


def block_backward_kernel(c_ref, grad_ref, h_ref, wd_ref, wu_ref, wo_ref, n_ref, r_ref, g_ref, *rest, grads, bands):
    if grads:
        l1_ref, x1_ref, x0_ref = rest[:3]
        z_other, x_other, z_own, x_own = rest[9:13]
        sums, rest = rest[14], rest[3:9] + rest[13:14]
    hg_ref, hsum_ref, middle_ref, branch_ref, sent_ref, sums_ref, total = rest
    step = pl.program_id(0)
    down = grad_ref[...].astype(bf16)
    low = (gelu_slope(h_ref[...]) * contract(down, wd_ref[...], 1, 1)).astype(bf16)
    hg_ref[...] = low
    hsum_ref[...] = column_sum(low)
    part = contract(low, wu_ref[...], 1, 1)
    if grads:
        sums[...] = contract(l1_ref[...], x1_ref[...], 0, 0) + contract(low, x0_ref[...], 0, 0)
        pairs = z_own.shape[0]
        n = sums.shape[0] // (2 * pairs)
        for q in range(pairs):
            for z, x, core in ((z_other, x_other, 1 - c_ref[0]), (z_own, x_own, c_ref[0])):
                start = pl.multiple_of((2 * q + core) * n, n)
                z[q] = sums[pl.ds(start, n // 2), :].astype(bf16)
                x[q] = sums[pl.ds(start + n // 2, n // 2), :].astype(bf16)

    @pl.when(step == 0)
    def _():
        total[...] = part

    @pl.when(step > 0)
    def _():
        total[...] += part

    @pl.when(step == pl.num_programs(0) - 1)
    def _():
        dv, gain, bias = norm_back(total[...], n_ref[...], r_ref[...], g_ref[...])
        middle = grad_ref[...] + dv
        middle_ref[...] = middle
        branch = middle.astype(bf16)
        branch_ref[...] = branch
        put_sums(sums_ref, gain, bias, column_sum(branch), column_sum(down))
        w = sent_ref.shape[2]
        attended = contract(branch, wo_ref[...], 1, 1).astype(bf16)
        for m in range(sent_ref.shape[0]):
            sent_ref[m] = attended[:, m * w : (m + 1) * w]


def block_backward(core, grad, hidden, w_down, w_up, w_out, n2, r2, gain, members, grads=()):
    t, d = grad.shape
    f = hidden.shape[1]
    block = 512
    bands = 2 * members
    full = spec((t, d), lambda i, c: (0, 0))
    wide = spec((t, block), lambda i, c: (0, i))
    sent = (members, t, d // members)
    shape = jax.ShapeDtypeStruct
    outs = [
        wide, spec((1, block), lambda i, c: (0, i)), full, full,
        spec(sent, lambda i, c: (0, 0, 0)), spec((8, d), lambda i, c: (0, 0)),
    ]
    shapes = [
        shape((t, f), bf16), shape((1, f), f32), shape((t, d), f32), shape((t, d), bf16),
        shape(sent, bf16), shape((8, d), f32),
    ]
    scratch = [pltpu.VMEM((t, d), f32)]
    if grads:
        n = f // bands
        pairs = block // (2 * n)
        part = spec((pairs, n // 2, d), lambda i, c: (i, 0, 0))
        outs += [part] * 4
        shapes += [shape((bands // 2, n // 2, d), bf16), shape((bands // 2, n // 2 + d // bands, d), bf16)] * 2
        scratch += [pltpu.VMEM((block, d), f32)]
    return pl.pallas_call(
        functools.partial(block_backward_kernel, grads=bool(grads), bands=bands),
        grid_spec=pltpu.PrefetchScalarGridSpec(
            num_scalar_prefetch=1,
            grid=(f // block,),
            in_specs=[
                full, wide, spec((block, d), lambda i, c: (i, 0)), spec((d, block), lambda i, c: (0, i)),
                spec((d, d), lambda i, c: (0, 0)), full, spec((t, 1), lambda i, c: (0, 0)),
                spec((1, d), lambda i, c: (0, 0)),
            ] + [wide, full, full][: len(grads)],
            out_specs=outs,
            scratch_shapes=scratch,
        ),
        out_shape=shapes,
        compiler_params=pltpu.CompilerParams(vmem_limit_bytes=(60 if grads else 48) * MIB),
        cost_estimate=cost(18 if grads else 14),
        name="block_backward",
    )(core.reshape(1), grad, hidden, w_down, w_up, w_out, n2, r2, gain.reshape(1, d), *grads)


def grad_out_kernel(c_ref, l1, l0, r1, r0, _, __, other_ref, own_ref, sums, *, pairs):
    sums[...] = contract(l1[...], r1[...], 0, 0) + contract(l0[...], r0[...], 0, 0)
    n = own_ref.shape[1]
    for q in range(pairs):
        for ref, core in ((other_ref, 1 - c_ref[0]), (own_ref, c_ref[0])):
            ref[q] = sums[pl.ds(pl.multiple_of((2 * q + core) * n, n), n), :].astype(bf16)


def grad_out(core, left, right, bands, other, own):
    tokens, m = left[0].shape
    count, height, d = own.shape
    n = m // bands
    pairs = max(1, 256 // (2 * n))
    columns = spec((tokens, 2 * n * pairs), lambda j, c: (0, j))
    whole = spec((tokens, d), lambda j, c: (0, 0))
    out = spec((pairs, n, d), lambda j, c: (j, height // n - 1, 0))
    anywhere = pl.BlockSpec(memory_space=pl.ANY)
    return pl.pallas_call(
        functools.partial(grad_out_kernel, pairs=pairs),
        grid_spec=pltpu.PrefetchScalarGridSpec(
            num_scalar_prefetch=1,
            grid=(count // pairs,),
            in_specs=[columns, columns, whole, whole, anywhere, anywhere],
            out_specs=[out, out],
            scratch_shapes=[pltpu.VMEM((2 * n * pairs, d), f32)],
        ),
        out_shape=[jax.ShapeDtypeStruct(own.shape, bf16)] * 2,
        input_output_aliases={5: 0, 6: 1},
        compiler_params=pltpu.CompilerParams(vmem_limit_bytes=60 * MIB),
        cost_estimate=cost(3),
        name="grad_out",
    )(core.reshape(1), *left, *right, other, own)


def qkv_backward_kernel(b_ref, wq_ref, wk_ref, wv_ref, m_ref, n_ref, r_ref, g_ref, grad_ref, low_ref, sums_ref, qv_ref, total):
    step = pl.program_id(0)
    w = b_ref.shape[3]
    part = None
    for m in range(b_ref.shape[0]):
        for i, ref in enumerate((wq_ref, wk_ref, wv_ref)):
            x = contract(b_ref[m, i], ref[:, m * w : (m + 1) * w], 1, 1)
            part = x if part is None else part + x
        qv_ref[0:1, m * w : (m + 1) * w] = column_sum(b_ref[m, 0])
        qv_ref[1:2, m * w : (m + 1) * w] = column_sum(b_ref[m, 2])

    @pl.when(step == 0)
    def _():
        total[...] = part

    @pl.when(step > 0)
    def _():
        total[...] += part

    @pl.when(step == pl.num_programs(0) - 1)
    def _():
        dv, gain, bias = norm_back(total[...], n_ref[...], r_ref[...], g_ref[...])
        grad = m_ref[...] + dv
        grad_ref[...] = grad
        low_ref[...] = grad[grad.shape[0] - low_ref.shape[0] :].astype(bf16)
        put_sums(sums_ref, gain, bias, column_sum(grad))


def qkv_backward(back, w_qkv, middle_grad, n1, r1, gain, low):
    members, _, t, w = back.shape
    d = members * w
    at_once = max(2, 128 // w)
    block = at_once * w
    shift = d // block
    full = spec((t, d), lambda i: (0, 0))
    weight = [spec((d, block), lambda i, s=s: (0, s * shift + i)) for s in range(3)]
    shape = jax.ShapeDtypeStruct
    return pl.pallas_call(
        qkv_backward_kernel,
        grid=(members // at_once,),
        in_specs=[spec((at_once, 3, t, w), lambda i: (i, 0, 0, 0))] + weight + [
            full, full, spec((t, 1), lambda i: (0, 0)), spec((1, d), lambda i: (0, 0)),
        ],
        out_specs=[
            full, spec((low, d), lambda i: (0, 0)), spec((8, d), lambda i: (0, 0)),
            spec((8, block), lambda i: (0, i)),
        ],
        out_shape=[
            shape((t, d), f32), shape((low, d), bf16), shape((8, d), f32), shape((8, d), f32),
        ],
        scratch_shapes=[pltpu.VMEM((t, d), f32)],
        compiler_params=pltpu.CompilerParams(vmem_limit_bytes=60 * MIB),
        cost_estimate=cost(12),
        name="qkv_backward",
    )(back, w_qkv, w_qkv, w_qkv, middle_grad, n1, r1, gain.reshape(1, d))


def grad_heads_kernel(d_ref, n_ref, *rest):
    out_ref = rest[-1]
    rows = d_ref.shape[2]
    for i in range(3):
        total = rest[0][i] if len(rest) == 2 else jnp.zeros(out_ref.shape[1:], f32)
        for m in range(d_ref.shape[0]):
            total += contract(d_ref[m, i], n_ref[m * rows : (m + 1) * rows, :], 0, 0)
        out_ref[i] = total.astype(out_ref.dtype)


def grad_heads(d, normed_all, add, kind):
    members, _, rows, width = d.shape
    dim = normed_all.shape[1]
    shape = (3, width, dim)
    out = spec((3, width, dim // 4), lambda i: (0, 0, i))
    extra = [] if add is None else [add]
    return pl.pallas_call(
        grad_heads_kernel,
        grid=(4,),
        in_specs=[
            spec(d.shape, lambda i: (0, 0, 0, 0)),
            spec((members * rows, dim // 4), lambda i: (0, i)),
        ]
        + [out] * len(extra),
        out_specs=out,
        out_shape=jax.ShapeDtypeStruct(shape, kind),
        compiler_params=pltpu.CompilerParams(vmem_limit_bytes=60 * MIB),
        cost_estimate=cost(5),
        name="grad_heads",
    )(d, normed_all, *extra)


def take_kernel(table, *refs):
    for i in range(refs[-1].shape[0]):
        total = refs[0][table[i]].astype(f32)
        for r in refs[1:-1]:
            total = total + r[table[i]].astype(f32)
        refs[-1][i] = total.astype(bf16)


def take(terms, table):
    shape = terms[0].shape
    count = table.shape[0]
    return pl.pallas_call(
        take_kernel,
        grid_spec=pltpu.PrefetchScalarGridSpec(
            num_scalar_prefetch=1,
            grid=(1,),
            in_specs=[spec(shape, lambda i, t: (0, 0, 0))] * len(terms),
            out_specs=spec((count,) + shape[1:], lambda i, t: (0, 0, 0)),
        ),
        out_shape=jax.ShapeDtypeStruct((count,) + shape[1:], bf16),
        compiler_params=pltpu.CompilerParams(vmem_limit_bytes=60 * MIB),
        cost_estimate=cost(3),
        name="take",
    )(table, *terms)


def join_kernel(i_ref, own_ref, other_ref, out_ref):
    half = other_ref.shape[0]
    out_ref[i_ref[0]] = own_ref[:half]
    out_ref[1 - i_ref[0]] = other_ref[...].astype(f32)


def join(index, own, other):
    half, d = other.shape
    full = spec((half, d), lambda i, c: (0, 0))
    return pl.pallas_call(
        join_kernel,
        grid_spec=pltpu.PrefetchScalarGridSpec(
            num_scalar_prefetch=1,
            grid=(1,),
            in_specs=[full, full],
            out_specs=spec((2, half, d), lambda i, c: (0, 0, 0)),
        ),
        out_shape=jax.ShapeDtypeStruct((2, half, d), f32),
        compiler_params=pltpu.CompilerParams(vmem_limit_bytes=8 * MIB),
        cost_estimate=cost(2),
        name="join",
    )(index.reshape(1), own, other)


def unit_tables(bands, x_count, width, dim):
    members = bands // 2
    unit = math.gcd(HD, 3 * dim // bands)
    per_band = 3 * dim // bands // unit
    made, slots, place = [], [], {}
    for g in range(members):
        units = [(b * dim + g * width) // unit + i for b in range(3) for i in range(width // unit)]
        by_low = [[] for _ in range(members)]
        for local, u in enumerate(units):
            band = u // per_band
            core, x, zl = band % 2, band // 2 % x_count, band // (2 * x_count) % 2
            low = (core * 2 + zl) * x_count + x
            place[u] = (g, len(by_low[low]))
            by_low[low].append(local)
        made.append(by_low)
    most = max(len(l) for by_low in made for l in by_low)
    send = np.zeros((members, members * most), np.int32)
    for g, by_low in enumerate(made):
        for low, locals_ in enumerate(by_low):
            for m, local in enumerate(locals_):
                send[g, low * most + m] = local
    keep = np.zeros((members, 2, per_band), np.int32)
    for u, (g, m) in place.items():
        band = u // per_band
        core, x, zl = band % 2, band // 2 % x_count, band // (2 * x_count) % 2
        low = (core * 2 + zl) * x_count + x
        keep[low, band // members, u % per_band] = g * most + m
    return unit, send, keep


def norm_parts(v):
    centred = v - jnp.mean(v, axis=-1, keepdims=True)
    r = lax.rsqrt(jnp.mean(centred * centred, axis=-1, keepdims=True) + EPS)
    return centred * r, r


def norm_back(dy, n, r, gain):
    dyg = dy * gain
    mean_one = jnp.mean(dyg, axis=-1, keepdims=True)
    mean_two = jnp.mean(dyg * n, axis=-1, keepdims=True)
    dv = r * (dyg - mean_one - n * mean_two)
    return dv, jnp.sum(dy * n, axis=0, keepdims=True), jnp.sum(dy, axis=0, keepdims=True)


def gelu(x):
    return 0.5 * x * (1.0 + jnp.tanh(GELU_A * (x + GELU_B * x * x * x)))


def gelu_slope(x):
    t = jnp.tanh(GELU_A * (x + GELU_B * x * x * x))
    return 0.5 * (1.0 + t) + 0.5 * x * (1.0 - t * t) * (GELU_A * (1.0 + 3.0 * GELU_B * x * x))


def dot(a, b):
    return jnp.dot(a, b, preferred_element_type=f32)


def dot_t(a, b):
    return contract(a, b, 1, 1)


def swap(x, axis):
    return lax.ppermute(x, axis, SWAP)


def pin(x, *first):
    return lax.optimization_barrier((x,) + first)[0]


def total(terms):
    out = terms[0].astype(f32)
    for t in terms[1:]:
        out = out + t.astype(f32)
    return out


class Share:
    def __init__(self, terms, names):
        self.terms = list(terms)
        self.names = list(names)

    def halve(self, axis, *first):
        if axis not in self.names:
            return self.terms[-1]
        dim = self.names.index(axis)
        i = lax.axis_index(axis)
        terms = [pin(t, *first) if first else t for t in self.terms[-1:]] + self.terms[:-1]
        there = [lax.dynamic_index_in_dim(t, 1 - i, dim, keepdims=False) for t in terms]
        self.terms = [lax.dynamic_index_in_dim(t, i, dim, keepdims=False) for t in terms]
        self.names.remove(axis)
        sent = total(there).astype(bf16)
        self.terms.append(swap(sent, axis))
        return sent


def body(
    fields,
    lead_bucket,
    cotangent,
    lead_table,
    ln1_gain,
    ln1_bias,
    w_qkv,
    q_bias,
    v_bias,
    w_out,
    out_bias,
    ln2_gain,
    ln2_bias,
    w_up,
    up_bias,
    w_down,
    down_bias,
    *,
    axes,
    x_axes,
    samp_count,
):
    band = tuple(axes)
    low = ("core", "zl") + x_axes[::-1]
    members = 2 ** len(low)
    order = x_axes + ("zl", "core")
    D = w_out.shape[0]
    W = D // members
    half = fields.shape[1]
    rows = 2 * half
    two = samp_count == 2
    zh = lax.axis_index("zh")
    me = lax.axis_index(low)

    def pick(x, i):
        return lax.dynamic_index_in_dim(x, i, 0, keepdims=False)

    def to_sample(x):
        return jnp.concatenate([pick(x, zh), swap(pick(x, 1 - zh), "zh")])

    def to_band(x):
        own = x[:half]
        other = swap(x[half:].astype(bf16), "zh").astype(x.dtype)
        return jnp.where(zh == 0, jnp.stack([own, other]), jnp.stack([other, own]))

    def gather(x):
        if len(x_axes) == 1:
            x_axis = x_axes[0]
            cut = x.shape[0] // 2
            by_x = swap(x, x_axis)
            by_z = swap(x, "zl")
            far = [swap(by_x[:cut], "zl"), swap(by_z[cut:], x_axis)]
            pieces = [(x, 0, 0), (by_x, 1, 0), (by_z, 2, 0), (far[0], 3, 0), (far[1], 3, cut)]
            pieces += [(swap(p, "core"), 4 + k, o) for p, k, o in pieces]
        else:
            pieces = [(x, 0, 0)]
            for bit, axis in enumerate(order):
                pieces += [(swap(p, axis), k + 2**bit, 0) for p, k, _ in pieces]
        out = jnp.zeros((members * rows, D), bf16)
        for piece, k, offset in pieces:
            out = lax.dynamic_update_slice(out, piece, ((me ^ k) * rows + offset, 0))
        return out

    lead_row = pick(lead_table, pick(lead_bucket, zh)).astype(f32)
    carried = to_sample(fields).astype(f32)

    def member_columns(x, block):
        return lax.dynamic_slice_in_dim(x, block * D + me * W, W, x.ndim - 1)

    kept = []
    inputs = carried + lead_row
    n1, r1 = norm_parts(inputs)
    normed = (n1 * ln1_gain + ln1_bias).astype(bf16)
    weights = (w_out, out_bias, ln2_gain, ln2_bias, w_up, up_bias, w_down, down_bias, lead_row, ln1_gain, ln1_bias)
    for index in range(STEPS):
        normed_all = gather(normed)
        queries = (dot(normed, w_qkv[:, :D]) + q_bias).astype(bf16)
        if index == 0:
            out_grad = to_sample(pin(cotangent, normed_all))
        attended = attend(queries, normed_all, w_qkv, v_bias)
        if index == 0:
            attended, out_grad = pin((attended, out_grad))
        last = index == STEPS - 1
        n2, r2, normed_two, hidden, activated, *after = block_forward(inputs, attended, weights, last)
        kept.append((n1, r1, normed_all, attended, n2, r2, normed_two, hidden, activated))
        if not last:
            inputs, n1, r1, normed = after
    carried = after[0]
    result = to_band(carried)

    grad = out_grad
    small = None
    core = lax.axis_index("core")
    y = lax.axis_index("samp")
    bands = 2 ** len(axes)
    names = axes[:-1]
    cube = (2,) * len(names)
    later = None
    w_heads = None
    unit, send_table, keep_table = unit_tables(bands, 2 ** len(x_axes), W, D)
    send_row, keep_row = pick(jnp.asarray(send_table), me), pick(jnp.asarray(keep_table), me)
    keep_rows = pick(keep_row, zh), pick(keep_row, 1 - zh)
    def split_rows(x, rows_two):
        n, r, c = x.shape
        return x.reshape(cube + ((2, r // 2) if rows_two else (r,)) + (c,))

    own_weight = jnp.concatenate([member_columns(w_qkv, i) for i in range(3)], axis=1)
    own_bias = jnp.concatenate([member_columns(q_bias, 0), jnp.zeros((W,), f32), member_columns(v_bias, 0)])

    def own_part(index):
        own = (dot(kept[index][2], own_weight) + own_bias).astype(bf16)
        return own[:, :W], own[:, W : 2 * W], own[:, 2 * W :]

    owns = {}
    for index in reversed(range(STEPS)):
        n1, r1, normed_all, attended, n2, r2, normed_two, hidden, activated = kept[index]
        last = index == 0
        if last:
            grads = (later[2], later[3], normed_two)
        else:
            down_grad = grad.astype(bf16)
            grads = ()
        hidden_grad, hidden_sum, middle_grad, branch_grad, sent, sums_two, *ups = block_backward(
            core, grad, hidden, w_down, w_up, w_out, n2, r2, ln2_gain, members, grads
        )
        own_grad = lax.all_to_all(sent, low, 0, 0, tiled=True).reshape(members * rows, W)
        if last:
            z_other, x_other, z_own, x_own = ups
            z_core = swap(z_other, "core")
            left, right = (later[0], pin(down_grad, sent)), (later[1], activated)
            d_other, d_own = grad_rows(core, left, right, bands, 0, 1)
            d_core = swap(d_other, "core")
            x_other, x_own = grad_out(
                core, (later[4], pin(branch_grad, d_other)), (later[5], attended), bands, x_other, x_own
            )
            x_core = swap(x_other, "core")
            samp = ("samp",) * two
            z_terms = pin((z_own, z_core), x_other)
            z_share = Share([split_rows(t, two) for t in z_terms], names + samp)
            d_terms = pin((d_own, d_core), z_share.halve("zl"))
            down_share = Share([split_rows(t, two) for t in d_terms], names + samp)
            x_terms = pin((x_own, x_core), down_share.halve("samp"))
            x_share = Share([split_rows(t, two) for t in x_terms], names + samp)
            own_grad = pin(own_grad, x_share.halve(x_axes[0]))
            heads = W // HD
            d_heads = attend_back(*owns[0], own_grad, members, range((heads + 1) // 2))
            own_grad, d_heads, z_share.terms[-1] = pin((own_grad, d_heads, z_share.terms[-1]))
            sent = z_share.halve("zh")
            if heads > 1:
                own_grad, d_heads = pin((own_grad, d_heads), sent)
                d_heads = attend_back(*owns[0], own_grad, members, range(heads // 2, heads), d_heads)
            shares = (z_share, x_share, down_share)
            waits = pin((d_heads, *(t.terms[-1] for t in shares)))
            d_heads = waits[0]
            for t, value in zip(shares, waits[1:]):
                t.terms[-1] = value
            sent = [x_share.halve("samp"), z_share.halve("samp")] + [down_share.halve(a) for a in x_axes]
            d_heads = pin(d_heads, *sent)
        else:
            own_grad, send_row, keep_rows = pin((own_grad, send_row, keep_rows), result)
            later = (down_grad, activated, hidden_grad, normed_two, branch_grad, attended)
            owns[index] = own_part(index)
            d_heads = attend_back(*owns[index], own_grad, members)
        back = lax.all_to_all(d_heads, low, 0, 0, tiled=True)
        w_heads = grad_heads(d_heads, normed_all, w_heads, bf16 if last else f32)
        if last:
            units = w_heads.reshape(-1, unit, D)
            if two:
                there = lax.dynamic_slice_in_dim(units, (1 - y) * (D // 2), D // 2, 2)
                here = lax.dynamic_slice_in_dim(units, y * (D // 2), D // 2, 2)
                units = [here, swap(there, "samp")]
            else:
                there, units = units, [units]
            back = pin(back, there)
            x_share.terms[-1], z_share.terms[-1] = pin((x_share.terms[-1], z_share.terms[-1]), back)
            sent = [x_share.halve(a) for a in x_axes[1:] + ("zl",)] + [z_share.halve(a) for a in x_axes]
            units[-1] = pin(units[-1], *sent)
            outgoing = take(units, send_row)
            incoming = lax.all_to_all(outgoing, low, 0, 0, tiled=True)
            down_share.terms[-1] = pin(down_share.terms[-1], outgoing)
            back = pin(back, down_share.halve("zl"))
        else:
            owns[0] = own_part(0)
            back = pin(back, w_heads, *owns[0])
        grad, low_grad, sums_one, sums_qv = qkv_backward(
            back, w_qkv, middle_grad, n1, r1, ln1_gain, half if last else rows
        )
        down_grad = low_grad
        step_small = (sums_one[:3], sums_qv[:2], sums_two[:4], hidden_sum)
        small = step_small if small is None else tuple(a + b for a, b in zip(small, step_small))
    fields_sent = low_grad
    fields_other = swap(fields_sent, "zh")
    x_share.terms[-1] = pin(x_share.terms[-1], fields_sent)
    incoming = pin(incoming, x_share.halve("zh"))
    there = take([incoming], keep_rows[1])
    other = swap(there, "zh")
    one, qv, two_sums, up_sum = pin(small, there)
    samples = 2 * samp_count
    slot = 2 * y + zh
    mine = lax.broadcasted_iota(jnp.int32, (samples, 1), 0) == slot
    leads = jnp.where(mine, one[2:3], 0.0)
    lane = lax.broadcasted_iota(jnp.int32, (bands, D // bands), 1) == slot
    bucket = jnp.where(lane & (me == 0), pick(lead_bucket, zh).astype(f32), 0.0)
    vectors = jnp.concatenate([one[:2], qv, two_sums, leads])
    vectors = vectors.reshape(-1, bands, D // bands).transpose(1, 0, 2).reshape(bands, -1)
    vectors = jnp.concatenate([vectors, up_sum.reshape(bands, -1), bucket], axis=1)
    sums = vectors
    vectors = lax.all_to_all(vectors, band, 0, 0, tiled=True)

    def both(x):
        x = x.astype(bf16)
        if not two:
            return lax.psum(x, "samp").astype(f32)
        other = swap(x, "samp")
        return jnp.concatenate([jnp.where(y == 0, x, other), jnp.where(y == 0, other, x)]).astype(f32)

    def both_cut(x, n):
        if not two:
            x = both(x)
            return x[:n], x[n:]
        x = x.astype(bf16)
        other = swap(x, "samp")
        first, second = jnp.where(y == 0, x, other), jnp.where(y == 0, other, x)
        x = jnp.concatenate([first, second]).astype(f32)
        return x[:n], x[n:]

    incoming, down_share.terms[-1], z_share.terms[-1] = pin((incoming, down_share.terms[-1], z_share.terms[-1]), sums)
    sent = down_share.halve("zh")
    own = take([incoming], keep_rows[0])
    up_first = total(z_share.terms).astype(bf16)
    late = (vectors, fields_other, other, down_share.terms[-1], x_share.terms[-1])
    late = pin(late, sent, own, up_first)
    vectors, fields_other, other, down_share.terms[-1], x_share.terms[-1] = late
    vectors = jnp.sum(vectors, axis=0)
    vectors = vectors + swap(vectors, "samp") if two else lax.psum(vectors, "samp")
    own = total([own, other]).astype(bf16).reshape(3 * D // bands, -1)
    if two:
        other = swap(own, "samp")
        own = jnp.concatenate([jnp.where(y == 0, own, other), jnp.where(y == 0, other, own)], axis=1)
    else:
        own = lax.psum(own, "samp")
    w_qkv_grad = own.astype(f32).T

    w_down_grad = both(total(down_share.terms)).T
    n_up = w_up.shape[1] // bands
    bottom = both_cut(total(x_share.terms), n_up // 2)
    w_out_grad = bottom[1].T
    w_up_grad = jnp.concatenate([both(up_first), bottom[0]]).T
    fields_grad = join(zh, grad, fields_other)

    w = D // bands
    leads = vectors[8 * w : (8 + samples) * w].reshape(samples, w)
    up_grad = vectors[(8 + samples) * w : -w]
    buckets = vectors[-w:][:samples].astype(jnp.int32)
    one_hot = (buckets[:, None] == jnp.arange(lead_table.shape[0], dtype=jnp.int32)[None, :]).astype(f32)
    lead_grad = jnp.dot(one_hot.T, leads, precision=lax.Precision.HIGHEST)
    rows_of = lambda i: vectors[i * w : (i + 1) * w]
    g = [rows_of(i) for i in (0, 1, 2, 3, 6, 4, 5)] + [up_grad, rows_of(7)]
    return (
        result,
        fields_grad,
        lead_grad,
        g[0],
        g[1],
        w_qkv_grad,
        g[2],
        g[3],
        w_out_grad,
        g[4],
        g[5],
        g[6],
        w_up_grad,
        g[7],
        w_down_grad,
        g[8],
    )


def solution(mesh):
    samp_count, band_count = mesh.shape["samp"], mesh.shape["band"]
    x_axes = tuple(f"x{i}" for i in range((band_count // 8).bit_length() - 1))
    axes = ("zh", "zl") + x_axes + ("core",)
    assert 2 ** len(axes) == band_count
    fine = Mesh(mesh.devices.reshape((samp_count,) + (2,) * len(axes)), ("samp",) + axes)
    tokens = P("samp", axes, None)
    columns, vector = P(None, axes), P(axes)
    in_specs = (tokens, P("samp"), tokens) + (P(),) * 14
    out_specs = (
        tokens,
        tokens,
        columns,
        vector,
        vector,
        columns,
        vector,
        vector,
        columns,
        vector,
        vector,
        vector,
        columns,
        vector,
        columns,
        vector,
    )
    run = functools.partial(body, axes=axes, x_axes=x_axes, samp_count=samp_count)
    return jax.shard_map(run, mesh=fine, in_specs=in_specs, out_specs=out_specs, check_vma=False)
```

```python
import functools
import math

import jax
import jax.numpy as jnp
import numpy as np
from jax import lax
from jax.experimental import pallas as pl
from jax.experimental.pallas import tpu as pltpu
from jax.sharding import Mesh
from jax.sharding import PartitionSpec as P

HD = 64
STEPS = 2
EPS = 1e-05
EXP_SCALE = 0.125 * 1.4426950408889634
GELU_A = 0.7978845608028654
GELU_B = 0.044715
MIB = 2**20
SWAP = [(0, 1), (1, 0)]
f32 = jnp.float32
bf16 = jnp.bfloat16


def cost(us):
    return pl.CostEstimate(flops=int(us * 1.15e9), bytes_accessed=1000, transcendentals=0)


def contract(a, b, a_dim, b_dim):
    return lax.dot_general(a, b, (((a_dim,), (b_dim,)), ((), ())), preferred_element_type=f32)


def head_part(x, h, heads):
    if heads == 1:
        return x
    lane = lax.broadcasted_iota(jnp.int32, x.shape, 1)
    return jnp.where(lane // HD == h, x, jnp.zeros_like(x))


def attend_kernel(q_ref, n_ref, wk_ref, wv_ref, b_ref, o_ref):
    normed = n_ref[...]
    keys = contract(normed, wk_ref[...], 1, 0).astype(bf16)
    values = (contract(normed, wv_ref[...], 1, 0) + b_ref[...]).astype(bf16)
    pair = 2 * HD
    for start in range(0, q_ref.shape[1], pair):
        q, k, v = q_ref[:, start : start + pair], keys[:, start : start + pair], values[:, start : start + pair]
        out = None
        for h in range(2):
            s = contract(head_part(q, h, 2), k, 1, 1)
            top = jnp.max(s, axis=-1, keepdims=True)
            e = jnp.exp2((s - top) * EXP_SCALE)
            total = jnp.sum(e, axis=-1, keepdims=True)
            o = head_part(contract(e.astype(bf16), v, 1, 0) / total, h, 2)
            out = o if out is None else out + o
        o_ref[:, start : start + pair] = out.astype(bf16)


def attend(q, normed_all, w_qkv, v_bias):
    rows, width = q.shape
    count = normed_all.shape[0]
    block = 4 * HD
    own = spec((rows, block), lambda j: (0, j))
    shift = width // block
    return pl.pallas_call(
        attend_kernel,
        grid=(width // block,),
        in_specs=[
            own,
            spec((count, width), lambda j: (0, 0)),
            spec((width, block), lambda j: (0, shift + j)),
            spec((width, block), lambda j: (0, 2 * shift + j)),
            spec((1, block), lambda j: (0, j)),
        ],
        out_specs=own,
        out_shape=jax.ShapeDtypeStruct((rows, width), bf16),
        compiler_params=pltpu.CompilerParams(vmem_limit_bytes=40 * MIB),
        cost_estimate=cost(24),
        name="attend",
    )(q, normed_all, w_qkv, w_qkv, v_bias.reshape(1, width))


def attend_back_kernel(q_ref, k_ref, v_ref, do_ref, *rest, heads, some):
    out_ref, dk_sum, dv_sum = rest[-3:]
    step = pl.program_id(0)
    rows = q_ref.shape[0]

    @pl.when(step == 0)
    def _():
        dk_sum[...] = jnp.zeros_like(dk_sum)
        dv_sum[...] = jnp.zeros_like(dv_sum)

    q, k, v, do = q_ref[...], k_ref[...], v_ref[...], do_ref[...]
    queries = [head_part(q, h, heads) for h in some]
    grads = [head_part(do, h, heads) for h in some]
    scores = [contract(x, k, 1, 1) for x in queries]
    prob_grads = [contract(x, v, 1, 1) for x in grads]
    dq = dk = dv = 0.0
    for h, qh, doh, s, dp in zip(some, queries, grads, scores, prob_grads):
        top = jnp.max(s, axis=-1, keepdims=True)
        e = jnp.exp2((s - top) * EXP_SCALE)
        inverse = 1.0 / jnp.sum(e, axis=-1, keepdims=True)
        inner = jnp.sum(e * dp, axis=-1, keepdims=True) * inverse
        p = e * inverse
        ds = (p * (dp - inner)).astype(bf16)
        dq = dq + head_part(contract(ds, k, 1, 0), h, heads)
        dk = dk + contract(ds, qh, 0, 0)
        dv = dv + contract(p.astype(bf16), doh, 0, 0)
    dk_sum[...] += dk
    dv_sum[...] += dv

    def put(m, i, x):
        if len(rest) == 4:
            x = x + rest[0][m, i].astype(f32)
        out_ref[m, i] = x.astype(bf16)

    put(step, 0, dq * 0.125)

    @pl.when(step == pl.num_programs(0) - 1)
    def _():
        for m in range(out_ref.shape[0]):
            put(m, 1, dk_sum[m * rows : (m + 1) * rows, :] * 0.125)
            put(m, 2, dv_sum[m * rows : (m + 1) * rows, :])


def attend_back(q, k, v, do, members, some=None, add=None):
    count, width = q.shape
    rows = count // members
    heads = width // HD
    part = pl.BlockSpec((rows, width), lambda i: (i, 0))
    full = pl.BlockSpec((count, width), lambda i: (0, 0))
    shape = (members, 3, rows, width)
    out = pl.BlockSpec(shape, lambda i: (0, 0, 0, 0))
    extra = [] if add is None else [add]
    return pl.pallas_call(
        functools.partial(attend_back_kernel, heads=heads, some=some or range(heads)),
        grid=(members,),
        in_specs=[part, full, full, part] + [out] * len(extra),
        out_specs=out,
        out_shape=jax.ShapeDtypeStruct(shape, bf16),
        scratch_shapes=[pltpu.VMEM((count, width), f32), pltpu.VMEM((count, width), f32)],
        compiler_params=pltpu.CompilerParams(vmem_limit_bytes=60 * MIB),
        cost_estimate=cost(33 if some is None else 17),
        name="attend_back",
    )(q, k, v, do, *extra)


def spec(block, index):
    return pl.BlockSpec(block, index)


def grad_rows_kernel(c_ref, l1, l0, r1, r0, other_ref, own_ref, sums):
    sums[...] = contract(l1[...], r1[...], 0, 0) + contract(l0[...], r0[...], 0, 0)
    count, n, _ = own_ref.shape
    for j in range(count):
        for ref, core in ((other_ref, 1 - c_ref[0]), (own_ref, c_ref[0])):
            ref[j] = sums[pl.ds(pl.multiple_of((2 * j + core) * n, n), n), :].astype(bf16)


def grad_rows(core, left, right, bands, part, parts):
    tokens, m = left[0].shape
    n = right[0].shape[1] // parts
    block = min(n, 512)
    first = part * (n // block)
    out = spec((bands // 2, m // bands, block), lambda j, c: (0, 0, j))
    whole = spec((tokens, m), lambda j, c: (0, 0))
    part = spec((tokens, block), lambda j, c: (0, first + j))
    return pl.pallas_call(
        grad_rows_kernel,
        grid_spec=pltpu.PrefetchScalarGridSpec(
            num_scalar_prefetch=1,
            grid=(n // block,),
            in_specs=[whole, whole, part, part],
            out_specs=[out, out],
            scratch_shapes=[pltpu.VMEM((m, block), f32)],
        ),
        out_shape=[jax.ShapeDtypeStruct((bands // 2, m // bands, n), bf16)] * 2,
        compiler_params=pltpu.CompilerParams(vmem_limit_bytes=60 * MIB),
        cost_estimate=cost(8),
        name="grad_rows",
    )(core.reshape(1), *left, *right)


def block_forward_kernel(
    x_ref, a_ref, wo_ref, bo_ref, g_ref, b_ref, wu_ref, bu_ref, wd_ref, bd_ref, lead_ref, g1_ref, b1_ref,
    n2_ref, r2_ref, low2_ref, hidden_ref, act_ref, *rest, last
):
    total = rest[-1]
    step = pl.program_id(0)

    @pl.when(step == 0)
    def _():
        middle = x_ref[...] + contract(a_ref[...], wo_ref[...], 1, 0) + bo_ref[...]
        n, r = norm_parts(middle)
        n2_ref[...] = n
        r2_ref[...] = r
        low2_ref[...] = (n * g_ref[...] + b_ref[...]).astype(bf16)
        total[...] = middle + bd_ref[...]

    hidden = contract(low2_ref[...], wu_ref[...], 1, 0) + bu_ref[...]
    hidden_ref[...] = hidden
    act = gelu(hidden).astype(bf16)
    act_ref[...] = act
    total[...] += contract(act, wd_ref[...], 1, 0)

    @pl.when(step == pl.num_programs(0) - 1)
    def _():
        carried = total[...]
        if last:
            rest[0][...] = carried.astype(bf16)
        else:
            x = carried + lead_ref[...]
            n, r = norm_parts(x)
            rest[0][...] = x
            rest[1][...] = n
            rest[2][...] = r
            rest[3][...] = (n * g1_ref[...] + b1_ref[...]).astype(bf16)


def block_forward(inputs, attended, weights, last):
    w_out, out_bias, ln2_gain, ln2_bias, w_up, up_bias, w_down, down_bias, lead, ln1_gain, ln1_bias = weights
    t, d = inputs.shape
    f = w_up.shape[1]
    block = 512
    row = lambda v: v.reshape(1, -1)
    full = spec((t, d), lambda i: (0, 0))
    vec = spec((1, d), lambda i: (0, 0))
    one = spec((t, 1), lambda i: (0, 0))
    wide = spec((t, block), lambda i: (0, i))
    shape = jax.ShapeDtypeStruct
    outs = [full, one, full, wide, wide] + ([full] if last else [full, full, one, full])
    shapes = [shape((t, d), f32), shape((t, 1), f32), shape((t, d), bf16), shape((t, f), f32), shape((t, f), bf16)]
    shapes += [shape((t, d), bf16)] if last else [
        shape((t, d), f32), shape((t, d), f32), shape((t, 1), f32), shape((t, d), bf16)
    ]
    return pl.pallas_call(
        functools.partial(block_forward_kernel, last=last),
        grid=(f // block,),
        in_specs=[
            full, full, spec((d, d), lambda i: (0, 0)), vec, vec, vec,
            spec((d, block), lambda i: (0, i)), spec((1, block), lambda i: (0, i)),
            spec((block, d), lambda i: (i, 0)), vec, vec, vec, vec,
        ],
        out_specs=outs,
        out_shape=shapes,
        scratch_shapes=[pltpu.VMEM((t, d), f32)],
        compiler_params=pltpu.CompilerParams(vmem_limit_bytes=40 * MIB),
        cost_estimate=cost(12),
        name="block_forward",
    )(
        inputs, attended, w_out, row(out_bias), row(ln2_gain), row(ln2_bias), w_up, row(up_bias), w_down,
        row(down_bias), row(lead), row(ln1_gain), row(ln1_bias),
    )


def put_sums(ref, *sums):
    for i, v in enumerate(sums):
        ref[i : i + 1, :] = v


def column_sum(x):
    return jnp.sum(x.astype(f32), axis=0, keepdims=True)


def block_backward_kernel(c_ref, grad_ref, h_ref, wd_ref, wu_ref, wo_ref, n_ref, r_ref, g_ref, *rest, grads, bands):
    if grads:
        l1_ref, x1_ref, x0_ref = rest[:3]
        z_other, x_other, z_own, x_own = rest[9:13]
        sums, rest = rest[14], rest[3:9] + rest[13:14]
    hg_ref, hsum_ref, middle_ref, branch_ref, sent_ref, sums_ref, total = rest
    step = pl.program_id(0)
    down = grad_ref[...].astype(bf16)
    low = (gelu_slope(h_ref[...]) * contract(down, wd_ref[...], 1, 1)).astype(bf16)
    hg_ref[...] = low
    hsum_ref[...] = column_sum(low)
    part = contract(low, wu_ref[...], 1, 1)
    if grads:
        sums[...] = contract(l1_ref[...], x1_ref[...], 0, 0) + contract(low, x0_ref[...], 0, 0)
        pairs = z_own.shape[0]
        n = sums.shape[0] // (2 * pairs)
        for q in range(pairs):
            for z, x, core in ((z_other, x_other, 1 - c_ref[0]), (z_own, x_own, c_ref[0])):
                start = pl.multiple_of((2 * q + core) * n, n)
                z[q] = sums[pl.ds(start, n // 2), :].astype(bf16)
                x[q] = sums[pl.ds(start + n // 2, n // 2), :].astype(bf16)

    @pl.when(step == 0)
    def _():
        total[...] = part

    @pl.when(step > 0)
    def _():
        total[...] += part

    @pl.when(step == pl.num_programs(0) - 1)
    def _():
        dv, gain, bias = norm_back(total[...], n_ref[...], r_ref[...], g_ref[...])
        middle = grad_ref[...] + dv
        middle_ref[...] = middle
        branch = middle.astype(bf16)
        branch_ref[...] = branch
        put_sums(sums_ref, gain, bias, column_sum(branch), column_sum(down))
        w = sent_ref.shape[2]
        attended = contract(branch, wo_ref[...], 1, 1).astype(bf16)
        for m in range(sent_ref.shape[0]):
            sent_ref[m] = attended[:, m * w : (m + 1) * w]


def block_backward(core, grad, hidden, w_down, w_up, w_out, n2, r2, gain, members, grads=()):
    t, d = grad.shape
    f = hidden.shape[1]
    block = 512
    bands = 2 * members
    full = spec((t, d), lambda i, c: (0, 0))
    wide = spec((t, block), lambda i, c: (0, i))
    sent = (members, t, d // members)
    shape = jax.ShapeDtypeStruct
    outs = [
        wide, spec((1, block), lambda i, c: (0, i)), full, full,
        spec(sent, lambda i, c: (0, 0, 0)), spec((8, d), lambda i, c: (0, 0)),
    ]
    shapes = [
        shape((t, f), bf16), shape((1, f), f32), shape((t, d), f32), shape((t, d), bf16),
        shape(sent, bf16), shape((8, d), f32),
    ]
    scratch = [pltpu.VMEM((t, d), f32)]
    if grads:
        n = f // bands
        pairs = block // (2 * n)
        part = spec((pairs, n // 2, d), lambda i, c: (i, 0, 0))
        outs += [part] * 4
        shapes += [shape((bands // 2, n // 2, d), bf16), shape((bands // 2, n // 2 + d // bands, d), bf16)] * 2
        scratch += [pltpu.VMEM((block, d), f32)]
    return pl.pallas_call(
        functools.partial(block_backward_kernel, grads=bool(grads), bands=bands),
        grid_spec=pltpu.PrefetchScalarGridSpec(
            num_scalar_prefetch=1,
            grid=(f // block,),
            in_specs=[
                full, wide, spec((block, d), lambda i, c: (i, 0)), spec((d, block), lambda i, c: (0, i)),
                spec((d, d), lambda i, c: (0, 0)), full, spec((t, 1), lambda i, c: (0, 0)),
                spec((1, d), lambda i, c: (0, 0)),
            ] + [wide, full, full][: len(grads)],
            out_specs=outs,
            scratch_shapes=scratch,
        ),
        out_shape=shapes,
        compiler_params=pltpu.CompilerParams(vmem_limit_bytes=(60 if grads else 48) * MIB),
        cost_estimate=cost(18 if grads else 14),
        name="block_backward",
    )(core.reshape(1), grad, hidden, w_down, w_up, w_out, n2, r2, gain.reshape(1, d), *grads)


def grad_out_kernel(c_ref, l1, l0, r1, r0, _, __, other_ref, own_ref, sums, *, pairs):
    sums[...] = contract(l1[...], r1[...], 0, 0) + contract(l0[...], r0[...], 0, 0)
    n = own_ref.shape[1]
    for q in range(pairs):
        for ref, core in ((other_ref, 1 - c_ref[0]), (own_ref, c_ref[0])):
            ref[q] = sums[pl.ds(pl.multiple_of((2 * q + core) * n, n), n), :].astype(bf16)


def grad_out(core, left, right, bands, other, own):
    tokens, m = left[0].shape
    count, height, d = own.shape
    n = m // bands
    pairs = max(1, 256 // (2 * n))
    columns = spec((tokens, 2 * n * pairs), lambda j, c: (0, j))
    whole = spec((tokens, d), lambda j, c: (0, 0))
    out = spec((pairs, n, d), lambda j, c: (j, height // n - 1, 0))
    anywhere = pl.BlockSpec(memory_space=pl.ANY)
    return pl.pallas_call(
        functools.partial(grad_out_kernel, pairs=pairs),
        grid_spec=pltpu.PrefetchScalarGridSpec(
            num_scalar_prefetch=1,
            grid=(count // pairs,),
            in_specs=[columns, columns, whole, whole, anywhere, anywhere],
            out_specs=[out, out],
            scratch_shapes=[pltpu.VMEM((2 * n * pairs, d), f32)],
        ),
        out_shape=[jax.ShapeDtypeStruct(own.shape, bf16)] * 2,
        input_output_aliases={5: 0, 6: 1},
        compiler_params=pltpu.CompilerParams(vmem_limit_bytes=60 * MIB),
        cost_estimate=cost(3),
        name="grad_out",
    )(core.reshape(1), *left, *right, other, own)


def qkv_backward_kernel(b_ref, wq_ref, wk_ref, wv_ref, m_ref, n_ref, r_ref, g_ref, grad_ref, low_ref, sums_ref, qv_ref, total):
    step = pl.program_id(0)
    w = b_ref.shape[3]
    part = None
    for m in range(b_ref.shape[0]):
        for i, ref in enumerate((wq_ref, wk_ref, wv_ref)):
            x = contract(b_ref[m, i], ref[:, m * w : (m + 1) * w], 1, 1)
            part = x if part is None else part + x
        qv_ref[0:1, m * w : (m + 1) * w] = column_sum(b_ref[m, 0])
        qv_ref[1:2, m * w : (m + 1) * w] = column_sum(b_ref[m, 2])

    @pl.when(step == 0)
    def _():
        total[...] = part

    @pl.when(step > 0)
    def _():
        total[...] += part

    @pl.when(step == pl.num_programs(0) - 1)
    def _():
        dv, gain, bias = norm_back(total[...], n_ref[...], r_ref[...], g_ref[...])
        grad = m_ref[...] + dv
        grad_ref[...] = grad
        low_ref[...] = grad[grad.shape[0] - low_ref.shape[0] :].astype(bf16)
        put_sums(sums_ref, gain, bias, column_sum(grad))


def qkv_backward(back, w_qkv, middle_grad, n1, r1, gain, low):
    members, _, t, w = back.shape
    d = members * w
    at_once = max(2, 128 // w)
    block = at_once * w
    shift = d // block
    full = spec((t, d), lambda i: (0, 0))
    weight = [spec((d, block), lambda i, s=s: (0, s * shift + i)) for s in range(3)]
    shape = jax.ShapeDtypeStruct
    return pl.pallas_call(
        qkv_backward_kernel,
        grid=(members // at_once,),
        in_specs=[spec((at_once, 3, t, w), lambda i: (i, 0, 0, 0))] + weight + [
            full, full, spec((t, 1), lambda i: (0, 0)), spec((1, d), lambda i: (0, 0)),
        ],
        out_specs=[
            full, spec((low, d), lambda i: (0, 0)), spec((8, d), lambda i: (0, 0)),
            spec((8, block), lambda i: (0, i)),
        ],
        out_shape=[
            shape((t, d), f32), shape((low, d), bf16), shape((8, d), f32), shape((8, d), f32),
        ],
        scratch_shapes=[pltpu.VMEM((t, d), f32)],
        compiler_params=pltpu.CompilerParams(vmem_limit_bytes=60 * MIB),
        cost_estimate=cost(12),
        name="qkv_backward",
    )(back, w_qkv, w_qkv, w_qkv, middle_grad, n1, r1, gain.reshape(1, d))


def grad_heads_kernel(d_ref, n_ref, *rest):
    out_ref = rest[-1]
    rows = d_ref.shape[2]
    for i in range(3):
        total = rest[0][i] if len(rest) == 2 else jnp.zeros(out_ref.shape[1:], f32)
        for m in range(d_ref.shape[0]):
            total += contract(d_ref[m, i], n_ref[m * rows : (m + 1) * rows, :], 0, 0)
        out_ref[i] = total.astype(out_ref.dtype)


def grad_heads(d, normed_all, add, kind):
    members, _, rows, width = d.shape
    dim = normed_all.shape[1]
    shape = (3, width, dim)
    out = spec((3, width, dim // 4), lambda i: (0, 0, i))
    extra = [] if add is None else [add]
    return pl.pallas_call(
        grad_heads_kernel,
        grid=(4,),
        in_specs=[
            spec(d.shape, lambda i: (0, 0, 0, 0)),
            spec((members * rows, dim // 4), lambda i: (0, i)),
        ]
        + [out] * len(extra),
        out_specs=out,
        out_shape=jax.ShapeDtypeStruct(shape, kind),
        compiler_params=pltpu.CompilerParams(vmem_limit_bytes=60 * MIB),
        cost_estimate=cost(5),
        name="grad_heads",
    )(d, normed_all, *extra)


def take_kernel(table, *refs):
    for i in range(refs[-1].shape[0]):
        total = refs[0][table[i]].astype(f32)
        for r in refs[1:-1]:
            total = total + r[table[i]].astype(f32)
        refs[-1][i] = total.astype(bf16)


def take(terms, table):
    shape = terms[0].shape
    count = table.shape[0]
    return pl.pallas_call(
        take_kernel,
        grid_spec=pltpu.PrefetchScalarGridSpec(
            num_scalar_prefetch=1,
            grid=(1,),
            in_specs=[spec(shape, lambda i, t: (0, 0, 0))] * len(terms),
            out_specs=spec((count,) + shape[1:], lambda i, t: (0, 0, 0)),
        ),
        out_shape=jax.ShapeDtypeStruct((count,) + shape[1:], bf16),
        compiler_params=pltpu.CompilerParams(vmem_limit_bytes=60 * MIB),
        cost_estimate=cost(3),
        name="take",
    )(table, *terms)


def join_kernel(i_ref, own_ref, other_ref, out_ref):
    half = other_ref.shape[0]
    out_ref[i_ref[0]] = own_ref[:half]
    out_ref[1 - i_ref[0]] = other_ref[...].astype(f32)


def join(index, own, other):
    half, d = other.shape
    full = spec((half, d), lambda i, c: (0, 0))
    return pl.pallas_call(
        join_kernel,
        grid_spec=pltpu.PrefetchScalarGridSpec(
            num_scalar_prefetch=1,
            grid=(1,),
            in_specs=[full, full],
            out_specs=spec((2, half, d), lambda i, c: (0, 0, 0)),
        ),
        out_shape=jax.ShapeDtypeStruct((2, half, d), f32),
        compiler_params=pltpu.CompilerParams(vmem_limit_bytes=8 * MIB),
        cost_estimate=cost(2),
        name="join",
    )(index.reshape(1), own, other)


def unit_tables(bands, x_count, width, dim):
    members = bands // 2
    unit = math.gcd(HD, 3 * dim // bands)
    per_band = 3 * dim // bands // unit
    made, slots, place = [], [], {}
    for g in range(members):
        units = [(b * dim + g * width) // unit + i for b in range(3) for i in range(width // unit)]
        by_low = [[] for _ in range(members)]
        for local, u in enumerate(units):
            band = u // per_band
            core, x, zl = band % 2, band // 2 % x_count, band // (2 * x_count) % 2
            low = (core * 2 + zl) * x_count + x
            place[u] = (g, len(by_low[low]))
            by_low[low].append(local)
        made.append(by_low)
    most = max(len(l) for by_low in made for l in by_low)
    send = np.zeros((members, members * most), np.int32)
    for g, by_low in enumerate(made):
        for low, locals_ in enumerate(by_low):
            for m, local in enumerate(locals_):
                send[g, low * most + m] = local
    keep = np.zeros((members, 2, per_band), np.int32)
    for u, (g, m) in place.items():
        band = u // per_band
        core, x, zl = band % 2, band // 2 % x_count, band // (2 * x_count) % 2
        low = (core * 2 + zl) * x_count + x
        keep[low, band // members, u % per_band] = g * most + m
    return unit, send, keep


def norm_parts(v):
    centred = v - jnp.mean(v, axis=-1, keepdims=True)
    r = lax.rsqrt(jnp.mean(centred * centred, axis=-1, keepdims=True) + EPS)
    return centred * r, r


def norm_back(dy, n, r, gain):
    dyg = dy * gain
    mean_one = jnp.mean(dyg, axis=-1, keepdims=True)
    mean_two = jnp.mean(dyg * n, axis=-1, keepdims=True)
    dv = r * (dyg - mean_one - n * mean_two)
    return dv, jnp.sum(dy * n, axis=0, keepdims=True), jnp.sum(dy, axis=0, keepdims=True)


def gelu(x):
    return 0.5 * x * (1.0 + jnp.tanh(GELU_A * (x + GELU_B * x * x * x)))


def gelu_slope(x):
    t = jnp.tanh(GELU_A * (x + GELU_B * x * x * x))
    return 0.5 * (1.0 + t) + 0.5 * x * (1.0 - t * t) * (GELU_A * (1.0 + 3.0 * GELU_B * x * x))


def dot(a, b):
    return jnp.dot(a, b, preferred_element_type=f32)


def dot_t(a, b):
    return contract(a, b, 1, 1)


def swap(x, axis):
    return lax.ppermute(x, axis, SWAP)


def pin(x, *first):
    return lax.optimization_barrier((x,) + first)[0]


def total(terms):
    out = terms[0].astype(f32)
    for t in terms[1:]:
        out = out + t.astype(f32)
    return out


class Share:
    def __init__(self, terms, names):
        self.terms = list(terms)
        self.names = list(names)

    def halve(self, axis, *first):
        if axis not in self.names:
            return self.terms[-1]
        dim = self.names.index(axis)
        i = lax.axis_index(axis)
        terms = [pin(t, *first) if first else t for t in self.terms[-1:]] + self.terms[:-1]
        there = [lax.dynamic_index_in_dim(t, 1 - i, dim, keepdims=False) for t in terms]
        self.terms = [lax.dynamic_index_in_dim(t, i, dim, keepdims=False) for t in terms]
        self.names.remove(axis)
        sent = total(there).astype(bf16)
        self.terms.append(swap(sent, axis))
        return sent


def body(
    fields,
    lead_bucket,
    cotangent,
    lead_table,
    ln1_gain,
    ln1_bias,
    w_qkv,
    q_bias,
    v_bias,
    w_out,
    out_bias,
    ln2_gain,
    ln2_bias,
    w_up,
    up_bias,
    w_down,
    down_bias,
    *,
    axes,
    x_axes,
    samp_count,
):
    band = tuple(axes)
    low = ("core", "zl") + x_axes[::-1]
    members = 2 ** len(low)
    order = x_axes + ("zl", "core")
    D = w_out.shape[0]
    W = D // members
    half = fields.shape[1]
    rows = 2 * half
    two = samp_count == 2
    zh = lax.axis_index("zh")
    me = lax.axis_index(low)

    def pick(x, i):
        return lax.dynamic_index_in_dim(x, i, 0, keepdims=False)

    def to_sample(x):
        return jnp.concatenate([pick(x, zh), swap(pick(x, 1 - zh), "zh")])

    def to_band(x):
        own = x[:half]
        other = swap(x[half:].astype(bf16), "zh").astype(x.dtype)
        return jnp.where(zh == 0, jnp.stack([own, other]), jnp.stack([other, own]))

    def gather(x):
        if len(x_axes) == 1:
            x_axis = x_axes[0]
            cut = x.shape[0] // 2
            by_x = swap(x, x_axis)
            by_z = swap(x, "zl")
            far = [swap(by_x[:cut], "zl"), swap(by_z[cut:], x_axis)]
            pieces = [(x, 0, 0), (by_x, 1, 0), (by_z, 2, 0), (far[0], 3, 0), (far[1], 3, cut)]
            pieces += [(swap(p, "core"), 4 + k, o) for p, k, o in pieces]
        else:
            pieces = [(x, 0, 0)]
            for bit, axis in enumerate(order):
                pieces += [(swap(p, axis), k + 2**bit, 0) for p, k, _ in pieces]
        out = jnp.zeros((members * rows, D), bf16)
        for piece, k, offset in pieces:
            out = lax.dynamic_update_slice(out, piece, ((me ^ k) * rows + offset, 0))
        return out

    lead_row = pick(lead_table, pick(lead_bucket, zh)).astype(f32)
    carried = to_sample(fields).astype(f32)

    def member_columns(x, block):
        return lax.dynamic_slice_in_dim(x, block * D + me * W, W, x.ndim - 1)

    kept = []
    inputs = carried + lead_row
    n1, r1 = norm_parts(inputs)
    normed = (n1 * ln1_gain + ln1_bias).astype(bf16)
    weights = (w_out, out_bias, ln2_gain, ln2_bias, w_up, up_bias, w_down, down_bias, lead_row, ln1_gain, ln1_bias)
    for index in range(STEPS):
        normed_all = gather(normed)
        queries = (dot(normed, w_qkv[:, :D]) + q_bias).astype(bf16)
        if index == 0:
            out_grad = to_sample(pin(cotangent, normed_all))
        attended = attend(queries, normed_all, w_qkv, v_bias)
        if index == 0:
            attended, out_grad = pin((attended, out_grad))
        last = index == STEPS - 1
        n2, r2, normed_two, hidden, activated, *after = block_forward(inputs, attended, weights, last)
        kept.append((n1, r1, normed_all, attended, n2, r2, normed_two, hidden, activated))
        if not last:
            inputs, n1, r1, normed = after
    carried = after[0]
    result = to_band(carried)

    grad = out_grad
    small = None
    core = lax.axis_index("core")
    y = lax.axis_index("samp")
    bands = 2 ** len(axes)
    names = axes[:-1]
    cube = (2,) * len(names)
    later = None
    w_heads = None
    unit, send_table, keep_table = unit_tables(bands, 2 ** len(x_axes), W, D)
    send_row, keep_row = pick(jnp.asarray(send_table), me), pick(jnp.asarray(keep_table), me)
    keep_rows = pick(keep_row, zh), pick(keep_row, 1 - zh)
    def split_rows(x, rows_two):
        n, r, c = x.shape
        return x.reshape(cube + ((2, r // 2) if rows_two else (r,)) + (c,))

    own_weight = jnp.concatenate([member_columns(w_qkv, i) for i in range(3)], axis=1)
    own_bias = jnp.concatenate([member_columns(q_bias, 0), jnp.zeros((W,), f32), member_columns(v_bias, 0)])

    def own_part(index):
        own = (dot(kept[index][2], own_weight) + own_bias).astype(bf16)
        return own[:, :W], own[:, W : 2 * W], own[:, 2 * W :]

    owns = {}
    for index in reversed(range(STEPS)):
        n1, r1, normed_all, attended, n2, r2, normed_two, hidden, activated = kept[index]
        last = index == 0
        if last:
            grads = (later[2], later[3], normed_two)
        else:
            down_grad = grad.astype(bf16)
            grads = ()
        hidden_grad, hidden_sum, middle_grad, branch_grad, sent, sums_two, *ups = block_backward(
            core, grad, hidden, w_down, w_up, w_out, n2, r2, ln2_gain, members, grads
        )
        own_grad = lax.all_to_all(sent, low, 0, 0, tiled=True).reshape(members * rows, W)
        if last:
            z_other, x_other, z_own, x_own = ups
            z_core = swap(z_other, "core")
            left, right = (later[0], pin(down_grad, sent)), (later[1], activated)
            d_other, d_own = grad_rows(core, left, right, bands, 0, 1)
            d_core = swap(d_other, "core")
            x_other, x_own = grad_out(
                core, (later[4], pin(branch_grad, d_other)), (later[5], attended), bands, x_other, x_own
            )
            x_core = swap(x_other, "core")
            samp = ("samp",) * two
            z_terms = pin((z_own, z_core), x_other)
            z_share = Share([split_rows(t, two) for t in z_terms], names + samp)
            d_terms = pin((d_own, d_core), z_share.halve("zl"))
            down_share = Share([split_rows(t, two) for t in d_terms], names + samp)
            x_terms = pin((x_own, x_core), down_share.halve("samp"))
            x_share = Share([split_rows(t, two) for t in x_terms], names + samp)
            own_grad = pin(own_grad, x_share.halve(x_axes[0]))
            heads = W // HD
            d_heads = attend_back(*owns[0], own_grad, members, range((heads + 1) // 2))
            own_grad, d_heads, z_share.terms[-1] = pin((own_grad, d_heads, z_share.terms[-1]))
            sent = z_share.halve("zh")
            if heads > 1:
                own_grad, d_heads = pin((own_grad, d_heads), sent)
                d_heads = attend_back(*owns[0], own_grad, members, range(heads // 2, heads), d_heads)
            shares = (z_share, x_share, down_share)
            waits = pin((d_heads, *(t.terms[-1] for t in shares)))
            d_heads = waits[0]
            for t, value in zip(shares, waits[1:]):
                t.terms[-1] = value
            sent = [x_share.halve("samp"), z_share.halve("samp")] + [down_share.halve("zh")]
            d_heads = pin(d_heads, *sent)
        else:
            own_grad, send_row, keep_rows = pin((own_grad, send_row, keep_rows), result)
            later = (down_grad, activated, hidden_grad, normed_two, branch_grad, attended)
            owns[index] = own_part(index)
            d_heads = attend_back(*owns[index], own_grad, members)
        back = lax.all_to_all(d_heads, low, 0, 0, tiled=True)
        w_heads = grad_heads(d_heads, normed_all, w_heads, bf16 if last else f32)
        if last:
            units = w_heads.reshape(-1, unit, D)
            if two:
                there = lax.dynamic_slice_in_dim(units, (1 - y) * (D // 2), D // 2, 2)
                here = lax.dynamic_slice_in_dim(units, y * (D // 2), D // 2, 2)
                units = [here, swap(there, "samp")]
            else:
                there, units = units, [units]
            back = pin(back, there)
            x_share.terms[-1], z_share.terms[-1] = pin((x_share.terms[-1], z_share.terms[-1]), back)
            sent = [x_share.halve(a) for a in x_axes[1:] + ("zl",)] + [z_share.halve(a) for a in x_axes]
            units[-1] = pin(units[-1], *sent)
            outgoing = take(units, send_row)
            incoming = lax.all_to_all(outgoing, low, 0, 0, tiled=True)
            down_share.terms[-1] = pin(down_share.terms[-1], outgoing)
            back = pin(back, *[down_share.halve(a) for a in x_axes])
        else:
            owns[0] = own_part(0)
            back = pin(back, w_heads, *owns[0])
        grad, low_grad, sums_one, sums_qv = qkv_backward(
            back, w_qkv, middle_grad, n1, r1, ln1_gain, half if last else rows
        )
        down_grad = low_grad
        step_small = (sums_one[:3], sums_qv[:2], sums_two[:4], hidden_sum)
        small = step_small if small is None else tuple(a + b for a, b in zip(small, step_small))
    fields_sent = low_grad
    fields_other = swap(fields_sent, "zh")
    x_share.terms[-1] = pin(x_share.terms[-1], fields_sent)
    incoming = pin(incoming, x_share.halve("zh"))
    there = take([incoming], keep_rows[1])
    other = swap(there, "zh")
    one, qv, two_sums, up_sum = pin(small, there)
    samples = 2 * samp_count
    slot = 2 * y + zh
    mine = lax.broadcasted_iota(jnp.int32, (samples, 1), 0) == slot
    leads = jnp.where(mine, one[2:3], 0.0)
    lane = lax.broadcasted_iota(jnp.int32, (bands, D // bands), 1) == slot
    bucket = jnp.where(lane & (me == 0), pick(lead_bucket, zh).astype(f32), 0.0)
    vectors = jnp.concatenate([one[:2], qv, two_sums, leads])
    vectors = vectors.reshape(-1, bands, D // bands).transpose(1, 0, 2).reshape(bands, -1)
    vectors = jnp.concatenate([vectors, up_sum.reshape(bands, -1), bucket], axis=1)
    sums = vectors
    vectors = lax.all_to_all(vectors, band, 0, 0, tiled=True)

    def both(x):
        x = x.astype(bf16)
        if not two:
            return lax.psum(x, "samp").astype(f32)
        other = swap(x, "samp")
        return jnp.concatenate([jnp.where(y == 0, x, other), jnp.where(y == 0, other, x)]).astype(f32)

    def both_cut(x, n):
        if not two:
            x = both(x)
            return x[:n], x[n:]
        x = x.astype(bf16)
        other = swap(x, "samp")
        first, second = jnp.where(y == 0, x, other), jnp.where(y == 0, other, x)
        x = jnp.concatenate([first, second]).astype(f32)
        return x[:n], x[n:]

    incoming, down_share.terms[-1], z_share.terms[-1] = pin((incoming, down_share.terms[-1], z_share.terms[-1]), sums)
    sent = down_share.halve("zl")
    own = take([incoming], keep_rows[0])
    up_first = total(z_share.terms).astype(bf16)
    late = (vectors, fields_other, other, down_share.terms[-1], x_share.terms[-1])
    late = pin(late, sent, own, up_first)
    vectors, fields_other, other, down_share.terms[-1], x_share.terms[-1] = late
    vectors = jnp.sum(vectors, axis=0)
    vectors = vectors + swap(vectors, "samp") if two else lax.psum(vectors, "samp")
    own = total([own, other]).astype(bf16).reshape(3 * D // bands, -1)
    if two:
        other = swap(own, "samp")
        own = jnp.concatenate([jnp.where(y == 0, own, other), jnp.where(y == 0, other, own)], axis=1)
    else:
        own = lax.psum(own, "samp")
    w_qkv_grad = own.astype(f32).T

    w_down_grad = both(total(down_share.terms)).T
    n_up = w_up.shape[1] // bands
    bottom = both_cut(total(x_share.terms), n_up // 2)
    w_out_grad = bottom[1].T
    w_up_grad = jnp.concatenate([both(up_first), bottom[0]]).T
    fields_grad = join(zh, grad, fields_other)

    w = D // bands
    leads = vectors[8 * w : (8 + samples) * w].reshape(samples, w)
    up_grad = vectors[(8 + samples) * w : -w]
    buckets = vectors[-w:][:samples].astype(jnp.int32)
    one_hot = (buckets[:, None] == jnp.arange(lead_table.shape[0], dtype=jnp.int32)[None, :]).astype(f32)
    lead_grad = jnp.dot(one_hot.T, leads, precision=lax.Precision.HIGHEST)
    rows_of = lambda i: vectors[i * w : (i + 1) * w]
    g = [rows_of(i) for i in (0, 1, 2, 3, 6, 4, 5)] + [up_grad, rows_of(7)]
    return (
        result,
        fields_grad,
        lead_grad,
        g[0],
        g[1],
        w_qkv_grad,
        g[2],
        g[3],
        w_out_grad,
        g[4],
        g[5],
        g[6],
        w_up_grad,
        g[7],
        w_down_grad,
        g[8],
    )


def solution(mesh):
    samp_count, band_count = mesh.shape["samp"], mesh.shape["band"]
    x_axes = tuple(f"x{i}" for i in range((band_count // 8).bit_length() - 1))
    axes = ("zh", "zl") + x_axes + ("core",)
    assert 2 ** len(axes) == band_count
    fine = Mesh(mesh.devices.reshape((samp_count,) + (2,) * len(axes)), ("samp",) + axes)
    tokens = P("samp", axes, None)
    columns, vector = P(None, axes), P(axes)
    in_specs = (tokens, P("samp"), tokens) + (P(),) * 14
    out_specs = (
        tokens,
        tokens,
        columns,
        vector,
        vector,
        columns,
        vector,
        vector,
        columns,
        vector,
        vector,
        vector,
        columns,
        vector,
        columns,
        vector,
    )
    run = functools.partial(body, axes=axes, x_axes=x_axes, samp_count=samp_count)
    return jax.shard_map(run, mesh=fine, in_specs=in_specs, out_specs=out_specs, check_vma=False)
```

```python
import functools
import math

import jax
import jax.numpy as jnp
import numpy as np
from jax import lax
from jax.experimental import pallas as pl
from jax.experimental.pallas import tpu as pltpu
from jax.sharding import Mesh
from jax.sharding import PartitionSpec as P

HD = 64
STEPS = 2
EPS = 1e-05
EXP_SCALE = 0.125 * 1.4426950408889634
GELU_A = 0.7978845608028654
GELU_B = 0.044715
MIB = 2**20
SWAP = [(0, 1), (1, 0)]
f32 = jnp.float32
bf16 = jnp.bfloat16


def cost(us):
    return pl.CostEstimate(flops=int(us * 1.15e9), bytes_accessed=1000, transcendentals=0)


def contract(a, b, a_dim, b_dim):
    return lax.dot_general(a, b, (((a_dim,), (b_dim,)), ((), ())), preferred_element_type=f32)


def head_part(x, h, heads):
    if heads == 1:
        return x
    lane = lax.broadcasted_iota(jnp.int32, x.shape, 1)
    return jnp.where(lane // HD == h, x, jnp.zeros_like(x))


def attend_kernel(q_ref, n_ref, wk_ref, wv_ref, b_ref, o_ref):
    normed = n_ref[...]
    keys = contract(normed, wk_ref[...], 1, 0).astype(bf16)
    values = (contract(normed, wv_ref[...], 1, 0) + b_ref[...]).astype(bf16)
    pair = 2 * HD
    for start in range(0, q_ref.shape[1], pair):
        q, k, v = q_ref[:, start : start + pair], keys[:, start : start + pair], values[:, start : start + pair]
        out = None
        for h in range(2):
            s = contract(head_part(q, h, 2), k, 1, 1)
            top = jnp.max(s, axis=-1, keepdims=True)
            e = jnp.exp2((s - top) * EXP_SCALE)
            total = jnp.sum(e, axis=-1, keepdims=True)
            o = head_part(contract(e.astype(bf16), v, 1, 0) / total, h, 2)
            out = o if out is None else out + o
        o_ref[:, start : start + pair] = out.astype(bf16)


def attend(q, normed_all, w_qkv, v_bias):
    rows, width = q.shape
    count = normed_all.shape[0]
    block = 4 * HD
    own = spec((rows, block), lambda j: (0, j))
    shift = width // block
    return pl.pallas_call(
        attend_kernel,
        grid=(width // block,),
        in_specs=[
            own,
            spec((count, width), lambda j: (0, 0)),
            spec((width, block), lambda j: (0, shift + j)),
            spec((width, block), lambda j: (0, 2 * shift + j)),
            spec((1, block), lambda j: (0, j)),
        ],
        out_specs=own,
        out_shape=jax.ShapeDtypeStruct((rows, width), bf16),
        compiler_params=pltpu.CompilerParams(vmem_limit_bytes=40 * MIB),
        cost_estimate=cost(24),
        name="attend",
    )(q, normed_all, w_qkv, w_qkv, v_bias.reshape(1, width))


def attend_back_kernel(q_ref, k_ref, v_ref, do_ref, *rest, heads, some):
    out_ref, dk_sum, dv_sum = rest[-3:]
    step = pl.program_id(0)
    rows = q_ref.shape[0]

    @pl.when(step == 0)
    def _():
        dk_sum[...] = jnp.zeros_like(dk_sum)
        dv_sum[...] = jnp.zeros_like(dv_sum)

    q, k, v, do = q_ref[...], k_ref[...], v_ref[...], do_ref[...]
    queries = [head_part(q, h, heads) for h in some]
    grads = [head_part(do, h, heads) for h in some]
    scores = [contract(x, k, 1, 1) for x in queries]
    prob_grads = [contract(x, v, 1, 1) for x in grads]
    dq = dk = dv = 0.0
    for h, qh, doh, s, dp in zip(some, queries, grads, scores, prob_grads):
        top = jnp.max(s, axis=-1, keepdims=True)
        e = jnp.exp2((s - top) * EXP_SCALE)
        inverse = 1.0 / jnp.sum(e, axis=-1, keepdims=True)
        inner = jnp.sum(e * dp, axis=-1, keepdims=True) * inverse
        p = e * inverse
        ds = (p * (dp - inner)).astype(bf16)
        dq = dq + head_part(contract(ds, k, 1, 0), h, heads)
        dk = dk + contract(ds, qh, 0, 0)
        dv = dv + contract(p.astype(bf16), doh, 0, 0)
    dk_sum[...] += dk
    dv_sum[...] += dv

    def put(m, i, x):
        if len(rest) == 4:
            x = x + rest[0][m, i].astype(f32)
        out_ref[m, i] = x.astype(bf16)

    put(step, 0, dq * 0.125)

    @pl.when(step == pl.num_programs(0) - 1)
    def _():
        for m in range(out_ref.shape[0]):
            put(m, 1, dk_sum[m * rows : (m + 1) * rows, :] * 0.125)
            put(m, 2, dv_sum[m * rows : (m + 1) * rows, :])


def attend_back(q, k, v, do, members, some=None, add=None):
    count, width = q.shape
    rows = count // members
    heads = width // HD
    part = pl.BlockSpec((rows, width), lambda i: (i, 0))
    full = pl.BlockSpec((count, width), lambda i: (0, 0))
    shape = (members, 3, rows, width)
    out = pl.BlockSpec(shape, lambda i: (0, 0, 0, 0))
    extra = [] if add is None else [add]
    return pl.pallas_call(
        functools.partial(attend_back_kernel, heads=heads, some=some or range(heads)),
        grid=(members,),
        in_specs=[part, full, full, part] + [out] * len(extra),
        out_specs=out,
        out_shape=jax.ShapeDtypeStruct(shape, bf16),
        scratch_shapes=[pltpu.VMEM((count, width), f32), pltpu.VMEM((count, width), f32)],
        compiler_params=pltpu.CompilerParams(vmem_limit_bytes=60 * MIB),
        cost_estimate=cost(33 if some is None else 17),
        name="attend_back",
    )(q, k, v, do, *extra)


def spec(block, index):
    return pl.BlockSpec(block, index)


def grad_rows_kernel(c_ref, l1, l0, r1, r0, other_ref, own_ref, sums):
    sums[...] = contract(l1[...], r1[...], 0, 0) + contract(l0[...], r0[...], 0, 0)
    count, n, _ = own_ref.shape
    for j in range(count):
        for ref, core in ((other_ref, 1 - c_ref[0]), (own_ref, c_ref[0])):
            ref[j] = sums[pl.ds(pl.multiple_of((2 * j + core) * n, n), n), :].astype(bf16)


def grad_rows(core, left, right, bands, part, parts):
    tokens, m = left[0].shape
    n = right[0].shape[1] // parts
    block = min(n, 512)
    first = part * (n // block)
    out = spec((bands // 2, m // bands, block), lambda j, c: (0, 0, j))
    whole = spec((tokens, m), lambda j, c: (0, 0))
    part = spec((tokens, block), lambda j, c: (0, first + j))
    return pl.pallas_call(
        grad_rows_kernel,
        grid_spec=pltpu.PrefetchScalarGridSpec(
            num_scalar_prefetch=1,
            grid=(n // block,),
            in_specs=[whole, whole, part, part],
            out_specs=[out, out],
            scratch_shapes=[pltpu.VMEM((m, block), f32)],
        ),
        out_shape=[jax.ShapeDtypeStruct((bands // 2, m // bands, n), bf16)] * 2,
        compiler_params=pltpu.CompilerParams(vmem_limit_bytes=60 * MIB),
        cost_estimate=cost(8),
        name="grad_rows",
    )(core.reshape(1), *left, *right)


def block_forward_kernel(
    x_ref, a_ref, wo_ref, bo_ref, g_ref, b_ref, wu_ref, bu_ref, wd_ref, bd_ref, lead_ref, g1_ref, b1_ref,
    n2_ref, r2_ref, low2_ref, hidden_ref, act_ref, *rest, last
):
    total = rest[-1]
    step = pl.program_id(0)

    @pl.when(step == 0)
    def _():
        middle = x_ref[...] + contract(a_ref[...], wo_ref[...], 1, 0) + bo_ref[...]
        n, r = norm_parts(middle)
        n2_ref[...] = n
        r2_ref[...] = r
        low2_ref[...] = (n * g_ref[...] + b_ref[...]).astype(bf16)
        total[...] = middle + bd_ref[...]

    hidden = contract(low2_ref[...], wu_ref[...], 1, 0) + bu_ref[...]
    hidden_ref[...] = hidden
    act = gelu(hidden).astype(bf16)
    act_ref[...] = act
    total[...] += contract(act, wd_ref[...], 1, 0)

    @pl.when(step == pl.num_programs(0) - 1)
    def _():
        carried = total[...]
        if last:
            rest[0][...] = carried.astype(bf16)
        else:
            x = carried + lead_ref[...]
            n, r = norm_parts(x)
            rest[0][...] = x
            rest[1][...] = n
            rest[2][...] = r
            rest[3][...] = (n * g1_ref[...] + b1_ref[...]).astype(bf16)


def block_forward(inputs, attended, weights, last):
    w_out, out_bias, ln2_gain, ln2_bias, w_up, up_bias, w_down, down_bias, lead, ln1_gain, ln1_bias = weights
    t, d = inputs.shape
    f = w_up.shape[1]
    block = 512
    row = lambda v: v.reshape(1, -1)
    full = spec((t, d), lambda i: (0, 0))
    vec = spec((1, d), lambda i: (0, 0))
    one = spec((t, 1), lambda i: (0, 0))
    wide = spec((t, block), lambda i: (0, i))
    shape = jax.ShapeDtypeStruct
    outs = [full, one, full, wide, wide] + ([full] if last else [full, full, one, full])
    shapes = [shape((t, d), f32), shape((t, 1), f32), shape((t, d), bf16), shape((t, f), f32), shape((t, f), bf16)]
    shapes += [shape((t, d), bf16)] if last else [
        shape((t, d), f32), shape((t, d), f32), shape((t, 1), f32), shape((t, d), bf16)
    ]
    return pl.pallas_call(
        functools.partial(block_forward_kernel, last=last),
        grid=(f // block,),
        in_specs=[
            full, full, spec((d, d), lambda i: (0, 0)), vec, vec, vec,
            spec((d, block), lambda i: (0, i)), spec((1, block), lambda i: (0, i)),
            spec((block, d), lambda i: (i, 0)), vec, vec, vec, vec,
        ],
        out_specs=outs,
        out_shape=shapes,
        scratch_shapes=[pltpu.VMEM((t, d), f32)],
        compiler_params=pltpu.CompilerParams(vmem_limit_bytes=40 * MIB),
        cost_estimate=cost(12),
        name="block_forward",
    )(
        inputs, attended, w_out, row(out_bias), row(ln2_gain), row(ln2_bias), w_up, row(up_bias), w_down,
        row(down_bias), row(lead), row(ln1_gain), row(ln1_bias),
    )


def put_sums(ref, *sums):
    for i, v in enumerate(sums):
        ref[i : i + 1, :] = v


def column_sum(x):
    return jnp.sum(x.astype(f32), axis=0, keepdims=True)


def block_backward_kernel(c_ref, grad_ref, h_ref, wd_ref, wu_ref, wo_ref, n_ref, r_ref, g_ref, *rest, grads, bands):
    if grads:
        l1_ref, x1_ref, x0_ref = rest[:3]
        z_other, x_other, z_own, x_own = rest[9:13]
        sums, rest = rest[14], rest[3:9] + rest[13:14]
    hg_ref, hsum_ref, middle_ref, branch_ref, sent_ref, sums_ref, total = rest
    step = pl.program_id(0)
    down = grad_ref[...].astype(bf16)
    low = (gelu_slope(h_ref[...]) * contract(down, wd_ref[...], 1, 1)).astype(bf16)
    hg_ref[...] = low
    hsum_ref[...] = column_sum(low)
    part = contract(low, wu_ref[...], 1, 1)
    if grads:
        sums[...] = contract(l1_ref[...], x1_ref[...], 0, 0) + contract(low, x0_ref[...], 0, 0)
        pairs = z_own.shape[0]
        n = sums.shape[0] // (2 * pairs)
        for q in range(pairs):
            for z, x, core in ((z_other, x_other, 1 - c_ref[0]), (z_own, x_own, c_ref[0])):
                start = pl.multiple_of((2 * q + core) * n, n)
                z[q] = sums[pl.ds(start, n // 2), :].astype(bf16)
                x[q] = sums[pl.ds(start + n // 2, n // 2), :].astype(bf16)

    @pl.when(step == 0)
    def _():
        total[...] = part

    @pl.when(step > 0)
    def _():
        total[...] += part

    @pl.when(step == pl.num_programs(0) - 1)
    def _():
        dv, gain, bias = norm_back(total[...], n_ref[...], r_ref[...], g_ref[...])
        middle = grad_ref[...] + dv
        middle_ref[...] = middle
        branch = middle.astype(bf16)
        branch_ref[...] = branch
        put_sums(sums_ref, gain, bias, column_sum(branch), column_sum(down))
        w = sent_ref.shape[2]
        attended = contract(branch, wo_ref[...], 1, 1).astype(bf16)
        for m in range(sent_ref.shape[0]):
            sent_ref[m] = attended[:, m * w : (m + 1) * w]


def block_backward(core, grad, hidden, w_down, w_up, w_out, n2, r2, gain, members, grads=()):
    t, d = grad.shape
    f = hidden.shape[1]
    block = 512
    bands = 2 * members
    full = spec((t, d), lambda i, c: (0, 0))
    wide = spec((t, block), lambda i, c: (0, i))
    sent = (members, t, d // members)
    shape = jax.ShapeDtypeStruct
    outs = [
        wide, spec((1, block), lambda i, c: (0, i)), full, full,
        spec(sent, lambda i, c: (0, 0, 0)), spec((8, d), lambda i, c: (0, 0)),
    ]
    shapes = [
        shape((t, f), bf16), shape((1, f), f32), shape((t, d), f32), shape((t, d), bf16),
        shape(sent, bf16), shape((8, d), f32),
    ]
    scratch = [pltpu.VMEM((t, d), f32)]
    if grads:
        n = f // bands
        pairs = block // (2 * n)
        part = spec((pairs, n // 2, d), lambda i, c: (i, 0, 0))
        outs += [part] * 4
        shapes += [shape((bands // 2, n // 2, d), bf16), shape((bands // 2, n // 2 + d // bands, d), bf16)] * 2
        scratch += [pltpu.VMEM((block, d), f32)]
    return pl.pallas_call(
        functools.partial(block_backward_kernel, grads=bool(grads), bands=bands),
        grid_spec=pltpu.PrefetchScalarGridSpec(
            num_scalar_prefetch=1,
            grid=(f // block,),
            in_specs=[
                full, wide, spec((block, d), lambda i, c: (i, 0)), spec((d, block), lambda i, c: (0, i)),
                spec((d, d), lambda i, c: (0, 0)), full, spec((t, 1), lambda i, c: (0, 0)),
                spec((1, d), lambda i, c: (0, 0)),
            ] + [wide, full, full][: len(grads)],
            out_specs=outs,
            scratch_shapes=scratch,
        ),
        out_shape=shapes,
        compiler_params=pltpu.CompilerParams(vmem_limit_bytes=(60 if grads else 48) * MIB),
        cost_estimate=cost(18 if grads else 14),
        name="block_backward",
    )(core.reshape(1), grad, hidden, w_down, w_up, w_out, n2, r2, gain.reshape(1, d), *grads)


def grad_out_kernel(c_ref, l1, l0, r1, r0, _, __, other_ref, own_ref, sums, *, pairs):
    sums[...] = contract(l1[...], r1[...], 0, 0) + contract(l0[...], r0[...], 0, 0)
    n = own_ref.shape[1]
    for q in range(pairs):
        for ref, core in ((other_ref, 1 - c_ref[0]), (own_ref, c_ref[0])):
            ref[q] = sums[pl.ds(pl.multiple_of((2 * q + core) * n, n), n), :].astype(bf16)


def grad_out(core, left, right, bands, other, own):
    tokens, m = left[0].shape
    count, height, d = own.shape
    n = m // bands
    pairs = max(1, 256 // (2 * n))
    columns = spec((tokens, 2 * n * pairs), lambda j, c: (0, j))
    whole = spec((tokens, d), lambda j, c: (0, 0))
    out = spec((pairs, n, d), lambda j, c: (j, height // n - 1, 0))
    anywhere = pl.BlockSpec(memory_space=pl.ANY)
    return pl.pallas_call(
        functools.partial(grad_out_kernel, pairs=pairs),
        grid_spec=pltpu.PrefetchScalarGridSpec(
            num_scalar_prefetch=1,
            grid=(count // pairs,),
            in_specs=[columns, columns, whole, whole, anywhere, anywhere],
            out_specs=[out, out],
            scratch_shapes=[pltpu.VMEM((2 * n * pairs, d), f32)],
        ),
        out_shape=[jax.ShapeDtypeStruct(own.shape, bf16)] * 2,
        input_output_aliases={5: 0, 6: 1},
        compiler_params=pltpu.CompilerParams(vmem_limit_bytes=60 * MIB),
        cost_estimate=cost(3),
        name="grad_out",
    )(core.reshape(1), *left, *right, other, own)


def qkv_backward_kernel(b_ref, wq_ref, wk_ref, wv_ref, m_ref, n_ref, r_ref, g_ref, grad_ref, low_ref, sums_ref, qv_ref, total):
    step = pl.program_id(0)
    w = b_ref.shape[3]
    part = None
    for m in range(b_ref.shape[0]):
        for i, ref in enumerate((wq_ref, wk_ref, wv_ref)):
            x = contract(b_ref[m, i], ref[:, m * w : (m + 1) * w], 1, 1)
            part = x if part is None else part + x
        qv_ref[0:1, m * w : (m + 1) * w] = column_sum(b_ref[m, 0])
        qv_ref[1:2, m * w : (m + 1) * w] = column_sum(b_ref[m, 2])

    @pl.when(step == 0)
    def _():
        total[...] = part

    @pl.when(step > 0)
    def _():
        total[...] += part

    @pl.when(step == pl.num_programs(0) - 1)
    def _():
        dv, gain, bias = norm_back(total[...], n_ref[...], r_ref[...], g_ref[...])
        grad = m_ref[...] + dv
        grad_ref[...] = grad
        low_ref[...] = grad[grad.shape[0] - low_ref.shape[0] :].astype(bf16)
        put_sums(sums_ref, gain, bias, column_sum(grad))


def qkv_backward(back, w_qkv, middle_grad, n1, r1, gain, low):
    members, _, t, w = back.shape
    d = members * w
    at_once = max(2, 128 // w)
    block = at_once * w
    shift = d // block
    full = spec((t, d), lambda i: (0, 0))
    weight = [spec((d, block), lambda i, s=s: (0, s * shift + i)) for s in range(3)]
    shape = jax.ShapeDtypeStruct
    return pl.pallas_call(
        qkv_backward_kernel,
        grid=(members // at_once,),
        in_specs=[spec((at_once, 3, t, w), lambda i: (i, 0, 0, 0))] + weight + [
            full, full, spec((t, 1), lambda i: (0, 0)), spec((1, d), lambda i: (0, 0)),
        ],
        out_specs=[
            full, spec((low, d), lambda i: (0, 0)), spec((8, d), lambda i: (0, 0)),
            spec((8, block), lambda i: (0, i)),
        ],
        out_shape=[
            shape((t, d), f32), shape((low, d), bf16), shape((8, d), f32), shape((8, d), f32),
        ],
        scratch_shapes=[pltpu.VMEM((t, d), f32)],
        compiler_params=pltpu.CompilerParams(vmem_limit_bytes=60 * MIB),
        cost_estimate=cost(12),
        name="qkv_backward",
    )(back, w_qkv, w_qkv, w_qkv, middle_grad, n1, r1, gain.reshape(1, d))


def grad_heads_kernel(d_ref, n_ref, *rest):
    out_ref = rest[-1]
    rows = d_ref.shape[2]
    for i in range(3):
        total = rest[0][i] if len(rest) == 2 else jnp.zeros(out_ref.shape[1:], f32)
        for m in range(d_ref.shape[0]):
            total += contract(d_ref[m, i], n_ref[m * rows : (m + 1) * rows, :], 0, 0)
        out_ref[i] = total.astype(out_ref.dtype)


def grad_heads(d, normed_all, add, kind):
    members, _, rows, width = d.shape
    dim = normed_all.shape[1]
    shape = (3, width, dim)
    out = spec((3, width, dim // 4), lambda i: (0, 0, i))
    extra = [] if add is None else [add]
    return pl.pallas_call(
        grad_heads_kernel,
        grid=(4,),
        in_specs=[
            spec(d.shape, lambda i: (0, 0, 0, 0)),
            spec((members * rows, dim // 4), lambda i: (0, i)),
        ]
        + [out] * len(extra),
        out_specs=out,
        out_shape=jax.ShapeDtypeStruct(shape, kind),
        compiler_params=pltpu.CompilerParams(vmem_limit_bytes=60 * MIB),
        cost_estimate=cost(5),
        name="grad_heads",
    )(d, normed_all, *extra)


def take_kernel(table, *refs):
    for i in range(refs[-1].shape[0]):
        total = refs[0][table[i]].astype(f32)
        for r in refs[1:-1]:
            total = total + r[table[i]].astype(f32)
        refs[-1][i] = total.astype(bf16)


def take(terms, table):
    shape = terms[0].shape
    count = table.shape[0]
    return pl.pallas_call(
        take_kernel,
        grid_spec=pltpu.PrefetchScalarGridSpec(
            num_scalar_prefetch=1,
            grid=(1,),
            in_specs=[spec(shape, lambda i, t: (0, 0, 0))] * len(terms),
            out_specs=spec((count,) + shape[1:], lambda i, t: (0, 0, 0)),
        ),
        out_shape=jax.ShapeDtypeStruct((count,) + shape[1:], bf16),
        compiler_params=pltpu.CompilerParams(vmem_limit_bytes=60 * MIB),
        cost_estimate=cost(3),
        name="take",
    )(table, *terms)


def join_kernel(i_ref, own_ref, other_ref, out_ref):
    half = other_ref.shape[0]
    out_ref[i_ref[0]] = own_ref[:half]
    out_ref[1 - i_ref[0]] = other_ref[...].astype(f32)


def join(index, own, other):
    half, d = other.shape
    full = spec((half, d), lambda i, c: (0, 0))
    return pl.pallas_call(
        join_kernel,
        grid_spec=pltpu.PrefetchScalarGridSpec(
            num_scalar_prefetch=1,
            grid=(1,),
            in_specs=[full, full],
            out_specs=spec((2, half, d), lambda i, c: (0, 0, 0)),
        ),
        out_shape=jax.ShapeDtypeStruct((2, half, d), f32),
        compiler_params=pltpu.CompilerParams(vmem_limit_bytes=8 * MIB),
        cost_estimate=cost(2),
        name="join",
    )(index.reshape(1), own, other)


def unit_tables(bands, x_count, width, dim):
    members = bands // 2
    unit = math.gcd(HD, 3 * dim // bands)
    per_band = 3 * dim // bands // unit
    made, slots, place = [], [], {}
    for g in range(members):
        units = [(b * dim + g * width) // unit + i for b in range(3) for i in range(width // unit)]
        by_low = [[] for _ in range(members)]
        for local, u in enumerate(units):
            band = u // per_band
            core, x, zl = band % 2, band // 2 % x_count, band // (2 * x_count) % 2
            low = (core * 2 + zl) * x_count + x
            place[u] = (g, len(by_low[low]))
            by_low[low].append(local)
        made.append(by_low)
    most = max(len(l) for by_low in made for l in by_low)
    send = np.zeros((members, members * most), np.int32)
    for g, by_low in enumerate(made):
        for low, locals_ in enumerate(by_low):
            for m, local in enumerate(locals_):
                send[g, low * most + m] = local
    keep = np.zeros((members, 2, per_band), np.int32)
    for u, (g, m) in place.items():
        band = u // per_band
        core, x, zl = band % 2, band // 2 % x_count, band // (2 * x_count) % 2
        low = (core * 2 + zl) * x_count + x
        keep[low, band // members, u % per_band] = g * most + m
    return unit, send, keep


def norm_parts(v):
    centred = v - jnp.mean(v, axis=-1, keepdims=True)
    r = lax.rsqrt(jnp.mean(centred * centred, axis=-1, keepdims=True) + EPS)
    return centred * r, r


def norm_back(dy, n, r, gain):
    dyg = dy * gain
    mean_one = jnp.mean(dyg, axis=-1, keepdims=True)
    mean_two = jnp.mean(dyg * n, axis=-1, keepdims=True)
    dv = r * (dyg - mean_one - n * mean_two)
    return dv, jnp.sum(dy * n, axis=0, keepdims=True), jnp.sum(dy, axis=0, keepdims=True)


def gelu(x):
    return 0.5 * x * (1.0 + jnp.tanh(GELU_A * (x + GELU_B * x * x * x)))


def gelu_slope(x):
    t = jnp.tanh(GELU_A * (x + GELU_B * x * x * x))
    return 0.5 * (1.0 + t) + 0.5 * x * (1.0 - t * t) * (GELU_A * (1.0 + 3.0 * GELU_B * x * x))


def dot(a, b):
    return jnp.dot(a, b, preferred_element_type=f32)


def dot_t(a, b):
    return contract(a, b, 1, 1)


def swap(x, axis):
    return lax.ppermute(x, axis, SWAP)


def pin(x, *first):
    return lax.optimization_barrier((x,) + first)[0]


def total(terms):
    out = terms[0].astype(f32)
    for t in terms[1:]:
        out = out + t.astype(f32)
    return out


class Share:
    def __init__(self, terms, names):
        self.terms = list(terms)
        self.names = list(names)

    def halve(self, axis, *first):
        if axis not in self.names:
            return self.terms[-1]
        dim = self.names.index(axis)
        i = lax.axis_index(axis)
        terms = [pin(t, *first) if first else t for t in self.terms[-1:]] + self.terms[:-1]
        there = [lax.dynamic_index_in_dim(t, 1 - i, dim, keepdims=False) for t in terms]
        self.terms = [lax.dynamic_index_in_dim(t, i, dim, keepdims=False) for t in terms]
        self.names.remove(axis)
        sent = total(there).astype(bf16)
        self.terms.append(swap(sent, axis))
        return sent


def body(
    fields,
    lead_bucket,
    cotangent,
    lead_table,
    ln1_gain,
    ln1_bias,
    w_qkv,
    q_bias,
    v_bias,
    w_out,
    out_bias,
    ln2_gain,
    ln2_bias,
    w_up,
    up_bias,
    w_down,
    down_bias,
    *,
    axes,
    x_axes,
    samp_count,
):
    band = tuple(axes)
    low = ("core", "zl") + x_axes[::-1]
    members = 2 ** len(low)
    order = x_axes + ("zl", "core")
    D = w_out.shape[0]
    W = D // members
    half = fields.shape[1]
    rows = 2 * half
    two = samp_count == 2
    zh = lax.axis_index("zh")
    me = lax.axis_index(low)

    def pick(x, i):
        return lax.dynamic_index_in_dim(x, i, 0, keepdims=False)

    def to_sample(x):
        return jnp.concatenate([pick(x, zh), swap(pick(x, 1 - zh), "zh")])

    def by_band(own, other):
        return jnp.where(zh == 0, jnp.stack([own, other]), jnp.stack([other, own]))

    def gather(x):
        if len(x_axes) == 1:
            x_axis = x_axes[0]
            cut = x.shape[0] // 2
            by_x = swap(x, x_axis)
            by_z = swap(x, "zl")
            far = [swap(by_x[:cut], "zl"), swap(by_z[cut:], x_axis)]
            pieces = [(x, 0, 0), (by_x, 1, 0), (by_z, 2, 0), (far[0], 3, 0), (far[1], 3, cut)]
            pieces += [(swap(p, "core"), 4 + k, o) for p, k, o in pieces]
        else:
            pieces = [(x, 0, 0)]
            for bit, axis in enumerate(order):
                pieces += [(swap(p, axis), k + 2**bit, 0) for p, k, _ in pieces]
        out = jnp.zeros((members * rows, D), bf16)
        for piece, k, offset in pieces:
            out = lax.dynamic_update_slice(out, piece, ((me ^ k) * rows + offset, 0))
        return out

    lead_row = pick(lead_table, pick(lead_bucket, zh)).astype(f32)
    carried = to_sample(fields).astype(f32)

    def member_columns(x, block):
        return lax.dynamic_slice_in_dim(x, block * D + me * W, W, x.ndim - 1)

    kept = []
    inputs = carried + lead_row
    n1, r1 = norm_parts(inputs)
    normed = (n1 * ln1_gain + ln1_bias).astype(bf16)
    weights = (w_out, out_bias, ln2_gain, ln2_bias, w_up, up_bias, w_down, down_bias, lead_row, ln1_gain, ln1_bias)
    for index in range(STEPS):
        normed_all = gather(normed)
        queries = (dot(normed, w_qkv[:, :D]) + q_bias).astype(bf16)
        if index == 0:
            out_grad = to_sample(pin(cotangent, normed_all))
        attended = attend(queries, normed_all, w_qkv, v_bias)
        if index == 0:
            attended, out_grad = pin((attended, out_grad))
        last = index == STEPS - 1
        n2, r2, normed_two, hidden, activated, *after = block_forward(inputs, attended, weights, last)
        kept.append((n1, r1, normed_all, attended, n2, r2, normed_two, hidden, activated))
        if not last:
            inputs, n1, r1, normed = after
    carried = after[0]

    grad = out_grad
    small = None
    core = lax.axis_index("core")
    y = lax.axis_index("samp")
    bands = 2 ** len(axes)
    names = axes[:-1]
    cube = (2,) * len(names)
    later = None
    w_heads = None
    unit, send_table, keep_table = unit_tables(bands, 2 ** len(x_axes), W, D)
    send_row, keep_row = pick(jnp.asarray(send_table), me), pick(jnp.asarray(keep_table), me)
    keep_rows = pick(keep_row, zh), pick(keep_row, 1 - zh)
    def split_rows(x, rows_two):
        n, r, c = x.shape
        return x.reshape(cube + ((2, r // 2) if rows_two else (r,)) + (c,))

    own_weight = jnp.concatenate([member_columns(w_qkv, i) for i in range(3)], axis=1)
    own_bias = jnp.concatenate([member_columns(q_bias, 0), jnp.zeros((W,), f32), member_columns(v_bias, 0)])

    def own_part(index):
        own = (dot(kept[index][2], own_weight) + own_bias).astype(bf16)
        return own[:, :W], own[:, W : 2 * W], own[:, 2 * W :]

    owns = {}
    for index in reversed(range(STEPS)):
        n1, r1, normed_all, attended, n2, r2, normed_two, hidden, activated = kept[index]
        last = index == 0
        if last:
            grads = (later[2], later[3], normed_two)
        else:
            down_grad = grad.astype(bf16)
            grads = ()
        hidden_grad, hidden_sum, middle_grad, branch_grad, sent, sums_two, *ups = block_backward(
            core, grad, hidden, w_down, w_up, w_out, n2, r2, ln2_gain, members, grads
        )
        own_grad = lax.all_to_all(sent, low, 0, 0, tiled=True).reshape(members * rows, W)
        if last:
            z_other, x_other, z_own, x_own = ups
            z_core = swap(z_other, "core")
            left, right = (later[0], pin(down_grad, sent)), (later[1], activated)
            d_other, d_own = grad_rows(core, left, right, bands, 0, 1)
            d_core = swap(d_other, "core")
            x_other, x_own = grad_out(
                core, (later[4], pin(branch_grad, d_other)), (later[5], attended), bands, x_other, x_own
            )
            x_core = swap(x_other, "core")
            samp = ("samp",) * two
            d_terms = pin((d_own, d_core), x_other)
            down_share = Share([split_rows(t, two) for t in d_terms], names + samp)
            z_terms = pin((z_own, z_core), down_share.halve("samp"))
            z_share = Share([split_rows(t, two) for t in z_terms], names + samp)
            x_terms = pin((x_own, x_core), z_share.halve("zl"))
            x_share = Share([split_rows(t, two) for t in x_terms], names + samp)
            own_grad = pin(own_grad, x_share.halve(x_axes[0]))
            heads = W // HD
            d_heads = attend_back(*owns[0], own_grad, members, range((heads + 1) // 2))
            own_grad, d_heads, z_share.terms[-1] = pin((own_grad, d_heads, z_share.terms[-1]))
            sent = z_share.halve("zh")
            if heads > 1:
                own_grad, d_heads = pin((own_grad, d_heads), sent)
                d_heads = attend_back(*owns[0], own_grad, members, range(heads // 2, heads), d_heads)
            shares = (z_share, x_share, down_share)
            waits = pin((d_heads, *(t.terms[-1] for t in shares)))
            d_heads = waits[0]
            for t, value in zip(shares, waits[1:]):
                t.terms[-1] = value
            sent = [x_share.halve("samp"), z_share.halve("samp")] + [down_share.halve("zh")]
            d_heads = pin(d_heads, *sent)
        else:
            result = swap(pin(carried[half:], sent), "zh")
            own_grad, send_row, keep_rows = pin((own_grad, send_row, keep_rows))
            later = (down_grad, activated, hidden_grad, normed_two, branch_grad, attended)
            owns[index] = own_part(index)
            d_heads, result = pin((attend_back(*owns[index], own_grad, members), result))
            result = by_band(carried[:half], result)
        back = lax.all_to_all(d_heads, low, 0, 0, tiled=True)
        w_heads = grad_heads(d_heads, normed_all, w_heads, bf16 if last else f32)
        if last:
            units = w_heads.reshape(-1, unit, D)
            if two:
                there = lax.dynamic_slice_in_dim(units, (1 - y) * (D // 2), D // 2, 2)
                here = lax.dynamic_slice_in_dim(units, y * (D // 2), D // 2, 2)
                units = [here, swap(there, "samp")]
            else:
                there, units = units, [units]
            back = pin(back, there)
            x_share.terms[-1], z_share.terms[-1] = pin((x_share.terms[-1], z_share.terms[-1]), back)
            sent = [x_share.halve(a) for a in x_axes[1:] + ("zl",)] + [z_share.halve(a) for a in x_axes]
            units[-1] = pin(units[-1], *sent)
            outgoing = take(units, send_row)
            incoming = lax.all_to_all(outgoing, low, 0, 0, tiled=True)
            down_share.terms[-1] = pin(down_share.terms[-1], outgoing)
            back = pin(back, *[down_share.halve(a) for a in x_axes])
        else:
            owns[0] = own_part(0)
            back = pin(back, w_heads, result, *owns[0])
        grad, low_grad, sums_one, sums_qv = qkv_backward(
            back, w_qkv, middle_grad, n1, r1, ln1_gain, half if last else rows
        )
        down_grad = low_grad
        step_small = (sums_one[:3], sums_qv[:2], sums_two[:4], hidden_sum)
        small = step_small if small is None else tuple(a + b for a, b in zip(small, step_small))
    fields_sent = low_grad
    fields_other = swap(fields_sent, "zh")
    x_share.terms[-1] = pin(x_share.terms[-1], fields_sent)
    incoming = pin(incoming, x_share.halve("zh"))
    there = take([incoming], keep_rows[1])
    other = swap(there, "zh")
    one, qv, two_sums, up_sum = pin(small, there)
    samples = 2 * samp_count
    slot = 2 * y + zh
    mine = lax.broadcasted_iota(jnp.int32, (samples, 1), 0) == slot
    leads = jnp.where(mine, one[2:3], 0.0)
    lane = lax.broadcasted_iota(jnp.int32, (bands, D // bands), 1) == slot
    bucket = jnp.where(lane & (me == 0), pick(lead_bucket, zh).astype(f32), 0.0)
    vectors = jnp.concatenate([one[:2], qv, two_sums, leads])
    vectors = vectors.reshape(-1, bands, D // bands).transpose(1, 0, 2).reshape(bands, -1)
    vectors = jnp.concatenate([vectors, up_sum.reshape(bands, -1), bucket], axis=1)
    sums = vectors
    vectors = lax.all_to_all(vectors, band, 0, 0, tiled=True)

    def both(x):
        x = x.astype(bf16)
        if not two:
            return lax.psum(x, "samp").astype(f32)
        other = swap(x, "samp")
        return jnp.concatenate([jnp.where(y == 0, x, other), jnp.where(y == 0, other, x)]).astype(f32)

    def both_cut(x, n):
        if not two:
            x = both(x)
            return x[:n], x[n:]
        x = x.astype(bf16)
        other = swap(x, "samp")
        first, second = jnp.where(y == 0, x, other), jnp.where(y == 0, other, x)
        x = jnp.concatenate([first, second]).astype(f32)
        return x[:n], x[n:]

    incoming, down_share.terms[-1], z_share.terms[-1] = pin((incoming, down_share.terms[-1], z_share.terms[-1]), sums)
    sent = down_share.halve("zl")
    own = take([incoming], keep_rows[0])
    up_first = total(z_share.terms).astype(bf16)
    late = (vectors, fields_other, other, down_share.terms[-1], x_share.terms[-1])
    late = pin(late, sent, own, up_first)
    vectors, fields_other, other, down_share.terms[-1], x_share.terms[-1] = late
    vectors = jnp.sum(vectors, axis=0)
    vectors = vectors + swap(vectors, "samp") if two else lax.psum(vectors, "samp")
    own = total([own, other]).astype(bf16).reshape(3 * D // bands, -1)
    if two:
        other = swap(own, "samp")
        own = jnp.concatenate([jnp.where(y == 0, own, other), jnp.where(y == 0, other, own)], axis=1)
    else:
        own = lax.psum(own, "samp")
    w_qkv_grad = own.astype(f32).T

    w_down_grad = both(total(down_share.terms)).T
    n_up = w_up.shape[1] // bands
    bottom = both_cut(total(x_share.terms), n_up // 2)
    w_out_grad = bottom[1].T
    w_up_grad = jnp.concatenate([both(up_first), bottom[0]]).T
    fields_grad = join(zh, grad, fields_other)

    w = D // bands
    leads = vectors[8 * w : (8 + samples) * w].reshape(samples, w)
    up_grad = vectors[(8 + samples) * w : -w]
    buckets = vectors[-w:][:samples].astype(jnp.int32)
    one_hot = (buckets[:, None] == jnp.arange(lead_table.shape[0], dtype=jnp.int32)[None, :]).astype(f32)
    lead_grad = jnp.dot(one_hot.T, leads, precision=lax.Precision.HIGHEST)
    rows_of = lambda i: vectors[i * w : (i + 1) * w]
    g = [rows_of(i) for i in (0, 1, 2, 3, 6, 4, 5)] + [up_grad, rows_of(7)]
    return (
        result,
        fields_grad,
        lead_grad,
        g[0],
        g[1],
        w_qkv_grad,
        g[2],
        g[3],
        w_out_grad,
        g[4],
        g[5],
        g[6],
        w_up_grad,
        g[7],
        w_down_grad,
        g[8],
    )


def solution(mesh):
    samp_count, band_count = mesh.shape["samp"], mesh.shape["band"]
    x_axes = tuple(f"x{i}" for i in range((band_count // 8).bit_length() - 1))
    axes = ("zh", "zl") + x_axes + ("core",)
    assert 2 ** len(axes) == band_count
    fine = Mesh(mesh.devices.reshape((samp_count,) + (2,) * len(axes)), ("samp",) + axes)
    tokens = P("samp", axes, None)
    columns, vector = P(None, axes), P(axes)
    in_specs = (tokens, P("samp"), tokens) + (P(),) * 14
    out_specs = (
        tokens,
        tokens,
        columns,
        vector,
        vector,
        columns,
        vector,
        vector,
        columns,
        vector,
        vector,
        vector,
        columns,
        vector,
        columns,
        vector,
    )
    run = functools.partial(body, axes=axes, x_axes=x_axes, samp_count=samp_count)
    return jax.shard_map(run, mesh=fine, in_specs=in_specs, out_specs=out_specs, check_vma=False)
```

```python
import functools
import math

import jax
import jax.numpy as jnp
import numpy as np
from jax import lax
from jax.experimental import pallas as pl
from jax.experimental.pallas import tpu as pltpu
from jax.sharding import Mesh
from jax.sharding import PartitionSpec as P

HD = 64
STEPS = 2
EPS = 1e-05
EXP_SCALE = 0.125 * 1.4426950408889634
GELU_A = 0.7978845608028654
GELU_B = 0.044715
MIB = 2**20
SWAP = [(0, 1), (1, 0)]
f32 = jnp.float32
bf16 = jnp.bfloat16


def cost(us):
    return pl.CostEstimate(flops=int(us * 1.15e9), bytes_accessed=1000, transcendentals=0)


def contract(a, b, a_dim, b_dim):
    return lax.dot_general(a, b, (((a_dim,), (b_dim,)), ((), ())), preferred_element_type=f32)


def head_part(x, h, heads):
    if heads == 1:
        return x
    lane = lax.broadcasted_iota(jnp.int32, x.shape, 1)
    return jnp.where(lane // HD == h, x, jnp.zeros_like(x))


def attend_kernel(q_ref, n_ref, wk_ref, wv_ref, b_ref, o_ref):
    normed = n_ref[...]
    keys = contract(normed, wk_ref[...], 1, 0).astype(bf16)
    values = (contract(normed, wv_ref[...], 1, 0) + b_ref[...]).astype(bf16)
    pair = 2 * HD
    for start in range(0, q_ref.shape[1], pair):
        q, k, v = q_ref[:, start : start + pair], keys[:, start : start + pair], values[:, start : start + pair]
        out = None
        for h in range(2):
            s = contract(head_part(q, h, 2), k, 1, 1)
            top = jnp.max(s, axis=-1, keepdims=True)
            e = jnp.exp2((s - top) * EXP_SCALE)
            total = jnp.sum(e, axis=-1, keepdims=True)
            o = head_part(contract(e.astype(bf16), v, 1, 0) / total, h, 2)
            out = o if out is None else out + o
        o_ref[:, start : start + pair] = out.astype(bf16)


def attend(q, normed_all, w_qkv, v_bias):
    rows, width = q.shape
    count = normed_all.shape[0]
    block = 4 * HD
    own = spec((rows, block), lambda j: (0, j))
    shift = width // block
    return pl.pallas_call(
        attend_kernel,
        grid=(width // block,),
        in_specs=[
            own,
            spec((count, width), lambda j: (0, 0)),
            spec((width, block), lambda j: (0, shift + j)),
            spec((width, block), lambda j: (0, 2 * shift + j)),
            spec((1, block), lambda j: (0, j)),
        ],
        out_specs=own,
        out_shape=jax.ShapeDtypeStruct((rows, width), bf16),
        compiler_params=pltpu.CompilerParams(vmem_limit_bytes=40 * MIB),
        cost_estimate=cost(24),
        name="attend",
    )(q, normed_all, w_qkv, w_qkv, v_bias.reshape(1, width))


def attend_back_kernel(q_ref, k_ref, v_ref, do_ref, *rest, heads, some):
    out_ref, dk_sum, dv_sum = rest[-3:]
    step = pl.program_id(0)
    rows = q_ref.shape[0]

    @pl.when(step == 0)
    def _():
        dk_sum[...] = jnp.zeros_like(dk_sum)
        dv_sum[...] = jnp.zeros_like(dv_sum)

    q, k, v, do = q_ref[...], k_ref[...], v_ref[...], do_ref[...]
    queries = [head_part(q, h, heads) for h in some]
    grads = [head_part(do, h, heads) for h in some]
    scores = [contract(x, k, 1, 1) for x in queries]
    prob_grads = [contract(x, v, 1, 1) for x in grads]
    dq = dk = dv = 0.0
    for h, qh, doh, s, dp in zip(some, queries, grads, scores, prob_grads):
        top = jnp.max(s, axis=-1, keepdims=True)
        e = jnp.exp2((s - top) * EXP_SCALE)
        inverse = 1.0 / jnp.sum(e, axis=-1, keepdims=True)
        inner = jnp.sum(e * dp, axis=-1, keepdims=True) * inverse
        p = e * inverse
        ds = (p * (dp - inner)).astype(bf16)
        dq = dq + head_part(contract(ds, k, 1, 0), h, heads)
        dk = dk + contract(ds, qh, 0, 0)
        dv = dv + contract(p.astype(bf16), doh, 0, 0)
    dk_sum[...] += dk
    dv_sum[...] += dv

    def put(m, i, x):
        if len(rest) == 4:
            x = x + rest[0][m, i].astype(f32)
        out_ref[m, i] = x.astype(bf16)

    put(step, 0, dq * 0.125)

    @pl.when(step == pl.num_programs(0) - 1)
    def _():
        for m in range(out_ref.shape[0]):
            put(m, 1, dk_sum[m * rows : (m + 1) * rows, :] * 0.125)
            put(m, 2, dv_sum[m * rows : (m + 1) * rows, :])


def attend_back(q, k, v, do, members, some=None, add=None):
    count, width = q.shape
    rows = count // members
    heads = width // HD
    part = pl.BlockSpec((rows, width), lambda i: (i, 0))
    full = pl.BlockSpec((count, width), lambda i: (0, 0))
    shape = (members, 3, rows, width)
    out = pl.BlockSpec(shape, lambda i: (0, 0, 0, 0))
    extra = [] if add is None else [add]
    return pl.pallas_call(
        functools.partial(attend_back_kernel, heads=heads, some=some or range(heads)),
        grid=(members,),
        in_specs=[part, full, full, part] + [out] * len(extra),
        out_specs=out,
        out_shape=jax.ShapeDtypeStruct(shape, bf16),
        scratch_shapes=[pltpu.VMEM((count, width), f32), pltpu.VMEM((count, width), f32)],
        compiler_params=pltpu.CompilerParams(vmem_limit_bytes=60 * MIB),
        cost_estimate=cost(33 if some is None else 17),
        name="attend_back",
    )(q, k, v, do, *extra)


def spec(block, index):
    return pl.BlockSpec(block, index)


def grad_rows_kernel(c_ref, l1, l0, r1, r0, other_ref, own_ref, sums):
    sums[...] = contract(l1[...], r1[...], 0, 0) + contract(l0[...], r0[...], 0, 0)
    count, n, _ = own_ref.shape
    for j in range(count):
        for ref, core in ((other_ref, 1 - c_ref[0]), (own_ref, c_ref[0])):
            ref[j] = sums[pl.ds(pl.multiple_of((2 * j + core) * n, n), n), :].astype(bf16)


def grad_rows(core, left, right, bands, part, parts):
    tokens, m = left[0].shape
    n = right[0].shape[1] // parts
    block = min(n, 512)
    first = part * (n // block)
    out = spec((bands // 2, m // bands, block), lambda j, c: (0, 0, j))
    whole = spec((tokens, m), lambda j, c: (0, 0))
    part = spec((tokens, block), lambda j, c: (0, first + j))
    return pl.pallas_call(
        grad_rows_kernel,
        grid_spec=pltpu.PrefetchScalarGridSpec(
            num_scalar_prefetch=1,
            grid=(n // block,),
            in_specs=[whole, whole, part, part],
            out_specs=[out, out],
            scratch_shapes=[pltpu.VMEM((m, block), f32)],
        ),
        out_shape=[jax.ShapeDtypeStruct((bands // 2, m // bands, n), bf16)] * 2,
        compiler_params=pltpu.CompilerParams(vmem_limit_bytes=60 * MIB),
        cost_estimate=cost(8),
        name="grad_rows",
    )(core.reshape(1), *left, *right)


def block_forward_kernel(
    x_ref, a_ref, wo_ref, bo_ref, g_ref, b_ref, wu_ref, bu_ref, wd_ref, bd_ref, lead_ref, g1_ref, b1_ref,
    n2_ref, r2_ref, low2_ref, hidden_ref, act_ref, *rest, last
):
    total = rest[-1]
    step = pl.program_id(0)

    @pl.when(step == 0)
    def _():
        middle = x_ref[...] + contract(a_ref[...], wo_ref[...], 1, 0) + bo_ref[...]
        n, r = norm_parts(middle)
        n2_ref[...] = n
        r2_ref[...] = r
        low2_ref[...] = (n * g_ref[...] + b_ref[...]).astype(bf16)
        total[...] = middle + bd_ref[...]

    hidden = contract(low2_ref[...], wu_ref[...], 1, 0) + bu_ref[...]
    hidden_ref[...] = hidden
    act = gelu(hidden).astype(bf16)
    act_ref[...] = act
    total[...] += contract(act, wd_ref[...], 1, 0)

    @pl.when(step == pl.num_programs(0) - 1)
    def _():
        carried = total[...]
        if last:
            rest[0][...] = carried.astype(bf16)
        else:
            x = carried + lead_ref[...]
            n, r = norm_parts(x)
            rest[0][...] = x
            rest[1][...] = n
            rest[2][...] = r
            rest[3][...] = (n * g1_ref[...] + b1_ref[...]).astype(bf16)


def block_forward(inputs, attended, weights, last):
    w_out, out_bias, ln2_gain, ln2_bias, w_up, up_bias, w_down, down_bias, lead, ln1_gain, ln1_bias = weights
    t, d = inputs.shape
    f = w_up.shape[1]
    block = 512
    row = lambda v: v.reshape(1, -1)
    full = spec((t, d), lambda i: (0, 0))
    vec = spec((1, d), lambda i: (0, 0))
    one = spec((t, 1), lambda i: (0, 0))
    wide = spec((t, block), lambda i: (0, i))
    shape = jax.ShapeDtypeStruct
    outs = [full, one, full, wide, wide] + ([full] if last else [full, full, one, full])
    shapes = [shape((t, d), f32), shape((t, 1), f32), shape((t, d), bf16), shape((t, f), f32), shape((t, f), bf16)]
    shapes += [shape((t, d), bf16)] if last else [
        shape((t, d), f32), shape((t, d), f32), shape((t, 1), f32), shape((t, d), bf16)
    ]
    return pl.pallas_call(
        functools.partial(block_forward_kernel, last=last),
        grid=(f // block,),
        in_specs=[
            full, full, spec((d, d), lambda i: (0, 0)), vec, vec, vec,
            spec((d, block), lambda i: (0, i)), spec((1, block), lambda i: (0, i)),
            spec((block, d), lambda i: (i, 0)), vec, vec, vec, vec,
        ],
        out_specs=outs,
        out_shape=shapes,
        scratch_shapes=[pltpu.VMEM((t, d), f32)],
        compiler_params=pltpu.CompilerParams(vmem_limit_bytes=40 * MIB),
        cost_estimate=cost(12),
        name="block_forward",
    )(
        inputs, attended, w_out, row(out_bias), row(ln2_gain), row(ln2_bias), w_up, row(up_bias), w_down,
        row(down_bias), row(lead), row(ln1_gain), row(ln1_bias),
    )


def put_sums(ref, *sums):
    for i, v in enumerate(sums):
        ref[i : i + 1, :] = v


def column_sum(x):
    return jnp.sum(x.astype(f32), axis=0, keepdims=True)


def block_backward_kernel(c_ref, grad_ref, h_ref, wd_ref, wu_ref, wo_ref, n_ref, r_ref, g_ref, *rest, grads, bands):
    if grads:
        l1_ref, x1_ref, x0_ref = rest[:3]
        z_other, x_other, z_own, x_own = rest[9:13]
        sums, rest = rest[14], rest[3:9] + rest[13:14]
    hg_ref, hsum_ref, middle_ref, branch_ref, sent_ref, sums_ref, total = rest
    step = pl.program_id(0)
    down = grad_ref[...].astype(bf16)
    low = (gelu_slope(h_ref[...]) * contract(down, wd_ref[...], 1, 1)).astype(bf16)
    hg_ref[...] = low
    hsum_ref[...] = column_sum(low)
    part = contract(low, wu_ref[...], 1, 1)
    if grads:
        sums[...] = contract(l1_ref[...], x1_ref[...], 0, 0) + contract(low, x0_ref[...], 0, 0)
        pairs = z_own.shape[0]
        n = sums.shape[0] // (2 * pairs)
        for q in range(pairs):
            for z, x, core in ((z_other, x_other, 1 - c_ref[0]), (z_own, x_own, c_ref[0])):
                start = pl.multiple_of((2 * q + core) * n, n)
                z[q] = sums[pl.ds(start, n // 2), :].astype(bf16)
                x[q] = sums[pl.ds(start + n // 2, n // 2), :].astype(bf16)

    @pl.when(step == 0)
    def _():
        total[...] = part

    @pl.when(step > 0)
    def _():
        total[...] += part

    @pl.when(step == pl.num_programs(0) - 1)
    def _():
        dv, gain, bias = norm_back(total[...], n_ref[...], r_ref[...], g_ref[...])
        middle = grad_ref[...] + dv
        middle_ref[...] = middle
        branch = middle.astype(bf16)
        branch_ref[...] = branch
        put_sums(sums_ref, gain, bias, column_sum(branch), column_sum(down))
        w = sent_ref.shape[2]
        attended = contract(branch, wo_ref[...], 1, 1).astype(bf16)
        for m in range(sent_ref.shape[0]):
            sent_ref[m] = attended[:, m * w : (m + 1) * w]


def block_backward(core, grad, hidden, w_down, w_up, w_out, n2, r2, gain, members, grads=()):
    t, d = grad.shape
    f = hidden.shape[1]
    block = 512
    bands = 2 * members
    full = spec((t, d), lambda i, c: (0, 0))
    wide = spec((t, block), lambda i, c: (0, i))
    sent = (members, t, d // members)
    shape = jax.ShapeDtypeStruct
    outs = [
        wide, spec((1, block), lambda i, c: (0, i)), full, full,
        spec(sent, lambda i, c: (0, 0, 0)), spec((8, d), lambda i, c: (0, 0)),
    ]
    shapes = [
        shape((t, f), bf16), shape((1, f), f32), shape((t, d), f32), shape((t, d), bf16),
        shape(sent, bf16), shape((8, d), f32),
    ]
    scratch = [pltpu.VMEM((t, d), f32)]
    if grads:
        n = f // bands
        pairs = block // (2 * n)
        part = spec((pairs, n // 2, d), lambda i, c: (i, 0, 0))
        outs += [part] * 4
        shapes += [shape((bands // 2, n // 2, d), bf16), shape((bands // 2, n // 2 + d // bands, d), bf16)] * 2
        scratch += [pltpu.VMEM((block, d), f32)]
    return pl.pallas_call(
        functools.partial(block_backward_kernel, grads=bool(grads), bands=bands),
        grid_spec=pltpu.PrefetchScalarGridSpec(
            num_scalar_prefetch=1,
            grid=(f // block,),
            in_specs=[
                full, wide, spec((block, d), lambda i, c: (i, 0)), spec((d, block), lambda i, c: (0, i)),
                spec((d, d), lambda i, c: (0, 0)), full, spec((t, 1), lambda i, c: (0, 0)),
                spec((1, d), lambda i, c: (0, 0)),
            ] + [wide, full, full][: len(grads)],
            out_specs=outs,
            scratch_shapes=scratch,
        ),
        out_shape=shapes,
        compiler_params=pltpu.CompilerParams(vmem_limit_bytes=(60 if grads else 48) * MIB),
        cost_estimate=cost(18 if grads else 14),
        name="block_backward",
    )(core.reshape(1), grad, hidden, w_down, w_up, w_out, n2, r2, gain.reshape(1, d), *grads)


def grad_out_kernel(c_ref, l1, l0, r1, r0, _, __, other_ref, own_ref, sums, *, pairs):
    sums[...] = contract(l1[...], r1[...], 0, 0) + contract(l0[...], r0[...], 0, 0)
    n = own_ref.shape[1]
    for q in range(pairs):
        for ref, core in ((other_ref, 1 - c_ref[0]), (own_ref, c_ref[0])):
            ref[q] = sums[pl.ds(pl.multiple_of((2 * q + core) * n, n), n), :].astype(bf16)


def grad_out(core, left, right, bands, other, own):
    tokens, m = left[0].shape
    count, height, d = own.shape
    n = m // bands
    pairs = max(1, 256 // (2 * n))
    columns = spec((tokens, 2 * n * pairs), lambda j, c: (0, j))
    whole = spec((tokens, d), lambda j, c: (0, 0))
    out = spec((pairs, n, d), lambda j, c: (j, height // n - 1, 0))
    anywhere = pl.BlockSpec(memory_space=pl.ANY)
    return pl.pallas_call(
        functools.partial(grad_out_kernel, pairs=pairs),
        grid_spec=pltpu.PrefetchScalarGridSpec(
            num_scalar_prefetch=1,
            grid=(count // pairs,),
            in_specs=[columns, columns, whole, whole, anywhere, anywhere],
            out_specs=[out, out],
            scratch_shapes=[pltpu.VMEM((2 * n * pairs, d), f32)],
        ),
        out_shape=[jax.ShapeDtypeStruct(own.shape, bf16)] * 2,
        input_output_aliases={5: 0, 6: 1},
        compiler_params=pltpu.CompilerParams(vmem_limit_bytes=60 * MIB),
        cost_estimate=cost(3),
        name="grad_out",
    )(core.reshape(1), *left, *right, other, own)


def qkv_backward_kernel(b_ref, wq_ref, wk_ref, wv_ref, m_ref, n_ref, r_ref, g_ref, grad_ref, low_ref, sums_ref, qv_ref, total):
    step = pl.program_id(0)
    w = b_ref.shape[3]
    part = None
    for m in range(b_ref.shape[0]):
        for i, ref in enumerate((wq_ref, wk_ref, wv_ref)):
            x = contract(b_ref[m, i], ref[:, m * w : (m + 1) * w], 1, 1)
            part = x if part is None else part + x
        qv_ref[0:1, m * w : (m + 1) * w] = column_sum(b_ref[m, 0])
        qv_ref[1:2, m * w : (m + 1) * w] = column_sum(b_ref[m, 2])

    @pl.when(step == 0)
    def _():
        total[...] = part

    @pl.when(step > 0)
    def _():
        total[...] += part

    @pl.when(step == pl.num_programs(0) - 1)
    def _():
        dv, gain, bias = norm_back(total[...], n_ref[...], r_ref[...], g_ref[...])
        grad = m_ref[...] + dv
        grad_ref[...] = grad
        low_ref[...] = grad[grad.shape[0] - low_ref.shape[0] :].astype(bf16)
        put_sums(sums_ref, gain, bias, column_sum(grad))


def qkv_backward(back, w_qkv, middle_grad, n1, r1, gain, low):
    members, _, t, w = back.shape
    d = members * w
    at_once = max(2, 128 // w)
    block = at_once * w
    shift = d // block
    full = spec((t, d), lambda i: (0, 0))
    weight = [spec((d, block), lambda i, s=s: (0, s * shift + i)) for s in range(3)]
    shape = jax.ShapeDtypeStruct
    return pl.pallas_call(
        qkv_backward_kernel,
        grid=(members // at_once,),
        in_specs=[spec((at_once, 3, t, w), lambda i: (i, 0, 0, 0))] + weight + [
            full, full, spec((t, 1), lambda i: (0, 0)), spec((1, d), lambda i: (0, 0)),
        ],
        out_specs=[
            full, spec((low, d), lambda i: (0, 0)), spec((8, d), lambda i: (0, 0)),
            spec((8, block), lambda i: (0, i)),
        ],
        out_shape=[
            shape((t, d), f32), shape((low, d), bf16), shape((8, d), f32), shape((8, d), f32),
        ],
        scratch_shapes=[pltpu.VMEM((t, d), f32)],
        compiler_params=pltpu.CompilerParams(vmem_limit_bytes=60 * MIB),
        cost_estimate=cost(12),
        name="qkv_backward",
    )(back, w_qkv, w_qkv, w_qkv, middle_grad, n1, r1, gain.reshape(1, d))


def grad_heads_kernel(d_ref, n_ref, *rest):
    out_ref = rest[-1]
    rows = d_ref.shape[2]
    for i in range(3):
        total = rest[0][i] if len(rest) == 2 else jnp.zeros(out_ref.shape[1:], f32)
        for m in range(d_ref.shape[0]):
            total += contract(d_ref[m, i], n_ref[m * rows : (m + 1) * rows, :], 0, 0)
        out_ref[i] = total.astype(out_ref.dtype)


def grad_heads(d, normed_all, add, kind):
    members, _, rows, width = d.shape
    dim = normed_all.shape[1]
    shape = (3, width, dim)
    out = spec((3, width, dim // 4), lambda i: (0, 0, i))
    extra = [] if add is None else [add]
    return pl.pallas_call(
        grad_heads_kernel,
        grid=(4,),
        in_specs=[
            spec(d.shape, lambda i: (0, 0, 0, 0)),
            spec((members * rows, dim // 4), lambda i: (0, i)),
        ]
        + [out] * len(extra),
        out_specs=out,
        out_shape=jax.ShapeDtypeStruct(shape, kind),
        compiler_params=pltpu.CompilerParams(vmem_limit_bytes=60 * MIB),
        cost_estimate=cost(5),
        name="grad_heads",
    )(d, normed_all, *extra)


def take_kernel(table, *refs):
    for i in range(refs[-1].shape[0]):
        total = refs[0][table[i]].astype(f32)
        for r in refs[1:-1]:
            total = total + r[table[i]].astype(f32)
        refs[-1][i] = total.astype(bf16)


def take(terms, table):
    shape = terms[0].shape
    count = table.shape[0]
    return pl.pallas_call(
        take_kernel,
        grid_spec=pltpu.PrefetchScalarGridSpec(
            num_scalar_prefetch=1,
            grid=(1,),
            in_specs=[spec(shape, lambda i, t: (0, 0, 0))] * len(terms),
            out_specs=spec((count,) + shape[1:], lambda i, t: (0, 0, 0)),
        ),
        out_shape=jax.ShapeDtypeStruct((count,) + shape[1:], bf16),
        compiler_params=pltpu.CompilerParams(vmem_limit_bytes=60 * MIB),
        cost_estimate=cost(3),
        name="take",
    )(table, *terms)


def join_kernel(i_ref, own_ref, other_ref, out_ref):
    half = other_ref.shape[0]
    out_ref[i_ref[0]] = own_ref[:half]
    out_ref[1 - i_ref[0]] = other_ref[...].astype(f32)


def join(index, own, other):
    half, d = other.shape
    full = spec((half, d), lambda i, c: (0, 0))
    return pl.pallas_call(
        join_kernel,
        grid_spec=pltpu.PrefetchScalarGridSpec(
            num_scalar_prefetch=1,
            grid=(1,),
            in_specs=[full, full],
            out_specs=spec((2, half, d), lambda i, c: (0, 0, 0)),
        ),
        out_shape=jax.ShapeDtypeStruct((2, half, d), f32),
        compiler_params=pltpu.CompilerParams(vmem_limit_bytes=8 * MIB),
        cost_estimate=cost(2),
        name="join",
    )(index.reshape(1), own, other)


def unit_tables(bands, x_count, width, dim):
    members = bands // 2
    unit = math.gcd(HD, 3 * dim // bands)
    per_band = 3 * dim // bands // unit
    made, slots, place = [], [], {}
    for g in range(members):
        units = [(b * dim + g * width) // unit + i for b in range(3) for i in range(width // unit)]
        by_low = [[] for _ in range(members)]
        for local, u in enumerate(units):
            band = u // per_band
            core, x, zl = band % 2, band // 2 % x_count, band // (2 * x_count) % 2
            low = (core * 2 + zl) * x_count + x
            place[u] = (g, len(by_low[low]))
            by_low[low].append(local)
        made.append(by_low)
    most = max(len(l) for by_low in made for l in by_low)
    send = np.zeros((members, members * most), np.int32)
    for g, by_low in enumerate(made):
        for low, locals_ in enumerate(by_low):
            for m, local in enumerate(locals_):
                send[g, low * most + m] = local
    keep = np.zeros((members, 2, per_band), np.int32)
    for u, (g, m) in place.items():
        band = u // per_band
        core, x, zl = band % 2, band // 2 % x_count, band // (2 * x_count) % 2
        low = (core * 2 + zl) * x_count + x
        keep[low, band // members, u % per_band] = g * most + m
    return unit, send, keep


def norm_parts(v):
    centred = v - jnp.mean(v, axis=-1, keepdims=True)
    r = lax.rsqrt(jnp.mean(centred * centred, axis=-1, keepdims=True) + EPS)
    return centred * r, r


def norm_back(dy, n, r, gain):
    dyg = dy * gain
    mean_one = jnp.mean(dyg, axis=-1, keepdims=True)
    mean_two = jnp.mean(dyg * n, axis=-1, keepdims=True)
    dv = r * (dyg - mean_one - n * mean_two)
    return dv, jnp.sum(dy * n, axis=0, keepdims=True), jnp.sum(dy, axis=0, keepdims=True)


def gelu(x):
    return 0.5 * x * (1.0 + jnp.tanh(GELU_A * (x + GELU_B * x * x * x)))


def gelu_slope(x):
    t = jnp.tanh(GELU_A * (x + GELU_B * x * x * x))
    return 0.5 * (1.0 + t) + 0.5 * x * (1.0 - t * t) * (GELU_A * (1.0 + 3.0 * GELU_B * x * x))


def dot(a, b):
    return jnp.dot(a, b, preferred_element_type=f32)


def dot_t(a, b):
    return contract(a, b, 1, 1)


def swap(x, axis):
    return lax.ppermute(x, axis, SWAP)


def pin(x, *first):
    return lax.optimization_barrier((x,) + first)[0]


def total(terms):
    out = terms[0].astype(f32)
    for t in terms[1:]:
        out = out + t.astype(f32)
    return out


class Share:
    def __init__(self, terms, names):
        self.terms = list(terms)
        self.names = list(names)

    def halve(self, axis, *first):
        if axis not in self.names:
            return self.terms[-1]
        dim = self.names.index(axis)
        i = lax.axis_index(axis)
        terms = [pin(t, *first) if first else t for t in self.terms[-1:]] + self.terms[:-1]
        there = [lax.dynamic_index_in_dim(t, 1 - i, dim, keepdims=False) for t in terms]
        self.terms = [lax.dynamic_index_in_dim(t, i, dim, keepdims=False) for t in terms]
        self.names.remove(axis)
        sent = total(there).astype(bf16)
        self.terms.append(swap(sent, axis))
        return sent


def body(
    fields,
    lead_bucket,
    cotangent,
    lead_table,
    ln1_gain,
    ln1_bias,
    w_qkv,
    q_bias,
    v_bias,
    w_out,
    out_bias,
    ln2_gain,
    ln2_bias,
    w_up,
    up_bias,
    w_down,
    down_bias,
    *,
    axes,
    x_axes,
    samp_count,
):
    band = tuple(axes)
    low = ("core", "zl") + x_axes[::-1]
    members = 2 ** len(low)
    order = x_axes + ("zl", "core")
    D = w_out.shape[0]
    W = D // members
    half = fields.shape[1]
    rows = 2 * half
    two = samp_count == 2
    zh = lax.axis_index("zh")
    me = lax.axis_index(low)

    def pick(x, i):
        return lax.dynamic_index_in_dim(x, i, 0, keepdims=False)

    def to_sample(x):
        return jnp.concatenate([pick(x, zh), swap(pick(x, 1 - zh), "zh")])

    def to_band(x):
        own = x[:half]
        other = swap(x[half:].astype(bf16), "zh").astype(x.dtype)
        return jnp.where(zh == 0, jnp.stack([own, other]), jnp.stack([other, own]))

    def gather(x):
        if len(x_axes) == 1:
            x_axis = x_axes[0]
            cut = x.shape[0] // 2
            by_x = swap(x, x_axis)
            by_z = swap(x, "zl")
            far = [swap(by_x[:cut], "zl"), swap(by_z[cut:], x_axis)]
            pieces = [(x, 0, 0), (by_x, 1, 0), (by_z, 2, 0), (far[0], 3, 0), (far[1], 3, cut)]
            pieces += [(swap(p, "core"), 4 + k, o) for p, k, o in pieces]
        else:
            pieces = [(x, 0, 0)]
            for bit, axis in enumerate(order):
                pieces += [(swap(p, axis), k + 2**bit, 0) for p, k, _ in pieces]
        out = jnp.zeros((members * rows, D), bf16)
        for piece, k, offset in pieces:
            out = lax.dynamic_update_slice(out, piece, ((me ^ k) * rows + offset, 0))
        return out

    lead_row = pick(lead_table, pick(lead_bucket, zh)).astype(f32)
    carried = to_sample(fields).astype(f32)

    def member_columns(x, block):
        return lax.dynamic_slice_in_dim(x, block * D + me * W, W, x.ndim - 1)

    kept = []
    inputs = carried + lead_row
    n1, r1 = norm_parts(inputs)
    normed = (n1 * ln1_gain + ln1_bias).astype(bf16)
    weights = (w_out, out_bias, ln2_gain, ln2_bias, w_up, up_bias, w_down, down_bias, lead_row, ln1_gain, ln1_bias)
    for index in range(STEPS):
        normed_all = gather(normed)
        queries = (dot(normed, w_qkv[:, :D]) + q_bias).astype(bf16)
        if index == 0:
            out_grad = to_sample(pin(cotangent, normed_all))
        attended = attend(queries, normed_all, w_qkv, v_bias)
        if index == 0:
            attended, out_grad = pin((attended, out_grad))
        last = index == STEPS - 1
        n2, r2, normed_two, hidden, activated, *after = block_forward(inputs, attended, weights, last)
        kept.append((n1, r1, normed_all, attended, n2, r2, normed_two, hidden, activated))
        if not last:
            inputs, n1, r1, normed = after
    carried = after[0]
    result = to_band(carried)

    grad = out_grad
    small = None
    core = lax.axis_index("core")
    y = lax.axis_index("samp")
    bands = 2 ** len(axes)
    names = axes[:-1]
    cube = (2,) * len(names)
    later = None
    w_heads = None
    unit, send_table, keep_table = unit_tables(bands, 2 ** len(x_axes), W, D)
    send_row, keep_row = pick(jnp.asarray(send_table), me), pick(jnp.asarray(keep_table), me)
    keep_rows = pick(keep_row, zh), pick(keep_row, 1 - zh)
    def split_rows(x, rows_two):
        n, r, c = x.shape
        return x.reshape(cube + ((2, r // 2) if rows_two else (r,)) + (c,))

    own_weight = jnp.concatenate([member_columns(w_qkv, i) for i in range(3)], axis=1)
    own_bias = jnp.concatenate([member_columns(q_bias, 0), jnp.zeros((W,), f32), member_columns(v_bias, 0)])

    def own_part(index):
        own = (dot(kept[index][2], own_weight) + own_bias).astype(bf16)
        return own[:, :W], own[:, W : 2 * W], own[:, 2 * W :]

    owns = {}
    for index in reversed(range(STEPS)):
        n1, r1, normed_all, attended, n2, r2, normed_two, hidden, activated = kept[index]
        last = index == 0
        if last:
            grads = (later[2], later[3], normed_two)
        else:
            down_grad = grad.astype(bf16)
            grads = ()
        hidden_grad, hidden_sum, middle_grad, branch_grad, sent, sums_two, *ups = block_backward(
            core, grad, hidden, w_down, w_up, w_out, n2, r2, ln2_gain, members, grads
        )
        own_grad = lax.all_to_all(sent, low, 0, 0, tiled=True).reshape(members * rows, W)
        if last:
            z_other, x_other, z_own, x_own = ups
            z_core = swap(z_other, "core")
            left, right = (later[0], pin(down_grad, sent)), (later[1], activated)
            d_other, d_own = grad_rows(core, left, right, bands, 0, 1)
            d_core = swap(d_other, "core")
            x_other, x_own = grad_out(
                core, (later[4], pin(branch_grad, d_other)), (later[5], attended), bands, x_other, x_own
            )
            x_core = swap(x_other, "core")
            samp = ("samp",) * two
            d_terms = pin((d_own, d_core), x_other)
            down_share = Share([split_rows(t, two) for t in d_terms], names + samp)
            z_terms = pin((z_own, z_core), down_share.halve("samp"))
            z_share = Share([split_rows(t, two) for t in z_terms], names + samp)
            x_terms = pin((x_own, x_core), z_share.halve("zl"))
            x_share = Share([split_rows(t, two) for t in x_terms], names + samp)
            own_grad = pin(own_grad, x_share.halve(x_axes[0]))
            heads = W // HD
            d_heads = attend_back(*owns[0], own_grad, members, range((heads + 1) // 2))
            own_grad, d_heads, z_share.terms[-1] = pin((own_grad, d_heads, z_share.terms[-1]))
            sent = z_share.halve("zh")
            if heads > 1:
                own_grad, d_heads = pin((own_grad, d_heads), sent)
                d_heads = attend_back(*owns[0], own_grad, members, range(heads // 2, heads), d_heads)
            shares = (z_share, x_share, down_share)
            waits = pin((d_heads, *(t.terms[-1] for t in shares)))
            d_heads = waits[0]
            for t, value in zip(shares, waits[1:]):
                t.terms[-1] = value
            sent = [x_share.halve("samp"), z_share.halve("samp")] + [down_share.halve(a) for a in x_axes]
            d_heads = pin(d_heads, *sent)
        else:
            own_grad, send_row, keep_rows = pin((own_grad, send_row, keep_rows), result)
            later = (down_grad, activated, hidden_grad, normed_two, branch_grad, attended)
            owns[index] = own_part(index)
            d_heads = attend_back(*owns[index], own_grad, members)
        back = lax.all_to_all(d_heads, low, 0, 0, tiled=True)
        w_heads = grad_heads(d_heads, normed_all, w_heads, bf16 if last else f32)
        if last:
            units = w_heads.reshape(-1, unit, D)
            if two:
                there = lax.dynamic_slice_in_dim(units, (1 - y) * (D // 2), D // 2, 2)
                here = lax.dynamic_slice_in_dim(units, y * (D // 2), D // 2, 2)
                units = [here, swap(there, "samp")]
            else:
                there, units = units, [units]
            back = pin(back, there)
            x_share.terms[-1], z_share.terms[-1] = pin((x_share.terms[-1], z_share.terms[-1]), back)
            sent = [x_share.halve(a) for a in x_axes[1:] + ("zl",)] + [z_share.halve(a) for a in x_axes]
            units[-1] = pin(units[-1], *sent)
            outgoing = take(units, send_row)
            incoming = lax.all_to_all(outgoing, low, 0, 0, tiled=True)
            down_share.terms[-1] = pin(down_share.terms[-1], outgoing)
            back = pin(back, down_share.halve("zl"))
        else:
            owns[0] = own_part(0)
            back = pin(back, w_heads, *owns[0])
        grad, low_grad, sums_one, sums_qv = qkv_backward(
            back, w_qkv, middle_grad, n1, r1, ln1_gain, half if last else rows
        )
        down_grad = low_grad
        step_small = (sums_one[:3], sums_qv[:2], sums_two[:4], hidden_sum)
        small = step_small if small is None else tuple(a + b for a, b in zip(small, step_small))
    fields_sent = low_grad
    fields_other = swap(fields_sent, "zh")
    x_share.terms[-1] = pin(x_share.terms[-1], fields_sent)
    incoming = pin(incoming, x_share.halve("zh"))
    there = take([incoming], keep_rows[1])
    other = swap(there, "zh")
    one, qv, two_sums, up_sum = pin(small, there)
    samples = 2 * samp_count
    slot = 2 * y + zh
    mine = lax.broadcasted_iota(jnp.int32, (samples, 1), 0) == slot
    leads = jnp.where(mine, one[2:3], 0.0)
    lane = lax.broadcasted_iota(jnp.int32, (bands, D // bands), 1) == slot
    bucket = jnp.where(lane & (me == 0), pick(lead_bucket, zh).astype(f32), 0.0)
    vectors = jnp.concatenate([one[:2], qv, two_sums, leads])
    vectors = vectors.reshape(-1, bands, D // bands).transpose(1, 0, 2).reshape(bands, -1)
    vectors = jnp.concatenate([vectors, up_sum.reshape(bands, -1), bucket], axis=1)
    sums = vectors
    vectors = lax.all_to_all(vectors, band, 0, 0, tiled=True)

    def both(x):
        x = x.astype(bf16)
        if not two:
            return lax.psum(x, "samp").astype(f32)
        other = swap(x, "samp")
        return jnp.concatenate([jnp.where(y == 0, x, other), jnp.where(y == 0, other, x)]).astype(f32)

    def both_cut(x, n):
        if not two:
            x = both(x)
            return x[:n], x[n:]
        x = x.astype(bf16)
        other = swap(x, "samp")
        first, second = jnp.where(y == 0, x, other), jnp.where(y == 0, other, x)
        x = jnp.concatenate([first, second]).astype(f32)
        return x[:n], x[n:]

    incoming, down_share.terms[-1], z_share.terms[-1] = pin((incoming, down_share.terms[-1], z_share.terms[-1]), sums)
    sent = down_share.halve("zh")
    own = take([incoming], keep_rows[0])
    up_first = total(z_share.terms).astype(bf16)
    late = (vectors, fields_other, other, down_share.terms[-1], x_share.terms[-1])
    late = pin(late, sent, own, up_first)
    vectors, fields_other, other, down_share.terms[-1], x_share.terms[-1] = late
    vectors = jnp.sum(vectors, axis=0)
    vectors = vectors + swap(vectors, "samp") if two else lax.psum(vectors, "samp")
    own = total([own, other]).astype(bf16).reshape(3 * D // bands, -1)
    if two:
        other = swap(own, "samp")
        own = jnp.concatenate([jnp.where(y == 0, own, other), jnp.where(y == 0, other, own)], axis=1)
    else:
        own = lax.psum(own, "samp")
    w_qkv_grad = own.astype(f32).T

    w_down_grad = both(total(down_share.terms)).T
    n_up = w_up.shape[1] // bands
    bottom = both_cut(total(x_share.terms), n_up // 2)
    w_out_grad = bottom[1].T
    w_up_grad = jnp.concatenate([both(up_first), bottom[0]]).T
    fields_grad = join(zh, grad, fields_other)

    w = D // bands
    leads = vectors[8 * w : (8 + samples) * w].reshape(samples, w)
    up_grad = vectors[(8 + samples) * w : -w]
    buckets = vectors[-w:][:samples].astype(jnp.int32)
    one_hot = (buckets[:, None] == jnp.arange(lead_table.shape[0], dtype=jnp.int32)[None, :]).astype(f32)
    lead_grad = jnp.dot(one_hot.T, leads, precision=lax.Precision.HIGHEST)
    rows_of = lambda i: vectors[i * w : (i + 1) * w]
    g = [rows_of(i) for i in (0, 1, 2, 3, 6, 4, 5)] + [up_grad, rows_of(7)]
    return (
        result,
        fields_grad,
        lead_grad,
        g[0],
        g[1],
        w_qkv_grad,
        g[2],
        g[3],
        w_out_grad,
        g[4],
        g[5],
        g[6],
        w_up_grad,
        g[7],
        w_down_grad,
        g[8],
    )


def solution(mesh):
    samp_count, band_count = mesh.shape["samp"], mesh.shape["band"]
    x_axes = tuple(f"x{i}" for i in range((band_count // 8).bit_length() - 1))
    axes = ("zh", "zl") + x_axes + ("core",)
    assert 2 ** len(axes) == band_count
    fine = Mesh(mesh.devices.reshape((samp_count,) + (2,) * len(axes)), ("samp",) + axes)
    tokens = P("samp", axes, None)
    columns, vector = P(None, axes), P(axes)
    in_specs = (tokens, P("samp"), tokens) + (P(),) * 14
    out_specs = (
        tokens,
        tokens,
        columns,
        vector,
        vector,
        columns,
        vector,
        vector,
        columns,
        vector,
        vector,
        vector,
        columns,
        vector,
        columns,
        vector,
    )
    run = functools.partial(body, axes=axes, x_axes=x_axes, samp_count=samp_count)
    return jax.shard_map(run, mesh=fine, in_specs=in_specs, out_specs=out_specs, check_vma=False)
```

```python
import functools
import math

import jax
import jax.numpy as jnp
import numpy as np
from jax import lax
from jax.experimental import pallas as pl
from jax.experimental.pallas import tpu as pltpu
from jax.sharding import Mesh
from jax.sharding import PartitionSpec as P

HD = 64
STEPS = 2
EPS = 1e-05
EXP_SCALE = 0.125 * 1.4426950408889634
GELU_A = 0.7978845608028654
GELU_B = 0.044715
MIB = 2**20
SWAP = [(0, 1), (1, 0)]
f32 = jnp.float32
bf16 = jnp.bfloat16


def cost(us):
    return pl.CostEstimate(flops=int(us * 1.15e9), bytes_accessed=1000, transcendentals=0)


def contract(a, b, a_dim, b_dim):
    return lax.dot_general(a, b, (((a_dim,), (b_dim,)), ((), ())), preferred_element_type=f32)


def head_part(x, h, heads):
    if heads == 1:
        return x
    lane = lax.broadcasted_iota(jnp.int32, x.shape, 1)
    return jnp.where(lane // HD == h, x, jnp.zeros_like(x))


def attend_kernel(q_ref, n_ref, wk_ref, wv_ref, b_ref, o_ref):
    normed = n_ref[...]
    keys = contract(normed, wk_ref[...], 1, 0).astype(bf16)
    values = (contract(normed, wv_ref[...], 1, 0) + b_ref[...]).astype(bf16)
    pair = 2 * HD
    for start in range(0, q_ref.shape[1], pair):
        q, k, v = q_ref[:, start : start + pair], keys[:, start : start + pair], values[:, start : start + pair]
        out = None
        for h in range(2):
            s = contract(head_part(q, h, 2), k, 1, 1)
            top = jnp.max(s, axis=-1, keepdims=True)
            e = jnp.exp2((s - top) * EXP_SCALE)
            total = jnp.sum(e, axis=-1, keepdims=True)
            o = head_part(contract(e.astype(bf16), v, 1, 0) / total, h, 2)
            out = o if out is None else out + o
        o_ref[:, start : start + pair] = out.astype(bf16)


def attend(q, normed_all, w_qkv, v_bias):
    rows, width = q.shape
    count = normed_all.shape[0]
    block = 4 * HD
    own = spec((rows, block), lambda j: (0, j))
    shift = width // block
    return pl.pallas_call(
        attend_kernel,
        grid=(width // block,),
        in_specs=[
            own,
            spec((count, width), lambda j: (0, 0)),
            spec((width, block), lambda j: (0, shift + j)),
            spec((width, block), lambda j: (0, 2 * shift + j)),
            spec((1, block), lambda j: (0, j)),
        ],
        out_specs=own,
        out_shape=jax.ShapeDtypeStruct((rows, width), bf16),
        compiler_params=pltpu.CompilerParams(vmem_limit_bytes=40 * MIB),
        cost_estimate=cost(24),
        name="attend",
    )(q, normed_all, w_qkv, w_qkv, v_bias.reshape(1, width))


def attend_back_kernel(q_ref, k_ref, v_ref, do_ref, *rest, heads, some):
    out_ref, dk_sum, dv_sum = rest[-3:]
    step = pl.program_id(0)
    rows = q_ref.shape[0]

    @pl.when(step == 0)
    def _():
        dk_sum[...] = jnp.zeros_like(dk_sum)
        dv_sum[...] = jnp.zeros_like(dv_sum)

    q, k, v, do = q_ref[...], k_ref[...], v_ref[...], do_ref[...]
    queries = [head_part(q, h, heads) for h in some]
    grads = [head_part(do, h, heads) for h in some]
    scores = [contract(x, k, 1, 1) for x in queries]
    prob_grads = [contract(x, v, 1, 1) for x in grads]
    dq = dk = dv = 0.0
    for h, qh, doh, s, dp in zip(some, queries, grads, scores, prob_grads):
        top = jnp.max(s, axis=-1, keepdims=True)
        e = jnp.exp2((s - top) * EXP_SCALE)
        inverse = 1.0 / jnp.sum(e, axis=-1, keepdims=True)
        inner = jnp.sum(e * dp, axis=-1, keepdims=True) * inverse
        p = e * inverse
        ds = (p * (dp - inner)).astype(bf16)
        dq = dq + head_part(contract(ds, k, 1, 0), h, heads)
        dk = dk + contract(ds, qh, 0, 0)
        dv = dv + contract(p.astype(bf16), doh, 0, 0)
    dk_sum[...] += dk
    dv_sum[...] += dv

    def put(m, i, x):
        if len(rest) == 4:
            x = x + rest[0][m, i].astype(f32)
        out_ref[m, i] = x.astype(bf16)

    put(step, 0, dq * 0.125)

    @pl.when(step == pl.num_programs(0) - 1)
    def _():
        for m in range(out_ref.shape[0]):
            put(m, 1, dk_sum[m * rows : (m + 1) * rows, :] * 0.125)
            put(m, 2, dv_sum[m * rows : (m + 1) * rows, :])


def attend_back(q, k, v, do, members, some=None, add=None):
    count, width = q.shape
    rows = count // members
    heads = width // HD
    part = pl.BlockSpec((rows, width), lambda i: (i, 0))
    full = pl.BlockSpec((count, width), lambda i: (0, 0))
    shape = (members, 3, rows, width)
    out = pl.BlockSpec(shape, lambda i: (0, 0, 0, 0))
    extra = [] if add is None else [add]
    return pl.pallas_call(
        functools.partial(attend_back_kernel, heads=heads, some=some or range(heads)),
        grid=(members,),
        in_specs=[part, full, full, part] + [out] * len(extra),
        out_specs=out,
        out_shape=jax.ShapeDtypeStruct(shape, bf16),
        scratch_shapes=[pltpu.VMEM((count, width), f32), pltpu.VMEM((count, width), f32)],
        compiler_params=pltpu.CompilerParams(vmem_limit_bytes=60 * MIB),
        cost_estimate=cost(33 if some is None else 17),
        name="attend_back",
    )(q, k, v, do, *extra)


def spec(block, index):
    return pl.BlockSpec(block, index)


def grad_rows_kernel(c_ref, l1, l0, r1, r0, other_ref, own_ref, sums):
    sums[...] = contract(l1[...], r1[...], 0, 0) + contract(l0[...], r0[...], 0, 0)
    count, n, _ = own_ref.shape
    for j in range(count):
        for ref, core in ((other_ref, 1 - c_ref[0]), (own_ref, c_ref[0])):
            ref[j] = sums[pl.ds(pl.multiple_of((2 * j + core) * n, n), n), :].astype(bf16)


def grad_rows(core, left, right, bands, part, parts):
    tokens, m = left[0].shape
    n = right[0].shape[1] // parts
    block = min(n, 512)
    first = part * (n // block)
    out = spec((bands // 2, m // bands, block), lambda j, c: (0, 0, j))
    whole = spec((tokens, m), lambda j, c: (0, 0))
    part = spec((tokens, block), lambda j, c: (0, first + j))
    return pl.pallas_call(
        grad_rows_kernel,
        grid_spec=pltpu.PrefetchScalarGridSpec(
            num_scalar_prefetch=1,
            grid=(n // block,),
            in_specs=[whole, whole, part, part],
            out_specs=[out, out],
            scratch_shapes=[pltpu.VMEM((m, block), f32)],
        ),
        out_shape=[jax.ShapeDtypeStruct((bands // 2, m // bands, n), bf16)] * 2,
        compiler_params=pltpu.CompilerParams(vmem_limit_bytes=60 * MIB),
        cost_estimate=cost(8),
        name="grad_rows",
    )(core.reshape(1), *left, *right)


def block_forward_kernel(
    x_ref, a_ref, wo_ref, bo_ref, g_ref, b_ref, wu_ref, bu_ref, wd_ref, bd_ref, lead_ref, g1_ref, b1_ref,
    n2_ref, r2_ref, low2_ref, hidden_ref, act_ref, *rest, last
):
    total = rest[-1]
    step = pl.program_id(0)

    @pl.when(step == 0)
    def _():
        middle = x_ref[...] + contract(a_ref[...], wo_ref[...], 1, 0) + bo_ref[...]
        n, r = norm_parts(middle)
        n2_ref[...] = n
        r2_ref[...] = r
        low2_ref[...] = (n * g_ref[...] + b_ref[...]).astype(bf16)
        total[...] = middle + bd_ref[...]

    hidden = contract(low2_ref[...], wu_ref[...], 1, 0) + bu_ref[...]
    hidden_ref[...] = hidden
    act = gelu(hidden).astype(bf16)
    act_ref[...] = act
    total[...] += contract(act, wd_ref[...], 1, 0)

    @pl.when(step == pl.num_programs(0) - 1)
    def _():
        carried = total[...]
        if last:
            rest[0][...] = carried.astype(bf16)
        else:
            x = carried + lead_ref[...]
            n, r = norm_parts(x)
            rest[0][...] = x
            rest[1][...] = n
            rest[2][...] = r
            rest[3][...] = (n * g1_ref[...] + b1_ref[...]).astype(bf16)


def block_forward(inputs, attended, weights, last):
    w_out, out_bias, ln2_gain, ln2_bias, w_up, up_bias, w_down, down_bias, lead, ln1_gain, ln1_bias = weights
    t, d = inputs.shape
    f = w_up.shape[1]
    block = 512
    row = lambda v: v.reshape(1, -1)
    full = spec((t, d), lambda i: (0, 0))
    vec = spec((1, d), lambda i: (0, 0))
    one = spec((t, 1), lambda i: (0, 0))
    wide = spec((t, block), lambda i: (0, i))
    shape = jax.ShapeDtypeStruct
    outs = [full, one, full, wide, wide] + ([full] if last else [full, full, one, full])
    shapes = [shape((t, d), f32), shape((t, 1), f32), shape((t, d), bf16), shape((t, f), f32), shape((t, f), bf16)]
    shapes += [shape((t, d), bf16)] if last else [
        shape((t, d), f32), shape((t, d), f32), shape((t, 1), f32), shape((t, d), bf16)
    ]
    return pl.pallas_call(
        functools.partial(block_forward_kernel, last=last),
        grid=(f // block,),
        in_specs=[
            full, full, spec((d, d), lambda i: (0, 0)), vec, vec, vec,
            spec((d, block), lambda i: (0, i)), spec((1, block), lambda i: (0, i)),
            spec((block, d), lambda i: (i, 0)), vec, vec, vec, vec,
        ],
        out_specs=outs,
        out_shape=shapes,
        scratch_shapes=[pltpu.VMEM((t, d), f32)],
        compiler_params=pltpu.CompilerParams(vmem_limit_bytes=40 * MIB),
        cost_estimate=cost(12),
        name="block_forward",
    )(
        inputs, attended, w_out, row(out_bias), row(ln2_gain), row(ln2_bias), w_up, row(up_bias), w_down,
        row(down_bias), row(lead), row(ln1_gain), row(ln1_bias),
    )


def put_sums(ref, *sums):
    for i, v in enumerate(sums):
        ref[i : i + 1, :] = v


def column_sum(x):
    return jnp.sum(x.astype(f32), axis=0, keepdims=True)


def block_backward_kernel(c_ref, grad_ref, h_ref, wd_ref, wu_ref, wo_ref, n_ref, r_ref, g_ref, *rest, grads, bands):
    if grads:
        l1_ref, x1_ref, x0_ref = rest[:3]
        z_other, x_other, z_own, x_own = rest[9:13]
        sums, rest = rest[14], rest[3:9] + rest[13:14]
    hg_ref, hsum_ref, middle_ref, branch_ref, sent_ref, sums_ref, total = rest
    step = pl.program_id(0)
    down = grad_ref[...].astype(bf16)
    low = (gelu_slope(h_ref[...]) * contract(down, wd_ref[...], 1, 1)).astype(bf16)
    hg_ref[...] = low
    hsum_ref[...] = column_sum(low)
    part = contract(low, wu_ref[...], 1, 1)
    if grads:
        sums[...] = contract(l1_ref[...], x1_ref[...], 0, 0) + contract(low, x0_ref[...], 0, 0)
        pairs = z_own.shape[0]
        n = sums.shape[0] // (2 * pairs)
        for q in range(pairs):
            for z, x, core in ((z_other, x_other, 1 - c_ref[0]), (z_own, x_own, c_ref[0])):
                start = pl.multiple_of((2 * q + core) * n, n)
                z[q] = sums[pl.ds(start, n // 2), :].astype(bf16)
                x[q] = sums[pl.ds(start + n // 2, n // 2), :].astype(bf16)

    @pl.when(step == 0)
    def _():
        total[...] = part

    @pl.when(step > 0)
    def _():
        total[...] += part

    @pl.when(step == pl.num_programs(0) - 1)
    def _():
        dv, gain, bias = norm_back(total[...], n_ref[...], r_ref[...], g_ref[...])
        middle = grad_ref[...] + dv
        middle_ref[...] = middle
        branch = middle.astype(bf16)
        branch_ref[...] = branch
        put_sums(sums_ref, gain, bias, column_sum(branch), column_sum(down))
        w = sent_ref.shape[2]
        attended = contract(branch, wo_ref[...], 1, 1).astype(bf16)
        for m in range(sent_ref.shape[0]):
            sent_ref[m] = attended[:, m * w : (m + 1) * w]


def block_backward(core, grad, hidden, w_down, w_up, w_out, n2, r2, gain, members, grads=()):
    t, d = grad.shape
    f = hidden.shape[1]
    block = 512
    bands = 2 * members
    full = spec((t, d), lambda i, c: (0, 0))
    wide = spec((t, block), lambda i, c: (0, i))
    sent = (members, t, d // members)
    shape = jax.ShapeDtypeStruct
    outs = [
        wide, spec((1, block), lambda i, c: (0, i)), full, full,
        spec(sent, lambda i, c: (0, 0, 0)), spec((8, d), lambda i, c: (0, 0)),
    ]
    shapes = [
        shape((t, f), bf16), shape((1, f), f32), shape((t, d), f32), shape((t, d), bf16),
        shape(sent, bf16), shape((8, d), f32),
    ]
    scratch = [pltpu.VMEM((t, d), f32)]
    if grads:
        n = f // bands
        pairs = block // (2 * n)
        part = spec((pairs, n // 2, d), lambda i, c: (i, 0, 0))
        outs += [part] * 4
        shapes += [shape((bands // 2, n // 2, d), bf16), shape((bands // 2, n // 2 + d // bands, d), bf16)] * 2
        scratch += [pltpu.VMEM((block, d), f32)]
    return pl.pallas_call(
        functools.partial(block_backward_kernel, grads=bool(grads), bands=bands),
        grid_spec=pltpu.PrefetchScalarGridSpec(
            num_scalar_prefetch=1,
            grid=(f // block,),
            in_specs=[
                full, wide, spec((block, d), lambda i, c: (i, 0)), spec((d, block), lambda i, c: (0, i)),
                spec((d, d), lambda i, c: (0, 0)), full, spec((t, 1), lambda i, c: (0, 0)),
                spec((1, d), lambda i, c: (0, 0)),
            ] + [wide, full, full][: len(grads)],
            out_specs=outs,
            scratch_shapes=scratch,
        ),
        out_shape=shapes,
        compiler_params=pltpu.CompilerParams(vmem_limit_bytes=(60 if grads else 48) * MIB),
        cost_estimate=cost(18 if grads else 14),
        name="block_backward",
    )(core.reshape(1), grad, hidden, w_down, w_up, w_out, n2, r2, gain.reshape(1, d), *grads)


def grad_out_kernel(c_ref, l1, l0, r1, r0, _, __, other_ref, own_ref, sums, *, pairs):
    sums[...] = contract(l1[...], r1[...], 0, 0) + contract(l0[...], r0[...], 0, 0)
    n = own_ref.shape[1]
    for q in range(pairs):
        for ref, core in ((other_ref, 1 - c_ref[0]), (own_ref, c_ref[0])):
            ref[q] = sums[pl.ds(pl.multiple_of((2 * q + core) * n, n), n), :].astype(bf16)


def grad_out(core, left, right, bands, other, own):
    tokens, m = left[0].shape
    count, height, d = own.shape
    n = m // bands
    pairs = max(1, 256 // (2 * n))
    columns = spec((tokens, 2 * n * pairs), lambda j, c: (0, j))
    whole = spec((tokens, d), lambda j, c: (0, 0))
    out = spec((pairs, n, d), lambda j, c: (j, height // n - 1, 0))
    anywhere = pl.BlockSpec(memory_space=pl.ANY)
    return pl.pallas_call(
        functools.partial(grad_out_kernel, pairs=pairs),
        grid_spec=pltpu.PrefetchScalarGridSpec(
            num_scalar_prefetch=1,
            grid=(count // pairs,),
            in_specs=[columns, columns, whole, whole, anywhere, anywhere],
            out_specs=[out, out],
            scratch_shapes=[pltpu.VMEM((2 * n * pairs, d), f32)],
        ),
        out_shape=[jax.ShapeDtypeStruct(own.shape, bf16)] * 2,
        input_output_aliases={5: 0, 6: 1},
        compiler_params=pltpu.CompilerParams(vmem_limit_bytes=60 * MIB),
        cost_estimate=cost(3),
        name="grad_out",
    )(core.reshape(1), *left, *right, other, own)


def qkv_backward_kernel(b_ref, wq_ref, wk_ref, wv_ref, m_ref, n_ref, r_ref, g_ref, *rest):
    grad_ref, low_ref, sums_ref, qv_ref, total = rest[-5:]
    added = rest[:-5]
    step = pl.program_id(0)
    w = b_ref.shape[3]
    part = None
    for m in range(b_ref.shape[0]):
        for i, ref in enumerate((wq_ref, wk_ref, wv_ref)):
            x = contract(b_ref[m, i], ref[:, m * w : (m + 1) * w], 1, 1)
            part = x if part is None else part + x
        for row, i in ((0, 0), (1, 2)):
            here = column_sum(b_ref[m, i])
            if added:
                here = here + added[1][row : row + 1, m * w : (m + 1) * w]
            qv_ref[row : row + 1, m * w : (m + 1) * w] = here

    @pl.when(step == 0)
    def _():
        total[...] = part

    @pl.when(step > 0)
    def _():
        total[...] += part

    @pl.when(step == pl.num_programs(0) - 1)
    def _():
        dv, gain, bias = norm_back(total[...], n_ref[...], r_ref[...], g_ref[...])
        grad = m_ref[...] + dv
        grad_ref[...] = grad
        low_ref[...] = grad[grad.shape[0] - low_ref.shape[0] :].astype(bf16)
        sums = (gain, bias, column_sum(grad))
        if added:
            sums = [v + added[0][i : i + 1, :] for i, v in enumerate(sums)]
        put_sums(sums_ref, *sums)


def qkv_backward(back, w_qkv, middle_grad, n1, r1, gain, low, added=()):
    members, _, t, w = back.shape
    d = members * w
    at_once = max(2, 128 // w)
    block = at_once * w
    shift = d // block
    full = spec((t, d), lambda i: (0, 0))
    weight = [spec((d, block), lambda i, s=s: (0, s * shift + i)) for s in range(3)]
    shape = jax.ShapeDtypeStruct
    return pl.pallas_call(
        qkv_backward_kernel,
        grid=(members // at_once,),
        in_specs=[spec((at_once, 3, t, w), lambda i: (i, 0, 0, 0))] + weight + [
            full, full, spec((t, 1), lambda i: (0, 0)), spec((1, d), lambda i: (0, 0)),
        ] + [spec((8, d), lambda i: (0, 0)), spec((8, block), lambda i: (0, i))][: len(added)],
        out_specs=[
            full, spec((low, d), lambda i: (0, 0)), spec((8, d), lambda i: (0, 0)),
            spec((8, block), lambda i: (0, i)),
        ],
        out_shape=[
            shape((t, d), f32), shape((low, d), bf16), shape((8, d), f32), shape((8, d), f32),
        ],
        scratch_shapes=[pltpu.VMEM((t, d), f32)],
        compiler_params=pltpu.CompilerParams(vmem_limit_bytes=60 * MIB),
        cost_estimate=cost(12),
        name="qkv_backward",
    )(back, w_qkv, w_qkv, w_qkv, middle_grad, n1, r1, gain.reshape(1, d), *added)


def grad_heads_kernel(d_ref, n_ref, *rest):
    out_ref = rest[-1]
    rows = d_ref.shape[2]
    for i in range(3):
        total = rest[0][i] if len(rest) == 2 else jnp.zeros(out_ref.shape[1:], f32)
        for m in range(d_ref.shape[0]):
            total += contract(d_ref[m, i], n_ref[m * rows : (m + 1) * rows, :], 0, 0)
        out_ref[i] = total.astype(out_ref.dtype)


def grad_heads(d, normed_all, add, kind):
    members, _, rows, width = d.shape
    dim = normed_all.shape[1]
    shape = (3, width, dim)
    out = spec((3, width, dim // 4), lambda i: (0, 0, i))
    extra = [] if add is None else [add]
    return pl.pallas_call(
        grad_heads_kernel,
        grid=(4,),
        in_specs=[
            spec(d.shape, lambda i: (0, 0, 0, 0)),
            spec((members * rows, dim // 4), lambda i: (0, i)),
        ]
        + [out] * len(extra),
        out_specs=out,
        out_shape=jax.ShapeDtypeStruct(shape, kind),
        compiler_params=pltpu.CompilerParams(vmem_limit_bytes=60 * MIB),
        cost_estimate=cost(5),
        name="grad_heads",
    )(d, normed_all, *extra)


def take_kernel(table, *refs):
    for i in range(refs[-1].shape[0]):
        total = refs[0][table[i]].astype(f32)
        for r in refs[1:-1]:
            total = total + r[table[i]].astype(f32)
        refs[-1][i] = total.astype(bf16)


def take(terms, table):
    shape = terms[0].shape
    count = table.shape[0]
    return pl.pallas_call(
        take_kernel,
        grid_spec=pltpu.PrefetchScalarGridSpec(
            num_scalar_prefetch=1,
            grid=(1,),
            in_specs=[spec(shape, lambda i, t: (0, 0, 0))] * len(terms),
            out_specs=spec((count,) + shape[1:], lambda i, t: (0, 0, 0)),
        ),
        out_shape=jax.ShapeDtypeStruct((count,) + shape[1:], bf16),
        compiler_params=pltpu.CompilerParams(vmem_limit_bytes=60 * MIB),
        cost_estimate=cost(3),
        name="take",
    )(table, *terms)


def join_kernel(i_ref, own_ref, other_ref, out_ref):
    half = other_ref.shape[0]
    out_ref[i_ref[0]] = own_ref[:half]
    out_ref[1 - i_ref[0]] = other_ref[...].astype(f32)


def join(index, own, other):
    half, d = other.shape
    full = spec((half, d), lambda i, c: (0, 0))
    return pl.pallas_call(
        join_kernel,
        grid_spec=pltpu.PrefetchScalarGridSpec(
            num_scalar_prefetch=1,
            grid=(1,),
            in_specs=[full, full],
            out_specs=spec((2, half, d), lambda i, c: (0, 0, 0)),
        ),
        out_shape=jax.ShapeDtypeStruct((2, half, d), f32),
        compiler_params=pltpu.CompilerParams(vmem_limit_bytes=8 * MIB),
        cost_estimate=cost(2),
        name="join",
    )(index.reshape(1), own, other)


def unit_tables(bands, x_count, width, dim):
    members = bands // 2
    unit = math.gcd(HD, 3 * dim // bands)
    per_band = 3 * dim // bands // unit
    made, slots, place = [], [], {}
    for g in range(members):
        units = [(b * dim + g * width) // unit + i for b in range(3) for i in range(width // unit)]
        by_low = [[] for _ in range(members)]
        for local, u in enumerate(units):
            band = u // per_band
            core, x, zl = band % 2, band // 2 % x_count, band // (2 * x_count) % 2
            low = (core * 2 + zl) * x_count + x
            place[u] = (g, len(by_low[low]))
            by_low[low].append(local)
        made.append(by_low)
    most = max(len(l) for by_low in made for l in by_low)
    send = np.zeros((members, members * most), np.int32)
    for g, by_low in enumerate(made):
        for low, locals_ in enumerate(by_low):
            for m, local in enumerate(locals_):
                send[g, low * most + m] = local
    keep = np.zeros((members, 2, per_band), np.int32)
    for u, (g, m) in place.items():
        band = u // per_band
        core, x, zl = band % 2, band // 2 % x_count, band // (2 * x_count) % 2
        low = (core * 2 + zl) * x_count + x
        keep[low, band // members, u % per_band] = g * most + m
    return unit, send, keep


def norm_parts(v):
    centred = v - jnp.mean(v, axis=-1, keepdims=True)
    r = lax.rsqrt(jnp.mean(centred * centred, axis=-1, keepdims=True) + EPS)
    return centred * r, r


def norm_back(dy, n, r, gain):
    dyg = dy * gain
    mean_one = jnp.mean(dyg, axis=-1, keepdims=True)
    mean_two = jnp.mean(dyg * n, axis=-1, keepdims=True)
    dv = r * (dyg - mean_one - n * mean_two)
    return dv, jnp.sum(dy * n, axis=0, keepdims=True), jnp.sum(dy, axis=0, keepdims=True)


def gelu(x):
    return 0.5 * x * (1.0 + jnp.tanh(GELU_A * (x + GELU_B * x * x * x)))


def gelu_slope(x):
    t = jnp.tanh(GELU_A * (x + GELU_B * x * x * x))
    return 0.5 * (1.0 + t) + 0.5 * x * (1.0 - t * t) * (GELU_A * (1.0 + 3.0 * GELU_B * x * x))


def dot(a, b):
    return jnp.dot(a, b, preferred_element_type=f32)


def dot_t(a, b):
    return contract(a, b, 1, 1)


def swap(x, axis):
    return lax.ppermute(x, axis, SWAP)


def pin(x, *first):
    return lax.optimization_barrier((x,) + first)[0]


def total(terms):
    out = terms[0].astype(f32)
    for t in terms[1:]:
        out = out + t.astype(f32)
    return out


class Share:
    def __init__(self, terms, names):
        self.terms = list(terms)
        self.names = list(names)

    def halve(self, axis, *first):
        if axis not in self.names:
            return self.terms[-1]
        dim = self.names.index(axis)
        i = lax.axis_index(axis)
        terms = [pin(t, *first) if first else t for t in self.terms[-1:]] + self.terms[:-1]
        there = [lax.dynamic_index_in_dim(t, 1 - i, dim, keepdims=False) for t in terms]
        self.terms = [lax.dynamic_index_in_dim(t, i, dim, keepdims=False) for t in terms]
        self.names.remove(axis)
        sent = total(there).astype(bf16)
        self.terms.append(swap(sent, axis))
        return sent


def body(
    fields,
    lead_bucket,
    cotangent,
    lead_table,
    ln1_gain,
    ln1_bias,
    w_qkv,
    q_bias,
    v_bias,
    w_out,
    out_bias,
    ln2_gain,
    ln2_bias,
    w_up,
    up_bias,
    w_down,
    down_bias,
    *,
    axes,
    x_axes,
    samp_count,
):
    band = tuple(axes)
    low = ("core", "zl") + x_axes[::-1]
    members = 2 ** len(low)
    order = x_axes + ("zl", "core")
    D = w_out.shape[0]
    W = D // members
    half = fields.shape[1]
    rows = 2 * half
    two = samp_count == 2
    zh = lax.axis_index("zh")
    me = lax.axis_index(low)

    def pick(x, i):
        return lax.dynamic_index_in_dim(x, i, 0, keepdims=False)

    def to_sample(x):
        return jnp.concatenate([pick(x, zh), swap(pick(x, 1 - zh), "zh")])

    def to_band(x):
        own = x[:half]
        other = swap(x[half:].astype(bf16), "zh").astype(x.dtype)
        return jnp.where(zh == 0, jnp.stack([own, other]), jnp.stack([other, own]))

    def gather(x):
        if len(x_axes) == 1:
            x_axis = x_axes[0]
            cut = x.shape[0] // 2
            by_x = swap(x, x_axis)
            by_z = swap(x, "zl")
            far = [swap(by_x[:cut], "zl"), swap(by_z[cut:], x_axis)]
            pieces = [(x, 0, 0), (by_x, 1, 0), (by_z, 2, 0), (far[0], 3, 0), (far[1], 3, cut)]
            pieces += [(swap(p, "core"), 4 + k, o) for p, k, o in pieces]
        else:
            pieces = [(x, 0, 0)]
            for bit, axis in enumerate(order):
                pieces += [(swap(p, axis), k + 2**bit, 0) for p, k, _ in pieces]
        out = jnp.zeros((members * rows, D), bf16)
        for piece, k, offset in pieces:
            out = lax.dynamic_update_slice(out, piece, ((me ^ k) * rows + offset, 0))
        return out

    lead_row = pick(lead_table, pick(lead_bucket, zh)).astype(f32)
    carried = to_sample(fields).astype(f32)

    def member_columns(x, block):
        return lax.dynamic_slice_in_dim(x, block * D + me * W, W, x.ndim - 1)

    kept = []
    inputs = carried + lead_row
    n1, r1 = norm_parts(inputs)
    normed = (n1 * ln1_gain + ln1_bias).astype(bf16)
    weights = (w_out, out_bias, ln2_gain, ln2_bias, w_up, up_bias, w_down, down_bias, lead_row, ln1_gain, ln1_bias)
    for index in range(STEPS):
        normed_all = gather(normed)
        queries = (dot(normed, w_qkv[:, :D]) + q_bias).astype(bf16)
        if index == 0:
            out_grad = to_sample(pin(cotangent, normed_all))
        attended = attend(queries, normed_all, w_qkv, v_bias)
        if index == 0:
            attended, out_grad = pin((attended, out_grad))
        last = index == STEPS - 1
        n2, r2, normed_two, hidden, activated, *after = block_forward(inputs, attended, weights, last)
        kept.append((n1, r1, normed_all, attended, n2, r2, normed_two, hidden, activated))
        if not last:
            inputs, n1, r1, normed = after
    carried = after[0]
    result = to_band(carried)

    grad = out_grad
    small = None
    added = ()
    core = lax.axis_index("core")
    y = lax.axis_index("samp")
    bands = 2 ** len(axes)
    names = axes[:-1]
    cube = (2,) * len(names)
    later = None
    w_heads = None
    unit, send_table, keep_table = unit_tables(bands, 2 ** len(x_axes), W, D)
    send_row, keep_row = pick(jnp.asarray(send_table), me), pick(jnp.asarray(keep_table), me)
    keep_rows = pick(keep_row, zh), pick(keep_row, 1 - zh)
    def split_rows(x, rows_two):
        n, r, c = x.shape
        return x.reshape(cube + ((2, r // 2) if rows_two else (r,)) + (c,))

    own_weight = jnp.concatenate([member_columns(w_qkv, i) for i in range(3)], axis=1)
    own_bias = jnp.concatenate([member_columns(q_bias, 0), jnp.zeros((W,), f32), member_columns(v_bias, 0)])

    def own_part(index):
        own = (dot(kept[index][2], own_weight) + own_bias).astype(bf16)
        return own[:, :W], own[:, W : 2 * W], own[:, 2 * W :]

    owns = {}
    for index in reversed(range(STEPS)):
        n1, r1, normed_all, attended, n2, r2, normed_two, hidden, activated = kept[index]
        last = index == 0
        if last:
            grads = (later[2], later[3], normed_two)
        else:
            down_grad = grad.astype(bf16)
            grads = ()
        hidden_grad, hidden_sum, middle_grad, branch_grad, sent, sums_two, *ups = block_backward(
            core, grad, hidden, w_down, w_up, w_out, n2, r2, ln2_gain, members, grads
        )
        own_grad = lax.all_to_all(sent, low, 0, 0, tiled=True).reshape(members * rows, W)
        if last:
            z_other, x_other, z_own, x_own = ups
            z_core = swap(z_other, "core")
            left, right = (later[0], pin(down_grad, sent)), (later[1], activated)
            d_other, d_own = grad_rows(core, left, right, bands, 0, 1)
            d_core = swap(d_other, "core")
            x_other, x_own = grad_out(
                core, (later[4], pin(branch_grad, d_other)), (later[5], attended), bands, x_other, x_own
            )
            x_core = swap(x_other, "core")
            samp = ("samp",) * two
            d_terms = pin((d_own, d_core), x_other)
            down_share = Share([split_rows(t, two) for t in d_terms], names + samp)
            z_terms = pin((z_own, z_core), down_share.halve("samp"))
            z_share = Share([split_rows(t, two) for t in z_terms], names + samp)
            x_terms = pin((x_own, x_core), z_share.halve("zl"))
            x_share = Share([split_rows(t, two) for t in x_terms], names + samp)
            own_grad = pin(own_grad, x_share.halve(x_axes[0]))
            heads = W // HD
            d_heads = attend_back(*owns[0], own_grad, members, range((heads + 1) // 2))
            own_grad, d_heads, z_share.terms[-1] = pin((own_grad, d_heads, z_share.terms[-1]))
            sent = z_share.halve("zh")
            if heads > 1:
                own_grad, d_heads = pin((own_grad, d_heads), sent)
                d_heads = attend_back(*owns[0], own_grad, members, range(heads // 2, heads), d_heads)
            shares = (z_share, x_share, down_share)
            waits = pin((d_heads, *(t.terms[-1] for t in shares)))
            d_heads = waits[0]
            for t, value in zip(shares, waits[1:]):
                t.terms[-1] = value
            sent = [x_share.halve("samp"), z_share.halve("samp")] + [down_share.halve(a) for a in x_axes]
            d_heads = pin(d_heads, *sent)
        else:
            own_grad, send_row, keep_rows = pin((own_grad, send_row, keep_rows), result)
            later = (down_grad, activated, hidden_grad, normed_two, branch_grad, attended)
            owns[index] = own_part(index)
            d_heads = attend_back(*owns[index], own_grad, members)
        back = lax.all_to_all(d_heads, low, 0, 0, tiled=True)
        w_heads = grad_heads(d_heads, normed_all, w_heads, bf16 if last else f32)
        if last:
            units = w_heads.reshape(-1, unit, D)
            if two:
                there = lax.dynamic_slice_in_dim(units, (1 - y) * (D // 2), D // 2, 2)
                here = lax.dynamic_slice_in_dim(units, y * (D // 2), D // 2, 2)
                units = [here, swap(there, "samp")]
            else:
                there, units = units, [units]
            back = pin(back, there)
            x_share.terms[-1], z_share.terms[-1] = pin((x_share.terms[-1], z_share.terms[-1]), back)
            sent = [x_share.halve(a) for a in x_axes[1:] + ("zl",)] + [z_share.halve(a) for a in x_axes]
            units[-1] = pin(units[-1], *sent)
            outgoing = take(units, send_row)
            incoming = lax.all_to_all(outgoing, low, 0, 0, tiled=True)
            down_share.terms[-1] = pin(down_share.terms[-1], outgoing)
            back = pin(back, down_share.halve("zl"))
        else:
            owns[0] = own_part(0)
            back = pin(back, w_heads, *owns[0])
        grad, low_grad, sums_one, sums_qv = qkv_backward(
            back, w_qkv, middle_grad, n1, r1, ln1_gain, half if last else rows, added
        )
        added = (sums_one, sums_qv)
        down_grad = low_grad
        step_small = (sums_two[:4], hidden_sum)
        small = step_small if small is None else tuple(a + b for a, b in zip(small, step_small))
    small = (sums_one[:3], sums_qv[:2]) + small
    fields_sent = low_grad
    fields_other = swap(fields_sent, "zh")
    x_share.terms[-1] = pin(x_share.terms[-1], fields_sent)
    incoming = pin(incoming, x_share.halve("zh"))
    there = take([incoming], keep_rows[1])
    other = swap(there, "zh")
    one, qv, two_sums, up_sum = pin(small, there)
    samples = 2 * samp_count
    slot = 2 * y + zh
    mine = lax.broadcasted_iota(jnp.int32, (samples, 1), 0) == slot
    leads = jnp.where(mine, one[2:3], 0.0)
    lane = lax.broadcasted_iota(jnp.int32, (bands, D // bands), 1) == slot
    bucket = jnp.where(lane & (me == 0), pick(lead_bucket, zh).astype(f32), 0.0)
    vectors = jnp.concatenate([one[:2], qv, two_sums, leads])
    vectors = vectors.reshape(-1, bands, D // bands).transpose(1, 0, 2).reshape(bands, -1)
    vectors = jnp.concatenate([vectors, up_sum.reshape(bands, -1), bucket], axis=1)
    sums = vectors
    vectors = lax.all_to_all(vectors, band, 0, 0, tiled=True)

    def both(x):
        x = x.astype(bf16)
        if not two:
            return lax.psum(x, "samp").astype(f32)
        other = swap(x, "samp")
        return jnp.concatenate([jnp.where(y == 0, x, other), jnp.where(y == 0, other, x)]).astype(f32)

    def both_cut(x, n):
        if not two:
            x = both(x)
            return x[:n], x[n:]
        x = x.astype(bf16)
        other = swap(x, "samp")
        first, second = jnp.where(y == 0, x, other), jnp.where(y == 0, other, x)
        x = jnp.concatenate([first, second]).astype(f32)
        return x[:n], x[n:]

    incoming, down_share.terms[-1], z_share.terms[-1] = pin((incoming, down_share.terms[-1], z_share.terms[-1]), sums)
    sent = down_share.halve("zh")
    own = take([incoming], keep_rows[0])
    up_first = total(z_share.terms).astype(bf16)
    late = (vectors, fields_other, other, down_share.terms[-1], x_share.terms[-1])
    late = pin(late, sent, own, up_first)
    vectors, fields_other, other, down_share.terms[-1], x_share.terms[-1] = late
    vectors = jnp.sum(vectors, axis=0)
    vectors = vectors + swap(vectors, "samp") if two else lax.psum(vectors, "samp")
    own = total([own, other]).astype(bf16).reshape(3 * D // bands, -1)
    if two:
        other = swap(own, "samp")
        own = jnp.concatenate([jnp.where(y == 0, own, other), jnp.where(y == 0, other, own)], axis=1)
    else:
        own = lax.psum(own, "samp")
    w_qkv_grad = own.astype(f32).T

    w_down_grad = both(total(down_share.terms)).T
    n_up = w_up.shape[1] // bands
    bottom = both_cut(total(x_share.terms), n_up // 2)
    w_out_grad = bottom[1].T
    w_up_grad = jnp.concatenate([both(up_first), bottom[0]]).T
    fields_grad = join(zh, grad, fields_other)

    w = D // bands
    leads = vectors[8 * w : (8 + samples) * w].reshape(samples, w)
    up_grad = vectors[(8 + samples) * w : -w]
    buckets = vectors[-w:][:samples].astype(jnp.int32)
    one_hot = (buckets[:, None] == jnp.arange(lead_table.shape[0], dtype=jnp.int32)[None, :]).astype(f32)
    lead_grad = jnp.dot(one_hot.T, leads, precision=lax.Precision.HIGHEST)
    rows_of = lambda i: vectors[i * w : (i + 1) * w]
    g = [rows_of(i) for i in (0, 1, 2, 3, 6, 4, 5)] + [up_grad, rows_of(7)]
    return (
        result,
        fields_grad,
        lead_grad,
        g[0],
        g[1],
        w_qkv_grad,
        g[2],
        g[3],
        w_out_grad,
        g[4],
        g[5],
        g[6],
        w_up_grad,
        g[7],
        w_down_grad,
        g[8],
    )


def solution(mesh):
    samp_count, band_count = mesh.shape["samp"], mesh.shape["band"]
    x_axes = tuple(f"x{i}" for i in range((band_count // 8).bit_length() - 1))
    axes = ("zh", "zl") + x_axes + ("core",)
    assert 2 ** len(axes) == band_count
    fine = Mesh(mesh.devices.reshape((samp_count,) + (2,) * len(axes)), ("samp",) + axes)
    tokens = P("samp", axes, None)
    columns, vector = P(None, axes), P(axes)
    in_specs = (tokens, P("samp"), tokens) + (P(),) * 14
    out_specs = (
        tokens,
        tokens,
        columns,
        vector,
        vector,
        columns,
        vector,
        vector,
        columns,
        vector,
        vector,
        vector,
        columns,
        vector,
        columns,
        vector,
    )
    run = functools.partial(body, axes=axes, x_axes=x_axes, samp_count=samp_count)
    return jax.shard_map(run, mesh=fine, in_specs=in_specs, out_specs=out_specs, check_vma=False)
```

```python
import functools
import math

import jax
import jax.numpy as jnp
import numpy as np
from jax import lax
from jax.experimental import pallas as pl
from jax.experimental.pallas import tpu as pltpu
from jax.sharding import Mesh
from jax.sharding import PartitionSpec as P

HD = 64
STEPS = 2
EPS = 1e-05
EXP_SCALE = 0.125 * 1.4426950408889634
GELU_A = 0.7978845608028654
GELU_B = 0.044715
MIB = 2**20
SWAP = [(0, 1), (1, 0)]
f32 = jnp.float32
bf16 = jnp.bfloat16


def cost(us):
    return pl.CostEstimate(flops=int(us * 1.15e9), bytes_accessed=1000, transcendentals=0)


def contract(a, b, a_dim, b_dim):
    return lax.dot_general(a, b, (((a_dim,), (b_dim,)), ((), ())), preferred_element_type=f32)


def head_part(x, h, heads):
    if heads == 1:
        return x
    lane = lax.broadcasted_iota(jnp.int32, x.shape, 1)
    return jnp.where(lane // HD == h, x, jnp.zeros_like(x))


def attend_kernel(q_ref, n_ref, wk_ref, wv_ref, b_ref, o_ref):
    normed = n_ref[...]
    keys = contract(normed, wk_ref[...], 1, 0).astype(bf16)
    values = (contract(normed, wv_ref[...], 1, 0) + b_ref[...]).astype(bf16)
    pair = 2 * HD
    for start in range(0, q_ref.shape[1], pair):
        q, k, v = q_ref[:, start : start + pair], keys[:, start : start + pair], values[:, start : start + pair]
        out = None
        for h in range(2):
            s = contract(head_part(q, h, 2), k, 1, 1)
            top = jnp.max(s, axis=-1, keepdims=True)
            e = jnp.exp2((s - top) * EXP_SCALE)
            total = jnp.sum(e, axis=-1, keepdims=True)
            o = head_part(contract(e.astype(bf16), v, 1, 0) / total, h, 2)
            out = o if out is None else out + o
        o_ref[:, start : start + pair] = out.astype(bf16)


def attend(q, normed_all, w_qkv, v_bias):
    rows, width = q.shape
    count = normed_all.shape[0]
    block = 4 * HD
    own = spec((rows, block), lambda j: (0, j))
    shift = width // block
    return pl.pallas_call(
        attend_kernel,
        grid=(width // block,),
        in_specs=[
            own,
            spec((count, width), lambda j: (0, 0)),
            spec((width, block), lambda j: (0, shift + j)),
            spec((width, block), lambda j: (0, 2 * shift + j)),
            spec((1, block), lambda j: (0, j)),
        ],
        out_specs=own,
        out_shape=jax.ShapeDtypeStruct((rows, width), bf16),
        compiler_params=pltpu.CompilerParams(vmem_limit_bytes=40 * MIB),
        cost_estimate=cost(24),
        name="attend",
    )(q, normed_all, w_qkv, w_qkv, v_bias.reshape(1, width))


def attend_back_kernel(q_ref, k_ref, v_ref, do_ref, *rest, heads, some):
    out_ref, dk_sum, dv_sum = rest[-3:]
    step = pl.program_id(0)
    rows = q_ref.shape[0]

    @pl.when(step == 0)
    def _():
        dk_sum[...] = jnp.zeros_like(dk_sum)
        dv_sum[...] = jnp.zeros_like(dv_sum)

    q, k, v, do = q_ref[...], k_ref[...], v_ref[...], do_ref[...]
    queries = [head_part(q, h, heads) for h in some]
    grads = [head_part(do, h, heads) for h in some]
    scores = [contract(x, k, 1, 1) for x in queries]
    prob_grads = [contract(x, v, 1, 1) for x in grads]
    dq = dk = dv = 0.0
    for h, qh, doh, s, dp in zip(some, queries, grads, scores, prob_grads):
        top = jnp.max(s, axis=-1, keepdims=True)
        e = jnp.exp2((s - top) * EXP_SCALE)
        inverse = 1.0 / jnp.sum(e, axis=-1, keepdims=True)
        inner = jnp.sum(e * dp, axis=-1, keepdims=True) * inverse
        p = e * inverse
        ds = (p * (dp - inner)).astype(bf16)
        dq = dq + head_part(contract(ds, k, 1, 0), h, heads)
        dk = dk + contract(ds, qh, 0, 0)
        dv = dv + contract(p.astype(bf16), doh, 0, 0)
    dk_sum[...] += dk
    dv_sum[...] += dv

    def put(m, i, x):
        if len(rest) == 4:
            x = x + rest[0][m, i].astype(f32)
        out_ref[m, i] = x.astype(bf16)

    put(step, 0, dq * 0.125)

    @pl.when(step == pl.num_programs(0) - 1)
    def _():
        for m in range(out_ref.shape[0]):
            put(m, 1, dk_sum[m * rows : (m + 1) * rows, :] * 0.125)
            put(m, 2, dv_sum[m * rows : (m + 1) * rows, :])


def attend_back(q, k, v, do, members, some=None, add=None):
    count, width = q.shape
    rows = count // members
    heads = width // HD
    part = pl.BlockSpec((rows, width), lambda i: (i, 0))
    full = pl.BlockSpec((count, width), lambda i: (0, 0))
    shape = (members, 3, rows, width)
    out = pl.BlockSpec(shape, lambda i: (0, 0, 0, 0))
    extra = [] if add is None else [add]
    return pl.pallas_call(
        functools.partial(attend_back_kernel, heads=heads, some=some or range(heads)),
        grid=(members,),
        in_specs=[part, full, full, part] + [out] * len(extra),
        out_specs=out,
        out_shape=jax.ShapeDtypeStruct(shape, bf16),
        scratch_shapes=[pltpu.VMEM((count, width), f32), pltpu.VMEM((count, width), f32)],
        compiler_params=pltpu.CompilerParams(vmem_limit_bytes=60 * MIB),
        cost_estimate=cost(33 if some is None else 17),
        name="attend_back",
    )(q, k, v, do, *extra)


def spec(block, index):
    return pl.BlockSpec(block, index)


def grad_rows_kernel(c_ref, l1, l0, r1, r0, other_ref, own_ref, sums):
    sums[...] = contract(l1[...], r1[...], 0, 0) + contract(l0[...], r0[...], 0, 0)
    count, n, _ = own_ref.shape
    for j in range(count):
        for ref, core in ((other_ref, 1 - c_ref[0]), (own_ref, c_ref[0])):
            ref[j] = sums[pl.ds(pl.multiple_of((2 * j + core) * n, n), n), :].astype(bf16)


def grad_rows(core, left, right, bands, part, parts):
    tokens, m = left[0].shape
    n = right[0].shape[1] // parts
    block = min(n, 512)
    first = part * (n // block)
    out = spec((bands // 2, m // bands, block), lambda j, c: (0, 0, j))
    whole = spec((tokens, m), lambda j, c: (0, 0))
    part = spec((tokens, block), lambda j, c: (0, first + j))
    return pl.pallas_call(
        grad_rows_kernel,
        grid_spec=pltpu.PrefetchScalarGridSpec(
            num_scalar_prefetch=1,
            grid=(n // block,),
            in_specs=[whole, whole, part, part],
            out_specs=[out, out],
            scratch_shapes=[pltpu.VMEM((m, block), f32)],
        ),
        out_shape=[jax.ShapeDtypeStruct((bands // 2, m // bands, n), bf16)] * 2,
        compiler_params=pltpu.CompilerParams(vmem_limit_bytes=60 * MIB),
        cost_estimate=cost(8),
        name="grad_rows",
    )(core.reshape(1), *left, *right)


def block_forward_kernel(
    x_ref, a_ref, wo_ref, bo_ref, g_ref, b_ref, wu_ref, bu_ref, wd_ref, bd_ref, lead_ref, g1_ref, b1_ref,
    n2_ref, r2_ref, low2_ref, hidden_ref, act_ref, *rest, last
):
    total = rest[-1]
    step = pl.program_id(0)

    @pl.when(step == 0)
    def _():
        middle = x_ref[...] + contract(a_ref[...], wo_ref[...], 1, 0) + bo_ref[...]
        n, r = norm_parts(middle)
        n2_ref[...] = n
        r2_ref[...] = r
        low2_ref[...] = (n * g_ref[...] + b_ref[...]).astype(bf16)
        total[...] = middle + bd_ref[...]

    hidden = contract(low2_ref[...], wu_ref[...], 1, 0) + bu_ref[...]
    hidden_ref[...] = hidden
    act = gelu(hidden).astype(bf16)
    act_ref[...] = act
    total[...] += contract(act, wd_ref[...], 1, 0)

    @pl.when(step == pl.num_programs(0) - 1)
    def _():
        carried = total[...]
        if last:
            rest[0][...] = carried.astype(bf16)
        else:
            x = carried + lead_ref[...]
            n, r = norm_parts(x)
            rest[0][...] = x
            rest[1][...] = n
            rest[2][...] = r
            rest[3][...] = (n * g1_ref[...] + b1_ref[...]).astype(bf16)


def block_forward(inputs, attended, weights, last):
    w_out, out_bias, ln2_gain, ln2_bias, w_up, up_bias, w_down, down_bias, lead, ln1_gain, ln1_bias = weights
    t, d = inputs.shape
    f = w_up.shape[1]
    block = 512
    row = lambda v: v.reshape(1, -1)
    full = spec((t, d), lambda i: (0, 0))
    vec = spec((1, d), lambda i: (0, 0))
    one = spec((t, 1), lambda i: (0, 0))
    wide = spec((t, block), lambda i: (0, i))
    shape = jax.ShapeDtypeStruct
    outs = [full, one, full, wide, wide] + ([full] if last else [full, full, one, full])
    shapes = [shape((t, d), f32), shape((t, 1), f32), shape((t, d), bf16), shape((t, f), f32), shape((t, f), bf16)]
    shapes += [shape((t, d), bf16)] if last else [
        shape((t, d), f32), shape((t, d), f32), shape((t, 1), f32), shape((t, d), bf16)
    ]
    return pl.pallas_call(
        functools.partial(block_forward_kernel, last=last),
        grid=(f // block,),
        in_specs=[
            full, full, spec((d, d), lambda i: (0, 0)), vec, vec, vec,
            spec((d, block), lambda i: (0, i)), spec((1, block), lambda i: (0, i)),
            spec((block, d), lambda i: (i, 0)), vec, vec, vec, vec,
        ],
        out_specs=outs,
        out_shape=shapes,
        scratch_shapes=[pltpu.VMEM((t, d), f32)],
        compiler_params=pltpu.CompilerParams(vmem_limit_bytes=40 * MIB),
        cost_estimate=cost(12),
        name="block_forward",
    )(
        inputs, attended, w_out, row(out_bias), row(ln2_gain), row(ln2_bias), w_up, row(up_bias), w_down,
        row(down_bias), row(lead), row(ln1_gain), row(ln1_bias),
    )


def put_sums(ref, *sums):
    for i, v in enumerate(sums):
        ref[i : i + 1, :] = v


def column_sum(x):
    return jnp.sum(x.astype(f32), axis=0, keepdims=True)


def block_backward_kernel(c_ref, grad_ref, h_ref, wd_ref, wu_ref, wo_ref, n_ref, r_ref, g_ref, *rest, grads, bands):
    if grads:
        l1_ref, x1_ref, x0_ref = rest[:3]
        z_other, x_other, z_own, x_own = rest[9:13]
        sums, rest = rest[14], rest[3:9] + rest[13:14]
    hg_ref, hsum_ref, middle_ref, branch_ref, sent_ref, sums_ref, total = rest
    step = pl.program_id(0)
    down = grad_ref[...].astype(bf16)
    low = (gelu_slope(h_ref[...]) * contract(down, wd_ref[...], 1, 1)).astype(bf16)
    hg_ref[...] = low
    hsum_ref[...] = column_sum(low)
    part = contract(low, wu_ref[...], 1, 1)
    if grads:
        sums[...] = contract(l1_ref[...], x1_ref[...], 0, 0) + contract(low, x0_ref[...], 0, 0)
        pairs = z_own.shape[0]
        n = sums.shape[0] // (2 * pairs)
        for q in range(pairs):
            for z, x, core in ((z_other, x_other, 1 - c_ref[0]), (z_own, x_own, c_ref[0])):
                start = pl.multiple_of((2 * q + core) * n, n)
                z[q] = sums[pl.ds(start, n // 2), :].astype(bf16)
                x[q] = sums[pl.ds(start + n // 2, n // 2), :].astype(bf16)

    @pl.when(step == 0)
    def _():
        total[...] = part

    @pl.when(step > 0)
    def _():
        total[...] += part

    @pl.when(step == pl.num_programs(0) - 1)
    def _():
        dv, gain, bias = norm_back(total[...], n_ref[...], r_ref[...], g_ref[...])
        middle = grad_ref[...] + dv
        middle_ref[...] = middle
        branch = middle.astype(bf16)
        branch_ref[...] = branch
        put_sums(sums_ref, gain, bias, column_sum(branch), column_sum(down))
        w = sent_ref.shape[2]
        attended = contract(branch, wo_ref[...], 1, 1).astype(bf16)
        for m in range(sent_ref.shape[0]):
            sent_ref[m] = attended[:, m * w : (m + 1) * w]


def block_backward(core, grad, hidden, w_down, w_up, w_out, n2, r2, gain, members, grads=()):
    t, d = grad.shape
    f = hidden.shape[1]
    block = 512
    bands = 2 * members
    full = spec((t, d), lambda i, c: (0, 0))
    wide = spec((t, block), lambda i, c: (0, i))
    sent = (members, t, d // members)
    shape = jax.ShapeDtypeStruct
    outs = [
        wide, spec((1, block), lambda i, c: (0, i)), full, full,
        spec(sent, lambda i, c: (0, 0, 0)), spec((8, d), lambda i, c: (0, 0)),
    ]
    shapes = [
        shape((t, f), bf16), shape((1, f), f32), shape((t, d), f32), shape((t, d), bf16),
        shape(sent, bf16), shape((8, d), f32),
    ]
    scratch = [pltpu.VMEM((t, d), f32)]
    if grads:
        n = f // bands
        pairs = block // (2 * n)
        part = spec((pairs, n // 2, d), lambda i, c: (i, 0, 0))
        outs += [part] * 4
        shapes += [shape((bands // 2, n // 2, d), bf16), shape((bands // 2, n // 2 + d // bands, d), bf16)] * 2
        scratch += [pltpu.VMEM((block, d), f32)]
    return pl.pallas_call(
        functools.partial(block_backward_kernel, grads=bool(grads), bands=bands),
        grid_spec=pltpu.PrefetchScalarGridSpec(
            num_scalar_prefetch=1,
            grid=(f // block,),
            in_specs=[
                full, wide, spec((block, d), lambda i, c: (i, 0)), spec((d, block), lambda i, c: (0, i)),
                spec((d, d), lambda i, c: (0, 0)), full, spec((t, 1), lambda i, c: (0, 0)),
                spec((1, d), lambda i, c: (0, 0)),
            ] + [wide, full, full][: len(grads)],
            out_specs=outs,
            scratch_shapes=scratch,
        ),
        out_shape=shapes,
        compiler_params=pltpu.CompilerParams(vmem_limit_bytes=(60 if grads else 48) * MIB),
        cost_estimate=cost(18 if grads else 14),
        name="block_backward",
    )(core.reshape(1), grad, hidden, w_down, w_up, w_out, n2, r2, gain.reshape(1, d), *grads)


def grad_out_kernel(c_ref, l1, l0, r1, r0, _, __, other_ref, own_ref, sums, *, pairs):
    sums[...] = contract(l1[...], r1[...], 0, 0) + contract(l0[...], r0[...], 0, 0)
    n = own_ref.shape[1]
    for q in range(pairs):
        for ref, core in ((other_ref, 1 - c_ref[0]), (own_ref, c_ref[0])):
            ref[q] = sums[pl.ds(pl.multiple_of((2 * q + core) * n, n), n), :].astype(bf16)


def grad_out(core, left, right, bands, other, own):
    tokens, m = left[0].shape
    count, height, d = own.shape
    n = m // bands
    pairs = max(1, 256 // (2 * n))
    columns = spec((tokens, 2 * n * pairs), lambda j, c: (0, j))
    whole = spec((tokens, d), lambda j, c: (0, 0))
    out = spec((pairs, n, d), lambda j, c: (j, height // n - 1, 0))
    anywhere = pl.BlockSpec(memory_space=pl.ANY)
    return pl.pallas_call(
        functools.partial(grad_out_kernel, pairs=pairs),
        grid_spec=pltpu.PrefetchScalarGridSpec(
            num_scalar_prefetch=1,
            grid=(count // pairs,),
            in_specs=[columns, columns, whole, whole, anywhere, anywhere],
            out_specs=[out, out],
            scratch_shapes=[pltpu.VMEM((2 * n * pairs, d), f32)],
        ),
        out_shape=[jax.ShapeDtypeStruct(own.shape, bf16)] * 2,
        input_output_aliases={5: 0, 6: 1},
        compiler_params=pltpu.CompilerParams(vmem_limit_bytes=60 * MIB),
        cost_estimate=cost(3),
        name="grad_out",
    )(core.reshape(1), *left, *right, other, own)


def qkv_backward_kernel(b_ref, wq_ref, wk_ref, wv_ref, m_ref, n_ref, r_ref, g_ref, grad_ref, low_ref, sums_ref, qv_ref, total):
    step = pl.program_id(0)
    w = b_ref.shape[3]
    part = None
    for m in range(b_ref.shape[0]):
        for i, ref in enumerate((wq_ref, wk_ref, wv_ref)):
            x = contract(b_ref[m, i], ref[:, m * w : (m + 1) * w], 1, 1)
            part = x if part is None else part + x
        qv_ref[0:1, m * w : (m + 1) * w] = column_sum(b_ref[m, 0])
        qv_ref[1:2, m * w : (m + 1) * w] = column_sum(b_ref[m, 2])

    @pl.when(step == 0)
    def _():
        total[...] = part

    @pl.when(step > 0)
    def _():
        total[...] += part

    @pl.when(step == pl.num_programs(0) - 1)
    def _():
        dv, gain, bias = norm_back(total[...], n_ref[...], r_ref[...], g_ref[...])
        grad = m_ref[...] + dv
        grad_ref[...] = grad
        low_ref[...] = grad[grad.shape[0] - low_ref.shape[0] :].astype(bf16)
        put_sums(sums_ref, gain, bias, column_sum(grad))


def qkv_backward(back, w_qkv, middle_grad, n1, r1, gain, low):
    members, _, t, w = back.shape
    d = members * w
    at_once = max(2, 128 // w)
    block = at_once * w
    shift = d // block
    full = spec((t, d), lambda i: (0, 0))
    weight = [spec((d, block), lambda i, s=s: (0, s * shift + i)) for s in range(3)]
    shape = jax.ShapeDtypeStruct
    return pl.pallas_call(
        qkv_backward_kernel,
        grid=(members // at_once,),
        in_specs=[spec((at_once, 3, t, w), lambda i: (i, 0, 0, 0))] + weight + [
            full, full, spec((t, 1), lambda i: (0, 0)), spec((1, d), lambda i: (0, 0)),
        ],
        out_specs=[
            full, spec((low, d), lambda i: (0, 0)), spec((8, d), lambda i: (0, 0)),
            spec((8, block), lambda i: (0, i)),
        ],
        out_shape=[
            shape((t, d), f32), shape((low, d), bf16), shape((8, d), f32), shape((8, d), f32),
        ],
        scratch_shapes=[pltpu.VMEM((t, d), f32)],
        compiler_params=pltpu.CompilerParams(vmem_limit_bytes=60 * MIB),
        cost_estimate=cost(12),
        name="qkv_backward",
    )(back, w_qkv, w_qkv, w_qkv, middle_grad, n1, r1, gain.reshape(1, d))


def grad_heads_kernel(d_ref, n_ref, *rest):
    out_ref = rest[-1]
    rows = d_ref.shape[2]
    for i in range(3):
        total = rest[0][i] if len(rest) == 2 else jnp.zeros(out_ref.shape[1:], f32)
        for m in range(d_ref.shape[0]):
            total += contract(d_ref[m, i], n_ref[m * rows : (m + 1) * rows, :], 0, 0)
        out_ref[i] = total.astype(out_ref.dtype)


def grad_heads(d, normed_all, add, kind):
    members, _, rows, width = d.shape
    dim = normed_all.shape[1]
    shape = (3, width, dim)
    out = spec((3, width, dim // 4), lambda i: (0, 0, i))
    extra = [] if add is None else [add]
    return pl.pallas_call(
        grad_heads_kernel,
        grid=(4,),
        in_specs=[
            spec(d.shape, lambda i: (0, 0, 0, 0)),
            spec((members * rows, dim // 4), lambda i: (0, i)),
        ]
        + [out] * len(extra),
        out_specs=out,
        out_shape=jax.ShapeDtypeStruct(shape, kind),
        compiler_params=pltpu.CompilerParams(vmem_limit_bytes=60 * MIB),
        cost_estimate=cost(5),
        name="grad_heads",
    )(d, normed_all, *extra)


def take_kernel(table, *refs):
    for i in range(refs[-1].shape[0]):
        total = refs[0][table[i]].astype(f32)
        for r in refs[1:-1]:
            total = total + r[table[i]].astype(f32)
        refs[-1][i] = total.astype(bf16)


def take(terms, table):
    shape = terms[0].shape
    count = table.shape[0]
    return pl.pallas_call(
        take_kernel,
        grid_spec=pltpu.PrefetchScalarGridSpec(
            num_scalar_prefetch=1,
            grid=(1,),
            in_specs=[spec(shape, lambda i, t: (0, 0, 0))] * len(terms),
            out_specs=spec((count,) + shape[1:], lambda i, t: (0, 0, 0)),
        ),
        out_shape=jax.ShapeDtypeStruct((count,) + shape[1:], bf16),
        compiler_params=pltpu.CompilerParams(vmem_limit_bytes=60 * MIB),
        cost_estimate=cost(3),
        name="take",
    )(table, *terms)


def join_kernel(i_ref, own_ref, other_ref, out_ref):
    half = other_ref.shape[0]
    out_ref[i_ref[0]] = own_ref[:half]
    out_ref[1 - i_ref[0]] = other_ref[...].astype(f32)


def join(index, own, other):
    half, d = other.shape
    full = spec((half, d), lambda i, c: (0, 0))
    return pl.pallas_call(
        join_kernel,
        grid_spec=pltpu.PrefetchScalarGridSpec(
            num_scalar_prefetch=1,
            grid=(1,),
            in_specs=[full, full],
            out_specs=spec((2, half, d), lambda i, c: (0, 0, 0)),
        ),
        out_shape=jax.ShapeDtypeStruct((2, half, d), f32),
        compiler_params=pltpu.CompilerParams(vmem_limit_bytes=8 * MIB),
        cost_estimate=cost(2),
        name="join",
    )(index.reshape(1), own, other)


def unit_tables(bands, x_count, width, dim):
    members = bands // 2
    unit = math.gcd(HD, 3 * dim // bands)
    per_band = 3 * dim // bands // unit
    made, slots, place = [], [], {}
    for g in range(members):
        units = [(b * dim + g * width) // unit + i for b in range(3) for i in range(width // unit)]
        by_low = [[] for _ in range(members)]
        for local, u in enumerate(units):
            band = u // per_band
            core, x, zl = band % 2, band // 2 % x_count, band // (2 * x_count) % 2
            low = (core * 2 + zl) * x_count + x
            place[u] = (g, len(by_low[low]))
            by_low[low].append(local)
        made.append(by_low)
    most = max(len(l) for by_low in made for l in by_low)
    send = np.zeros((members, members * most), np.int32)
    for g, by_low in enumerate(made):
        for low, locals_ in enumerate(by_low):
            for m, local in enumerate(locals_):
                send[g, low * most + m] = local
    keep = np.zeros((members, 2, per_band), np.int32)
    for u, (g, m) in place.items():
        band = u // per_band
        core, x, zl = band % 2, band // 2 % x_count, band // (2 * x_count) % 2
        low = (core * 2 + zl) * x_count + x
        keep[low, band // members, u % per_band] = g * most + m
    return unit, send, keep


def norm_parts(v):
    centred = v - jnp.mean(v, axis=-1, keepdims=True)
    r = lax.rsqrt(jnp.mean(centred * centred, axis=-1, keepdims=True) + EPS)
    return centred * r, r


def norm_back(dy, n, r, gain):
    dyg = dy * gain
    mean_one = jnp.mean(dyg, axis=-1, keepdims=True)
    mean_two = jnp.mean(dyg * n, axis=-1, keepdims=True)
    dv = r * (dyg - mean_one - n * mean_two)
    return dv, jnp.sum(dy * n, axis=0, keepdims=True), jnp.sum(dy, axis=0, keepdims=True)


def gelu(x):
    return 0.5 * x * (1.0 + jnp.tanh(GELU_A * (x + GELU_B * x * x * x)))


def gelu_slope(x):
    t = jnp.tanh(GELU_A * (x + GELU_B * x * x * x))
    return 0.5 * (1.0 + t) + 0.5 * x * (1.0 - t * t) * (GELU_A * (1.0 + 3.0 * GELU_B * x * x))


def dot(a, b):
    return jnp.dot(a, b, preferred_element_type=f32)


def dot_t(a, b):
    return contract(a, b, 1, 1)


def swap(x, axis):
    return lax.ppermute(x, axis, SWAP)


def pin(x, *first):
    return lax.optimization_barrier((x,) + first)[0]


def total(terms):
    out = terms[0].astype(f32)
    for t in terms[1:]:
        out = out + t.astype(f32)
    return out


class Share:
    def __init__(self, terms, names):
        self.terms = list(terms)
        self.names = list(names)

    def halve(self, axis, *first):
        if axis not in self.names:
            return self.terms[-1]
        dim = self.names.index(axis)
        i = lax.axis_index(axis)
        terms = [pin(t, *first) if first else t for t in self.terms[-1:]] + self.terms[:-1]
        there = [lax.dynamic_index_in_dim(t, 1 - i, dim, keepdims=False) for t in terms]
        self.terms = [lax.dynamic_index_in_dim(t, i, dim, keepdims=False) for t in terms]
        self.names.remove(axis)
        sent = total(there).astype(bf16)
        self.terms.append(swap(sent, axis))
        return sent


def body(
    fields,
    lead_bucket,
    cotangent,
    lead_table,
    ln1_gain,
    ln1_bias,
    w_qkv,
    q_bias,
    v_bias,
    w_out,
    out_bias,
    ln2_gain,
    ln2_bias,
    w_up,
    up_bias,
    w_down,
    down_bias,
    *,
    axes,
    x_axes,
    samp_count,
):
    band = tuple(axes)
    low = ("core", "zl") + x_axes[::-1]
    members = 2 ** len(low)
    order = x_axes + ("zl", "core")
    D = w_out.shape[0]
    W = D // members
    half = fields.shape[1]
    rows = 2 * half
    two = samp_count == 2
    zh = lax.axis_index("zh")
    me = lax.axis_index(low)

    def pick(x, i):
        return lax.dynamic_index_in_dim(x, i, 0, keepdims=False)

    def to_sample(x):
        return jnp.concatenate([pick(x, zh), swap(pick(x, 1 - zh), "zh")])

    def to_band(x):
        own = x[:half]
        other = swap(x[half:].astype(bf16), "zh").astype(x.dtype)
        return jnp.where(zh == 0, jnp.stack([own, other]), jnp.stack([other, own]))

    def gather(x):
        if len(x_axes) == 1:
            x_axis = x_axes[0]
            cut = x.shape[0] // 2
            by_x = swap(x, x_axis)
            by_z = swap(x, "zl")
            far = [swap(by_x[:cut], "zl"), swap(by_z[cut:], x_axis)]
            pieces = [(x, 0, 0), (by_x, 1, 0), (by_z, 2, 0), (far[0], 3, 0), (far[1], 3, cut)]
            pieces += [(swap(p, "core"), 4 + k, o) for p, k, o in pieces]
        else:
            pieces = [(x, 0, 0)]
            for bit, axis in enumerate(order):
                pieces += [(swap(p, axis), k + 2**bit, 0) for p, k, _ in pieces]
        out = jnp.zeros((members * rows, D), bf16)
        for piece, k, offset in pieces:
            out = lax.dynamic_update_slice(out, piece, ((me ^ k) * rows + offset, 0))
        return out

    lead_row = pick(lead_table, pick(lead_bucket, zh)).astype(f32)
    carried = to_sample(fields).astype(f32)

    def member_columns(x, block):
        return lax.dynamic_slice_in_dim(x, block * D + me * W, W, x.ndim - 1)

    kept = []
    inputs = carried + lead_row
    n1, r1 = norm_parts(inputs)
    normed = (n1 * ln1_gain + ln1_bias).astype(bf16)
    weights = (w_out, out_bias, ln2_gain, ln2_bias, w_up, up_bias, w_down, down_bias, lead_row, ln1_gain, ln1_bias)
    for index in range(STEPS):
        normed_all = gather(normed)
        queries = (dot(normed, w_qkv[:, :D]) + q_bias).astype(bf16)
        if index == 0:
            out_grad = to_sample(pin(cotangent, normed_all))
        attended = attend(queries, normed_all, w_qkv, v_bias)
        if index == 0:
            attended, out_grad = pin((attended, out_grad))
        last = index == STEPS - 1
        n2, r2, normed_two, hidden, activated, *after = block_forward(inputs, attended, weights, last)
        kept.append((n1, r1, normed_all, attended, n2, r2, normed_two, hidden, activated))
        if not last:
            inputs, n1, r1, normed = after
    carried = after[0]
    result = to_band(carried)

    grad = out_grad
    small = None
    core = lax.axis_index("core")
    y = lax.axis_index("samp")
    bands = 2 ** len(axes)
    names = axes[:-1]
    cube = (2,) * len(names)
    later = None
    w_heads = None
    unit, send_table, keep_table = unit_tables(bands, 2 ** len(x_axes), W, D)
    send_row, keep_row = pick(jnp.asarray(send_table), me), pick(jnp.asarray(keep_table), me)
    keep_rows = pick(keep_row, zh), pick(keep_row, 1 - zh)
    def split_rows(x, rows_two):
        n, r, c = x.shape
        return x.reshape(cube + ((2, r // 2) if rows_two else (r,)) + (c,))

    own_weight = jnp.concatenate([member_columns(w_qkv, i) for i in range(3)], axis=1)
    own_bias = jnp.concatenate([member_columns(q_bias, 0), jnp.zeros((W,), f32), member_columns(v_bias, 0)])

    def own_part(index):
        own = (dot(kept[index][2], own_weight) + own_bias).astype(bf16)
        return own[:, :W], own[:, W : 2 * W], own[:, 2 * W :]

    owns = {}
    for index in reversed(range(STEPS)):
        n1, r1, normed_all, attended, n2, r2, normed_two, hidden, activated = kept[index]
        last = index == 0
        if last:
            grads = (later[2], later[3], normed_two)
        else:
            down_grad = grad.astype(bf16)
            grads = ()
        hidden_grad, hidden_sum, middle_grad, branch_grad, sent, sums_two, *ups = block_backward(
            core, grad, hidden, w_down, w_up, w_out, n2, r2, ln2_gain, members, grads
        )
        own_grad = lax.all_to_all(sent, low, 0, 0, tiled=True).reshape(members * rows, W)
        if last:
            z_other, x_other, z_own, x_own = ups
            z_core = swap(z_other, "core")
            left, right = (later[0], pin(down_grad, sent)), (later[1], activated)
            d_other, d_own = grad_rows(core, left, right, bands, 0, 1)
            d_core = swap(d_other, "core")
            x_other, x_own = grad_out(
                core, (later[4], pin(branch_grad, d_other)), (later[5], attended), bands, x_other, x_own
            )
            x_core = swap(x_other, "core")
            samp = ("samp",) * two
            d_terms = pin((d_own, d_core), x_other)
            down_share = Share([split_rows(t, two) for t in d_terms], names + samp)
            z_terms = pin((z_own, z_core), down_share.halve("samp"))
            z_share = Share([split_rows(t, two) for t in z_terms], names + samp)
            x_terms = pin((x_own, x_core), z_share.halve("zl"))
            x_share = Share([split_rows(t, two) for t in x_terms], names + samp)
            own_grad = pin(own_grad, x_share.halve(x_axes[0]))
            heads = W // HD
            d_heads = attend_back(*owns[0], own_grad, members, range((heads + 1) // 2))
            own_grad, d_heads, z_share.terms[-1] = pin((own_grad, d_heads, z_share.terms[-1]))
            sent = z_share.halve("zh")
            if heads > 1:
                own_grad, d_heads = pin((own_grad, d_heads), sent)
                d_heads = attend_back(*owns[0], own_grad, members, range(heads // 2, heads), d_heads)
            shares = (z_share, x_share, down_share)
            waits = pin((d_heads, *(t.terms[-1] for t in shares)))
            d_heads = waits[0]
            for t, value in zip(shares, waits[1:]):
                t.terms[-1] = value
            sent = [x_share.halve("samp"), z_share.halve("samp")] + [down_share.halve("zh")]
            d_heads = pin(d_heads, *sent)
        else:
            own_grad, send_row, keep_rows = pin((own_grad, send_row, keep_rows), result)
            later = (down_grad, activated, hidden_grad, normed_two, branch_grad, attended)
            owns[index] = own_part(index)
            d_heads = attend_back(*owns[index], own_grad, members)
        back = lax.all_to_all(d_heads, low, 0, 0, tiled=True)
        w_heads = grad_heads(d_heads, normed_all, w_heads, bf16 if last else f32)
        if last:
            units = w_heads.reshape(-1, unit, D)
            if two:
                there = lax.dynamic_slice_in_dim(units, (1 - y) * (D // 2), D // 2, 2)
                here = lax.dynamic_slice_in_dim(units, y * (D // 2), D // 2, 2)
                units = [here, swap(there, "samp")]
            else:
                there, units = units, [units]
            back = pin(back, there)
            x_share.terms[-1], z_share.terms[-1] = pin((x_share.terms[-1], z_share.terms[-1]), back)
            sent = [x_share.halve(a) for a in x_axes[1:] + ("zl",)] + [z_share.halve(a) for a in x_axes]
            units[-1] = pin(units[-1], *sent)
            outgoing = take(units, send_row)
            incoming = lax.all_to_all(outgoing, low, 0, 0, tiled=True)
            down_share.terms[-1] = pin(down_share.terms[-1], outgoing)
            back = pin(back, *[down_share.halve(a) for a in x_axes])
        else:
            owns[0] = own_part(0)
            back = pin(back, w_heads, *owns[0])
        grad, low_grad, sums_one, sums_qv = qkv_backward(
            back, w_qkv, middle_grad, n1, r1, ln1_gain, half if last else rows
        )
        down_grad = low_grad
        step_small = (sums_one[:3], sums_qv[:2], sums_two[:4], hidden_sum)
        small = step_small if small is None else tuple(a + b for a, b in zip(small, step_small))
    fields_sent = low_grad
    fields_other = swap(fields_sent, "zh")
    x_share.terms[-1] = pin(x_share.terms[-1], fields_sent)
    incoming = pin(incoming, x_share.halve("zh"))
    there = take([incoming], keep_rows[1])
    other = swap(there, "zh")
    one, qv, two_sums, up_sum = pin(small, there)
    samples = 2 * samp_count
    slot = 2 * y + zh
    mine = lax.broadcasted_iota(jnp.int32, (samples, 1), 0) == slot
    leads = jnp.where(mine, one[2:3], 0.0)
    lane = lax.broadcasted_iota(jnp.int32, (bands, D // bands), 1) == slot
    bucket = jnp.where(lane & (me == 0), pick(lead_bucket, zh).astype(f32), 0.0)
    vectors = jnp.concatenate([one[:2], qv, two_sums, leads])
    vectors = vectors.reshape(-1, bands, D // bands).transpose(1, 0, 2).reshape(bands, -1)
    vectors = jnp.concatenate([vectors, up_sum.reshape(bands, -1), bucket], axis=1)
    sums = vectors
    vectors = lax.all_to_all(vectors, band, 0, 0, tiled=True)

    def both(x):
        x = x.astype(bf16)
        if not two:
            return lax.psum(x, "samp").astype(f32)
        other = swap(x, "samp")
        return jnp.concatenate([jnp.where(y == 0, x, other), jnp.where(y == 0, other, x)]).astype(f32)

    def both_cut(x, n):
        if not two:
            x = both(x)
            return x[:n], x[n:]
        x = x.astype(bf16)
        other = swap(x, "samp")
        first, second = jnp.where(y == 0, x, other), jnp.where(y == 0, other, x)
        x = jnp.concatenate([first, second]).astype(f32)
        return x[:n], x[n:]

    incoming, down_share.terms[-1], z_share.terms[-1] = pin((incoming, down_share.terms[-1], z_share.terms[-1]), sums)
    sent = down_share.halve("zl")
    own = take([incoming], keep_rows[0])
    up_first = total(z_share.terms).astype(bf16)
    late = (vectors, fields_other, other, down_share.terms[-1], x_share.terms[-1])
    late = pin(late, sent, own, up_first)
    vectors, fields_other, other, down_share.terms[-1], x_share.terms[-1] = late
    vectors = jnp.sum(vectors, axis=0)
    vectors = vectors + swap(vectors, "samp") if two else lax.psum(vectors, "samp")
    own = total([own, other]).astype(bf16).reshape(3 * D // bands, -1)
    if two:
        other = swap(own, "samp")
        own = jnp.concatenate([jnp.where(y == 0, own, other), jnp.where(y == 0, other, own)], axis=1)
    else:
        own = lax.psum(own, "samp")
    w_qkv_grad = own.astype(f32).T

    w_down_grad = both(total(down_share.terms)).T
    n_up = w_up.shape[1] // bands
    bottom = both_cut(total(x_share.terms), n_up // 2)
    w_out_grad = bottom[1].T
    w_up_grad = jnp.concatenate([both(up_first), bottom[0]]).T
    fields_grad = join(zh, grad, fields_other)

    w = D // bands
    leads = vectors[8 * w : (8 + samples) * w].reshape(samples, w)
    up_grad = vectors[(8 + samples) * w : -w]
    buckets = vectors[-w:][:samples].astype(jnp.int32)
    one_hot = (buckets[:, None] == jnp.arange(lead_table.shape[0], dtype=jnp.int32)[None, :]).astype(f32)
    lead_grad = jnp.dot(one_hot.T, leads, precision=lax.Precision.HIGHEST)
    rows_of = lambda i: vectors[i * w : (i + 1) * w]
    g = [rows_of(i) for i in (0, 1, 2, 3, 6, 4, 5)] + [up_grad, rows_of(7)]
    return (
        result,
        fields_grad,
        lead_grad,
        g[0],
        g[1],
        w_qkv_grad,
        g[2],
        g[3],
        w_out_grad,
        g[4],
        g[5],
        g[6],
        w_up_grad,
        g[7],
        w_down_grad,
        g[8],
    )


def solution(mesh):
    samp_count, band_count = mesh.shape["samp"], mesh.shape["band"]
    x_axes = tuple(f"x{i}" for i in range((band_count // 8).bit_length() - 1))
    axes = ("zh", "zl") + x_axes + ("core",)
    assert 2 ** len(axes) == band_count
    fine = Mesh(mesh.devices.reshape((samp_count,) + (2,) * len(axes)), ("samp",) + axes)
    tokens = P("samp", axes, None)
    columns, vector = P(None, axes), P(axes)
    in_specs = (tokens, P("samp"), tokens) + (P(),) * 14
    out_specs = (
        tokens,
        tokens,
        columns,
        vector,
        vector,
        columns,
        vector,
        vector,
        columns,
        vector,
        vector,
        vector,
        columns,
        vector,
        columns,
        vector,
    )
    run = functools.partial(body, axes=axes, x_axes=x_axes, samp_count=samp_count)
    return jax.shard_map(run, mesh=fine, in_specs=in_specs, out_specs=out_specs, check_vma=False)
```
